256 devices in a mesh: group: 32 (over x, y, core), box: 8 (over z).
Axes of the slice: x: 4, y: 4, z: 8, core: 2. Of those that a mesh axis runs over, the one named last changes fastest.
Arguments:
- fine_state: float32 [32, 8, 48, 4, 1024], P('group', 'box'), may hold values from 0.05 to 2
- coarse_state: float32 [32, 8, 48, 1152], P('group', 'box'), may hold values from 0.05 to 2
- coag_kernel: bfloat16 [48, 2304], replicated, may hold values from -0.125 to 0.125
- diffusion: float32 [48], replicated, may hold values from 0.004 to 0.04
- levels: int32 [32, 8], P('group'), may hold values from 1 to 2
- ghost_src: int32 [32, 8, 576], P('group', 'box'), may hold values from 0 to 36863, as said below
Outputs:
- fine_out: float32 [32, 8, 48, 4, 1024], P('group', 'box')
- coarse_out: float32 [32, 8, 48, 1152], P('group', 'box')
The draws below stay inside these ranges and needn't reach their ends.
Inputs may be any that keep to these rules, and one draw needn't show every extreme that they name: `ghost_src`: an entry o * 1152 + c names coarse cell c of the owner in group o of the same box column; entries of one box come from a few owners and from scattered ones.
All inputs are finite; a program needn't handle non-finite values.
Results may differ from the reference program's by a relative error of at most 0.00065.
Values sent between devices are 32-bit elements; how exact they have to be, the bound alone decides.
No kernel may reach another device: no remote copies, remote signals or barrier semaphores. Data moves between devices by JAX's collectives and lax.ppermute only.
A program may use at most 128 MiB of HBM per device.

```python
import math
import jax
import jax.numpy as jnp
from jax import lax

SECTIONS = 48
BOX_X = 4
BOX_Y = 32
BOX_Z = 32
GHOSTS = 576
COARSE = 1152
GROUPS = 32
BOXES = 8


def draw_ghost_src(key, part):
    key = jax.random.fold_in(key, 7)
    keys = jax.random.split(key, 5)
    parent_one = jax.random.randint(keys[0], (GROUPS, BOXES, 1), 0, GROUPS)
    parent_two = jax.random.randint(keys[1], (GROUPS, BOXES, 1), 0, GROUPS)
    parent = jnp.minimum(parent_one, parent_two)
    coin = jax.random.randint(keys[2], (GROUPS, BOXES, GHOSTS), 0, 2)
    other = jax.random.randint(keys[3], (GROUPS, BOXES, GHOSTS), 0, GROUPS)
    owner_id = jnp.where(coin == 0, parent, other)
    cell_id = jax.random.randint(keys[4], (GROUPS, BOXES, GHOSTS), 0, COARSE)
    result = owner_id * COARSE + cell_id
    result = result.at[GROUPS - 1, :, GHOSTS - 1].set(GROUPS * COARSE - 1)
    result = result.at[0, :, 0].set(0)
    return result.astype(jnp.int32)


def touch_ends(array, stream_key, low, largest):
    index_at = [jax.random.randint(jax.random.fold_in(stream_key, axis), (), 0, length) for axis, length in enumerate(array.shape)]
    main_axis = array.shape.index(max(array.shape))
    neighbour = index_at[:main_axis] + [(index_at[main_axis] + 1) % array.shape[main_axis]] + index_at[main_axis + 1:]
    return array.at[tuple(index_at)].set(low).at[tuple(neighbour)].set(largest)


def shard_levels(rng, extent, pieces, least, top_value):
    factor_of, own = 1.0, jax.random.fold_in(rng, 6)
    for position, blocks in pieces:
        draws = jnp.exp(jax.random.uniform(jax.random.fold_in(own, position), (blocks,), jnp.float32, least / len(pieces), top_value / len(pieces)))
        factor_of = factor_of * jnp.repeat(draws, extent[position] // blocks).reshape([-1 if axis == position else 1 for axis in range(len(extent))])
    return factor_of


def bell_draw(own_key, extent, scale, reach, held_as=jnp.bfloat16):
    return jnp.clip(scale * jax.random.normal(own_key, extent, jnp.float32), -reach, reach).astype(held_as)


def setup_inputs(seed: int = 0) -> dict:
    key_of = jax.random.split(jax.random.key(seed), 7)
    fine_state = jnp.clip(jnp.exp(math.log(2.0) - 3.6888794 * jax.random.uniform(key_of[0], (GROUPS, BOXES, SECTIONS, BOX_X, BOX_Y * BOX_Z), jnp.float32) ** shard_levels(key_of[0], (GROUPS, BOXES, SECTIONS, BOX_X, BOX_Y * BOX_Z), ((0, 32), (1, 8)), -0.2, 0.2)), 0.05, 2.0)
    coarse_state = jnp.clip(jnp.exp(math.log(2.0) - 3.6888794 * jax.random.uniform(key_of[1], (GROUPS, BOXES, SECTIONS, COARSE), jnp.float32) ** shard_levels(key_of[1], (GROUPS, BOXES, SECTIONS, COARSE), ((0, 32), (1, 8)), -0.2, 0.2)), 0.05, 2.0)
    coag_kernel = bell_draw(key_of[2], (SECTIONS, SECTIONS * SECTIONS), (SECTIONS * SECTIONS) ** -0.5, 0.125)
    diffusion = jnp.clip(jnp.exp(jax.random.uniform(key_of[3], (SECTIONS,), jnp.float32, math.log(0.004), math.log(0.04))), 0.004, 0.04)
    levels = touch_ends(jax.random.randint(key_of[4], (GROUPS, BOXES), 1, 3), jax.random.fold_in(key_of[4], 1), 1, 2).astype(jnp.int32)
    ghost_src = draw_ghost_src(jax.random.fold_in(key_of[6], 71), 0)
    return dict(fine_state=fine_state, coarse_state=coarse_state, coag_kernel=coag_kernel, diffusion=diffusion, levels=levels, ghost_src=ghost_src)


step_size = 0.25


def coagulate(field, kernel):
    sections = field.shape[0]
    cells = field.shape[1]
    block_width = math.gcd(cells, 1024)
    blocks = jnp.moveaxis(field.reshape(sections, cells // block_width, block_width), 1, 0)

    def one_block(block_cells):
        pair_rows = (block_cells[:, None, :] * block_cells[None, :, :]).reshape(sections * sections, block_width).astype(jnp.bfloat16)
        return jnp.dot(kernel, pair_rows, preferred_element_type=jnp.float32)

    return jnp.moveaxis(lax.map(one_block, blocks), 0, 1).reshape(sections, cells)


def face_values(ghost_strip, box_shape):
    sections, width_x, width_y, width_z = box_shape
    y_count = width_x * width_z // 2
    y_coarse = ghost_strip[:, :y_count].reshape(sections, 2, width_x // 2, width_z // 2)
    x_coarse = ghost_strip[:, y_count:].reshape(sections, 2, width_y // 2, width_z // 2)
    y_ghost = jnp.repeat(jnp.repeat(y_coarse, 2, axis=2), 2, axis=3)
    x_ghost = jnp.repeat(jnp.repeat(x_coarse, 2, axis=2), 2, axis=3)
    return y_ghost, x_ghost


def laplacian(current, x_lower, x_upper, y_ghost):
    along_x = jnp.concatenate([x_lower[:, None], current, x_upper[:, None]], axis=1)
    along_y = jnp.concatenate([y_ghost[:, 0][:, :, None], current, y_ghost[:, 1][:, :, None]], axis=2)
    along_z = jnp.concatenate([current[..., :1], current, current[..., -1:]], axis=3)
    spread = along_x[:, 2:] + along_x[:, :-2] + along_y[:, :, 2:] + along_y[:, :, :-2]
    spread = spread + along_z[..., 2:] + along_z[..., :-2]
    return spread - 6.0 * current


def box_rate(current, lower_plane, upper_plane, ghost_strip, use_low, use_high, box_factor, diffusion, kernel):
    y_ghost, x_ghost = face_values(ghost_strip, current.shape)
    x_lower = jnp.where(use_low, lower_plane, x_ghost[:, 0])
    x_upper = jnp.where(use_high, upper_plane, x_ghost[:, 1])
    spread = laplacian(current, x_lower, x_upper, y_ghost)
    sections = current.shape[0]
    growth = coagulate(current.reshape(sections, -1), kernel).reshape(current.shape)
    return (box_factor * diffusion)[:, None, None, None] * spread + step_size * growth


def coarsen(plane):
    sections, first_len, last_len = plane.shape
    return plane.reshape(sections, first_len // 2, 2, last_len // 2, 2).mean(axis=(2, 4)).reshape(sections, -1)


def register_terms(mean_field, ghost_strip, use_low, use_high, box_factor, diffusion):
    sections, width_x, width_y, width_z = mean_field.shape
    below = jnp.concatenate([coarsen(mean_field[:, :, 0, :]), coarsen(mean_field[:, :, -1, :]), coarsen(mean_field[:, 0]), coarsen(mean_field[:, -1])], axis=1)
    y_count = width_x * width_z // 2
    x_each = width_y * width_z // 4
    face_mask = jnp.concatenate([jnp.ones((y_count,), jnp.float32), jnp.ones((x_each,), jnp.float32) * jnp.where(use_low, 0.0, 1.0), jnp.ones((x_each,), jnp.float32) * jnp.where(use_high, 0.0, 1.0)])
    return ((box_factor - 1.0) * diffusion)[:, None] * (ghost_strip - below) * face_mask[None, :]


def reference(fine_state, coarse_state, coag_kernel, diffusion, levels, ghost_src):
    groups, boxes = levels.shape
    sections = fine_state.shape[2]
    merged_shape = fine_state.shape
    fine_state = fine_state.reshape(groups, boxes, sections, BOX_X, BOX_Y, BOX_Z)
    cells_c = coarse_state.shape[3]
    columns = jnp.transpose(coarse_state, (1, 2, 0, 3)).reshape(boxes, sections, groups * cells_c)
    pick_column = jax.vmap(lambda column, slot_index: jnp.take(column, slot_index, axis=1))
    strips = jax.vmap(pick_column, in_axes=(None, 0))(columns, ghost_src)
    factor = jnp.power(2.0, levels.astype(jnp.float32))
    box_pos = jnp.arange(boxes)[None, :]
    left_level = jnp.concatenate([levels[:, :1], levels[:, :-1]], axis=1)
    right_level = jnp.concatenate([levels[:, 1:], levels[:, -1:]], axis=1)
    same_low = (box_pos > 0) & (left_level == levels)
    same_high = (box_pos < boxes - 1) & (right_level == levels)

    def flatten_boxes(array_in):
        return array_in.reshape((groups * boxes,) + array_in.shape[2:])

    def all_rates(current):
        lower = jnp.concatenate([jnp.zeros_like(current[:, :1, :, -1]), current[:, :-1, :, -1]], axis=1)
        upper = jnp.concatenate([current[:, 1:, :, 0], jnp.zeros_like(current[:, :1, :, 0])], axis=1)

        def one_box(box_inputs):
            fine_box, lower_plane, upper_plane, ghost_strip, use_low, use_high, box_factor = box_inputs
            return box_rate(fine_box, lower_plane, upper_plane, ghost_strip, use_low, use_high, box_factor, diffusion, coag_kernel)

        box_inputs = (flatten_boxes(current), flatten_boxes(lower), flatten_boxes(upper), flatten_boxes(strips), flatten_boxes(same_low), flatten_boxes(same_high), flatten_boxes(factor))
        return lax.map(one_box, box_inputs).reshape(current.shape)

    rate_one = all_rates(fine_state)
    middle = fine_state + rate_one
    rate_two = all_rates(middle)
    fine_out = fine_state + 0.5 * (rate_one + rate_two)
    mean_field = 0.5 * (fine_state + middle)
    registers = jax.vmap(register_terms, in_axes=(0, 0, 0, 0, 0, None))(flatten_boxes(mean_field), flatten_boxes(strips), flatten_boxes(same_low), flatten_boxes(same_high), flatten_boxes(factor), diffusion)
    registers = registers.reshape(groups, boxes, sections, -1)

    def column_sum(updates, slot_index):
        spread_rows = jnp.moveaxis(updates, 0, 1).reshape(sections, -1)
        return jnp.zeros((sections, groups * cells_c), jnp.float32).at[:, slot_index.reshape(-1)].add(spread_rows)

    column_sums = jax.vmap(column_sum, in_axes=(1, 1))(registers, ghost_src)
    reflux = column_sums.reshape(boxes, sections, groups, cells_c).transpose(2, 0, 1, 3)
    growth = lax.map(lambda owner_cells: coagulate(owner_cells, coag_kernel), coarse_state.reshape(groups * boxes, sections, cells_c))
    coarse_out = coarse_state + step_size * growth.reshape(coarse_state.shape) - reflux
    return fine_out.reshape(merged_shape), coarse_out
```

```python
import jax
import jax.numpy as jnp
from jax import lax
from jax.experimental import pallas as pl
from jax.experimental.pallas import tpu as pltpu
from jax.sharding import Mesh, PartitionSpec as P

S = 48
X = 4
PLANE = 1024
CELLS = 1152
GHOSTS = 576
WIDE = 640
STEP = 0.25
MIB = 1024 * 1024

f32 = jnp.float32
bf16 = jnp.bfloat16
i32 = jnp.int32
VMEM = pl.BlockSpec(memory_space=pltpu.VMEM)
SMEM = pl.BlockSpec(memory_space=pltpu.SMEM)


def sds(*shape):
    return jax.ShapeDtypeStruct(shape, f32)


def call(kernel, out_shape, in_specs, *operands, scratch=(), flops=0, name=None):
    many = isinstance(out_shape, list)
    return pl.pallas_call(
        kernel,
        out_shape=out_shape,
        in_specs=in_specs,
        out_specs=[VMEM] * len(out_shape) if many else VMEM,
        scratch_shapes=list(scratch),
        compiler_params=pltpu.CompilerParams(vmem_limit_bytes=40 * MIB),
        cost_estimate=pl.CostEstimate(flops=flops, bytes_accessed=4 * MIB, transcendentals=0),
        name=name,
    )(*operands)


def mm(a, b):
    return jnp.dot(a, b, preferred_element_type=f32)


def halves(value):
    high = value.astype(bf16)
    return high, (value - high.astype(f32)).astype(bf16)


def rows_of(values):
    parts = []
    for value in values:
        parts.extend(halves(value))
    return jnp.concatenate(parts, axis=0)


def sums_of(product, count):
    return [product[2 * S * i : 2 * S * i + S] + product[2 * S * i + S : 2 * S * (i + 1)] for i in range(count)]


def ones_where(mask):
    return jnp.where(mask, 1.0, 0.0).astype(bf16)


def split_planes(fine):
    def kernel(fine_ref, *planes):
        for x in range(X):
            planes[x][...] = fine_ref[:, x, :]

    return call(kernel, [sds(S, PLANE)] * X, [VMEM], fine, name="split_planes")


def coagulate(kernel_matrix, fields, name):
    count = len(fields)

    def kernel(matrix_ref, *refs):
        for field_ref, out_ref in zip(refs[:count], refs[count:]):
            width = field_ref.shape[1]
            for start in range(0, width, 1024):
                stop = min(start + 1024, width)
                v = field_ref[:, start:stop]
                pairs = jnp.concatenate([(v[j : j + 1] * v).astype(bf16) for j in range(S)], axis=0)
                out_ref[:, start:stop] = mm(matrix_ref[...], pairs)

    cells = sum(f.shape[1] for f in fields)
    return call(
        kernel,
        [sds(*f.shape) for f in fields],
        [VMEM] * (count + 1),
        kernel_matrix,
        *fields,
        flops=6 * cells * 2304 * 128,
        name=name,
    )


def owner_and_cell(request):
    owner = jnp.floor((request.astype(f32) + 0.5) * (1.0 / CELLS)).astype(i32)
    return owner, jnp.where(request < 0, -1, request - owner * CELLS)


def gather_columns(requests, sources, shifts, before, name):
    count = len(sources)

    def kernel(*refs):
        request_refs, source_refs = refs[:4], refs[4 : 4 + count]
        before_refs = refs[4 + count : 4 + count + len(before)]
        outs = refs[4 + count + len(before) : 8 + count + len(before)]
        x, y, c = lax.axis_index("x"), lax.axis_index("y"), lax.axis_index("core")
        rows = rows_of([ref[...] for ref in source_refs])
        cell_id = lax.broadcasted_iota(i32, (CELLS, 2 * WIDE), 0)
        for half in range(2):
            request = jnp.concatenate([request_refs[2 * half][...], request_refs[2 * half + 1][...]], axis=1)
            owner, cell = owner_and_cell(request)
            product = mm(rows, ones_where(jnp.broadcast_to(cell, (CELLS, 2 * WIDE)) == cell_id))
            total = jnp.zeros((S, 2 * WIDE), f32)
            for part, (shift, mate) in zip(sums_of(product, count), shifts):
                from_x = jnp.bitwise_and(x - shift, 3)
                source_owner = (from_x * 4 + y) * 2 + (1 - c if mate else c)
                total = total + jnp.where(owner == source_owner, part, 0.0)
            for i in range(2):
                part = total[:, i * WIDE : (i + 1) * WIDE]
                if before:
                    part = part + before_refs[2 * half + i][...]
                outs[2 * half + i][...] = part

    return call(
        kernel,
        [sds(S, WIDE)] * 4,
        [VMEM] * (4 + count + len(before)),
        *requests,
        *sources,
        *before,
        flops=2 * 4 * WIDE * CELLS * 256,
        name=name,
    )


def scatter_columns(requests, registers):
    total = 8 * WIDE

    def kernel(request_a, request_b, *refs):
        register_refs, outs, rows_ref, cell_ref = refs[:8], refs[8:12], refs[12], refs[13]
        x, y, c = lax.axis_index("x"), lax.axis_index("y"), lax.axis_index("core")
        lane = lax.broadcasted_iota(i32, (1, 256), 1)
        for i in range(8):
            request = (request_a if i < 4 else request_b)[i % 4 : i % 4 + 1, :]
            owner, cell = owner_and_cell(request)
            high, low = halves(register_refs[i][...])
            for k in range(4):
                to_x = jnp.bitwise_and(x + k, 3)
                mine = jnp.broadcast_to(jnp.where(owner == (to_x * 4 + y) * 2 + c, 1.0, 0.0).astype(bf16), (S, WIDE))
                rows_ref[2 * S * k : 2 * S * k + S, i * WIDE : (i + 1) * WIDE] = high * mine
                rows_ref[2 * S * k + S : 2 * S * (k + 1), i * WIDE : (i + 1) * WIDE] = low * mine
            for t in range(WIDE // 128):
                block = jnp.broadcast_to(cell[:, t * 128 : (t + 1) * 128].astype(f32), (128, 128))
                cell_ref[i * WIDE + t * 128 : i * WIDE + (t + 1) * 128, :] = block.T.astype(i32)

        def block(start, width):
            marks = [
                ones_where(cell_ref[...] == lane[:, :128] + (start + 128 * t)) for t in range(width // 128)
            ]
            product = mm(rows_ref[...], jnp.concatenate(marks, axis=1))
            return sums_of(product, 4)

        def body(i, carry):
            start = pl.multiple_of(i * 256, 256)
            for out, part in zip(outs, block(start, 256)):
                out[:, pl.ds(start, 256)] = part
            return carry

        lax.fori_loop(0, 4, body, 0)
        for out, part in zip(outs, block(1024, 128)):
            out[:, 1024:CELLS] = part

    return call(
        kernel,
        [sds(S, CELLS)] * 4,
        [VMEM] * 10,
        *requests,
        *registers,
        scratch=[pltpu.VMEM((8 * S, total), bf16), pltpu.VMEM((total, 128), i32)],
        flops=2 * total * CELLS * 384,
        name="scatter_columns",
    )


def box_facts(levels_ref):
    box = lax.axis_index("box")
    last = 7
    own = levels_ref[0, box]
    use_low = (box > 0) & (levels_ref[0, jnp.maximum(box - 1, 0)] == own)
    use_high = (box < last) & (levels_ref[0, jnp.minimum(box + 1, last)] == own)
    factor = lax.shift_left(1, own).astype(f32)
    return use_low, use_high, factor


def laplacian(planes, lower, upper, y_ghosts):
    lane = lax.broadcasted_iota(i32, (S, PLANE), 1)
    z = jnp.bitwise_and(lane, 31)
    wide = lax.broadcasted_iota(i32, (S, 128), 1)
    result = []
    for x in range(X):
        v = planes[x]
        ghost = y_ghosts[x // 2]
        before_y = pltpu.roll(v, 32, 1)
        after_y = pltpu.roll(v, PLANE - 32, 1)
        before_y = jnp.concatenate(
            [jnp.where(wide < 32, ghost[:, :128], before_y[:, :128]), before_y[:, 128:]], axis=1
        )
        after_y = jnp.concatenate(
            [after_y[:, :896], jnp.where(wide >= 96, ghost[:, 128:], after_y[:, 896:])], axis=1
        )
        before_z = jnp.where(z == 0, v, pltpu.roll(v, 1, 1))
        after_z = jnp.where(z == 31, v, pltpu.roll(v, PLANE - 1, 1))
        before_x = planes[x - 1] if x > 0 else lower
        after_x = planes[x + 1] if x < X - 1 else upper
        result.append(before_x + after_x + before_y + after_y + before_z + after_z - 6.0 * v)
    return result


def y_code(shape, lane_dim, row_dim, half):
    lane = lax.broadcasted_iota(i32, shape, lane_dim)
    row = lax.broadcasted_iota(i32, shape, row_dim)
    fine = jnp.where(lane < 32, lane, lane - 192)
    code = jnp.where(lane < 32, half * 16 + (lane >> 1), 32 + half * 16 + ((lane - 224) >> 1))
    return ones_where((code == row) & ((lane < 32) | (lane >= 224)))


def x_code(shape, lane_dim, row_dim):
    lane = lax.broadcasted_iota(i32, shape, lane_dim)
    row = lax.broadcasted_iota(i32, shape, row_dim)
    return ones_where((((lane >> 6) << 4) | ((lane >> 1) & 15)) == row)


def first_stage(levels, diffusion, planes, growth, strips, below_plane, above_plane):
    def kernel(levels_ref, diffusion_ref, *refs):
        plane_refs, growth_refs, strip_refs = refs[:4], refs[4:8], refs[8:12]
        lower_ref, upper_ref = refs[12:14]
        middle_refs, base_refs = refs[14:18], refs[18:22]
        registers_ref, x_low_ref, x_high_ref = refs[22:25]
        y_refs = refs[25:27]
        use_low, use_high, factor = box_facts(levels_ref)
        diffusion_column = diffusion_ref[...]
        strip = strip_refs[0][...] + strip_refs[1][...] + strip_refs[2][...] + strip_refs[3][...]
        x_low, x_high = sums_of(mm(rows_of([strip[:, :256], strip[:, 256:512]]), x_code((256, PLANE), 1, 0)), 2)
        y_rows = rows_of([strip[:, 512:640]])
        y_ghosts = [sums_of(mm(y_rows, y_code((128, 256), 1, 0, half)), 1)[0] for half in range(2)]
        x_low_ref[...] = x_low
        x_high_ref[...] = x_high
        for ref, ghost in zip(y_refs, y_ghosts):
            ref[...] = ghost
        lower = jnp.where(use_low, lower_ref[...], x_low)
        upper = jnp.where(use_high, upper_ref[...], x_high)
        values = [ref[...] for ref in plane_refs]
        spread = laplacian(values, lower, upper, y_ghosts)
        means = []
        for x in range(X):
            rate = (factor * diffusion_column) * spread[x] + STEP * growth_refs[x][...]
            middle = values[x] + rate
            middle_refs[x][...] = middle
            base_refs[x][...] = values[x] + 0.5 * rate
            means.append(0.5 * (values[x] + middle))
        x_below = sums_of(mm(rows_of([means[0], means[3]]), x_code((PLANE, 256), 0, 1)), 2)
        y_below = jnp.zeros((S, 128), f32)
        for half in range(2):
            both = means[2 * half] + means[2 * half + 1]
            ends = jnp.concatenate([both[:, :128], both[:, 896:]], axis=1)
            y_below = y_below + sums_of(mm(rows_of([ends]), y_code((256, 128), 0, 1, half)), 1)[0]
        below = 0.25 * jnp.concatenate(x_below + [y_below], axis=1)
        column = lax.broadcasted_iota(i32, (1, WIDE), 1)
        keep_low = jnp.where(use_low, 0.0, 1.0)
        keep_high = jnp.where(use_high, 0.0, 1.0)
        keep = jnp.where(column < 256, keep_low, jnp.where(column < 512, keep_high, 1.0))
        registers_ref[...] = ((factor - 1.0) * diffusion_column) * (strip - below) * keep

    outs = call(
        kernel,
        [sds(S, PLANE)] * 8 + [sds(S, WIDE)] + [sds(S, PLANE)] * 2 + [sds(S, 256)] * 2,
        [SMEM] + [VMEM] * 15,
        levels,
        diffusion,
        *planes,
        *growth,
        *strips,
        below_plane,
        above_plane,
        flops=10**9,
        name="first_stage",
    )
    return outs[:4], outs[4:8], outs[8], outs[9:11], outs[11:13]


def second_stage(levels, diffusion, middle, base, growth, x_ghosts, y_ghosts, below_plane, above_plane):
    def kernel(levels_ref, diffusion_ref, *refs):
        middle_refs, base_refs, growth_refs = refs[:4], refs[4:8], refs[8:12]
        x_low_ref, x_high_ref, y_a, y_b, lower_ref, upper_ref, out_ref = refs[12:]
        use_low, use_high, factor = box_facts(levels_ref)
        lower = jnp.where(use_low, lower_ref[...], x_low_ref[...])
        upper = jnp.where(use_high, upper_ref[...], x_high_ref[...])
        spread = laplacian([ref[...] for ref in middle_refs], lower, upper, [y_a[...], y_b[...]])
        for x in range(X):
            rate = (factor * diffusion_ref[...]) * spread[x] + STEP * growth_refs[x][...]
            out_ref[:, x, :] = base_refs[x][...] + 0.5 * rate

    return call(
        kernel,
        sds(S, X, PLANE),
        [SMEM] + [VMEM] * 19,
        levels,
        diffusion,
        *middle,
        *base,
        *growth,
        *x_ghosts,
        *y_ghosts,
        below_plane,
        above_plane,
        flops=10**8,
        name="second_stage",
    )


def finish_coarse(coarse, growth, parts):
    def kernel(coarse_ref, growth_ref, a, b, c, d, out_ref):
        total = (a[...] + b[...]) + (c[...] + d[...])
        out_ref[...] = coarse_ref[...] + STEP * growth_ref[...] - total

    return call(kernel, sds(S, CELLS), [VMEM] * 6, coarse, growth, *parts, flops=10**7, name="finish_coarse")


def shifted(value, axis, shift):
    size = lax.axis_size(axis)
    return lax.ppermute(value, axis, [(i, (i + shift) % size) for i in range(size)])


def along_box(value, shift):
    size = lax.axis_size("box")
    pairs = [(i, i + shift) for i in range(size) if 0 <= i + shift < size]
    return lax.ppermute(value, "box", pairs)


def on_device(fine_state, coarse_state, coag_kernel, diffusion, levels, ghost_src):
    fine = fine_state[0, 0]
    coarse = coarse_state[0, 0]
    column = diffusion.reshape(S, 1)
    source = ghost_src[0]
    y_count = GHOSTS - 512
    own_request = jnp.concatenate(
        [source[:, y_count:], source[:, :y_count], jnp.full((1, WIDE - GHOSTS), -1, i32)], axis=1
    )

    far = {k: shifted(coarse, "x", k) for k in (2, 1, 3)}
    mate = shifted(coarse, "core", 1)
    requests = [own_request] + [shifted(own_request, "y", k) for k in (1, 2, 3)]

    planes = split_planes(fine)
    below_plane, above_plane = along_box(planes[3], 1), along_box(planes[0], -1)
    growth = coagulate(coag_kernel, planes, "coagulate_fine")
    coarse_growth = coagulate(coag_kernel, [coarse], "coagulate_coarse")[0]

    part = gather_columns(requests, [coarse, mate], [(0, False), (0, True)], [], "gather_own")
    sources, shifts = [], []
    for k in (1, 3):
        sources += [far[k], shifted(far[k], "core", 1)]
        shifts += [(k, False), (k, True)]
    part = gather_columns(requests, sources, shifts, part, "gather_near")
    part = gather_columns(
        requests, [far[2], shifted(far[2], "core", 1)], [(2, False), (2, True)], part, "gather_far"
    )
    strips = [part[0]] + [shifted(part[k], "y", 4 - k) for k in (1, 2, 3)]

    middle, base, registers, x_ghosts, y_ghosts = first_stage(
        levels, column, planes, growth, strips, below_plane, above_plane
    )

    held = [registers] + [shifted(registers, "y", k) for k in (1, 2, 3)]
    below_plane, above_plane = along_box(middle[3], 1), along_box(middle[0], -1)
    request_rows = jnp.concatenate(requests, axis=0)
    mate_rows = shifted(request_rows, "core", 1)
    growth = coagulate(coag_kernel, middle, "coagulate_middle")
    mates = [shifted(value, "core", 1) for value in held]
    parts = scatter_columns([request_rows, mate_rows], held + mates)
    sent = [parts[0]] + [shifted(parts[k], "x", k) for k in (2, 1, 3)]
    fine_out = second_stage(levels, column, middle, base, growth, x_ghosts, y_ghosts, below_plane, above_plane)
    coarse_out = finish_coarse(coarse, coarse_growth, sent)
    return fine_out[None, None], coarse_out[None, None]


def solution(mesh):
    group = ("x", "y", "core")
    split = Mesh(mesh.devices.reshape(4, 4, 2, 8), group + ("box",))
    return jax.shard_map(
        on_device,
        mesh=split,
        in_specs=(
            P(group, "box", None, None, None),
            P(group, "box", None, None),
            P(),
            P(),
            P(group, None),
            P(group, "box", None),
        ),
        out_specs=(P(group, "box", None, None, None), P(group, "box", None, None)),
        check_vma=False,
    )
```

```python
import jax
import jax.numpy as jnp
from jax import lax
from jax.experimental import pallas as pl
from jax.experimental.pallas import tpu as pltpu
from jax.sharding import Mesh, PartitionSpec as P

S = 48
X = 4
PLANE = 1024
CELLS = 1152
GHOSTS = 576
WIDE = 640
STEP = 0.25
MIB = 1024 * 1024
COST = pl.CostEstimate(flops=1000, bytes_accessed=1000, transcendentals=0)

f32 = jnp.float32
bf16 = jnp.bfloat16
i32 = jnp.int32
VMEM = pl.BlockSpec(memory_space=pltpu.VMEM)
SMEM = pl.BlockSpec(memory_space=pltpu.SMEM)


def sds(*shape):
    return jax.ShapeDtypeStruct(shape, f32)


def call(kernel, out_shape, in_specs, *operands, scratch=(), name=None):
    many = isinstance(out_shape, list)
    return pl.pallas_call(
        kernel,
        out_shape=out_shape,
        in_specs=in_specs,
        out_specs=[VMEM] * len(out_shape) if many else VMEM,
        scratch_shapes=list(scratch),
        compiler_params=pltpu.CompilerParams(vmem_limit_bytes=40 * MIB),
        cost_estimate=COST,
        name=name,
    )(*operands)


def mm(a, b):
    return jnp.dot(a, b, preferred_element_type=f32)


def halves(value):
    high = value.astype(bf16)
    return high, (value - high.astype(f32)).astype(bf16)


def rows_of(values):
    parts = []
    for value in values:
        parts.extend(halves(value))
    return jnp.concatenate(parts, axis=0)


def sums_of(product, count):
    return [product[2 * S * i : 2 * S * i + S] + product[2 * S * i + S : 2 * S * (i + 1)] for i in range(count)]


def ones_where(mask):
    return jnp.where(mask, 1.0, 0.0).astype(bf16)


def split_planes(fine):
    def kernel(fine_ref, *planes):
        for x in range(X):
            planes[x][...] = fine_ref[:, x, :]

    return call(kernel, [sds(S, PLANE)] * X, [VMEM], fine, name="split_planes")


def coagulate(kernel_matrix, fields, name):
    count = len(fields)

    def kernel(matrix_ref, *refs):
        for field_ref, out_ref in zip(refs[:count], refs[count:]):
            width = field_ref.shape[1]
            for start in range(0, width, 1024):
                stop = min(start + 1024, width)
                v = field_ref[:, start:stop]
                pairs = jnp.concatenate([(v[j : j + 1] * v).astype(bf16) for j in range(S)], axis=0)
                out_ref[:, start:stop] = mm(matrix_ref[...], pairs)

    return call(
        kernel,
        [sds(*f.shape) for f in fields],
        [VMEM] * (count + 1),
        kernel_matrix,
        *fields,
        name=name,
    )


def owner_and_cell(request):
    owner = jnp.floor((request.astype(f32) + 0.5) * (1.0 / CELLS)).astype(i32)
    return owner, jnp.where(request < 0, -1, request - owner * CELLS)


def gather_columns(requests, sources, shifts):
    count = len(sources)

    def kernel(*refs):
        request_refs, source_refs, outs, rows_ref = refs[:2], refs[2 : 2 + count], refs[2 + count : 6 + count], refs[6 + count]
        x, y, c = lax.axis_index("x"), lax.axis_index("y"), lax.axis_index("core")
        for i in range(count):
            high, low = halves(source_refs[i][...])
            rows_ref[2 * S * i : 2 * S * i + S] = high
            rows_ref[2 * S * i + S : 2 * S * (i + 1)] = low
        cell_id = lax.broadcasted_iota(i32, (CELLS, WIDE), 0)
        for i in range(4):
            owner, cell = owner_and_cell(request_refs[i // 2][i % 2 : i % 2 + 1, :])
            product = mm(rows_ref[...], ones_where(jnp.broadcast_to(cell, (CELLS, WIDE)) == cell_id))
            total = jnp.zeros((S, WIDE), f32)
            for part, (shift, mate) in zip(sums_of(product, count), shifts):
                from_x = jnp.bitwise_and(x - shift, 3)
                source_owner = (from_x * 4 + y) * 2 + (1 - c if mate else c)
                total = total + jnp.where(owner == source_owner, part, 0.0)
            outs[i][...] = total

    return call(
        kernel,
        [sds(S, WIDE)] * 4,
        [VMEM] * (2 + count),
        *requests,
        *sources,
        scratch=[pltpu.VMEM((2 * S * count, CELLS), bf16)],
        name="gather_columns",
    )


def cells_by_row(requests):
    def kernel(request_a, request_b, out_ref):
        for i in range(8):
            cell = owner_and_cell((request_a if i < 4 else request_b)[i % 4 : i % 4 + 1, :])[1].astype(f32)
            for t in range(WIDE // 128):
                block = jnp.broadcast_to(cell[:, t * 128 : (t + 1) * 128], (128, 128))
                out_ref[i * WIDE + t * 128 : i * WIDE + (t + 1) * 128, :] = block.T.astype(i32)

    out = jax.ShapeDtypeStruct((8 * WIDE, 128), i32)
    return call(kernel, out, [VMEM] * 2, *requests, name="cells_by_row")


def scatter_columns(requests, cells, registers):
    total = 8 * WIDE

    def kernel(request_a, request_b, cell_ref, *refs):
        register_refs, outs, rows_ref = refs[:8], refs[8:12], refs[12]
        x, y, c = lax.axis_index("x"), lax.axis_index("y"), lax.axis_index("core")
        lane = lax.broadcasted_iota(i32, (1, 128), 1)
        for i in range(8):
            request = (request_a if i < 4 else request_b)[i % 4 : i % 4 + 1, :]
            owner, _ = owner_and_cell(request)
            high, low = halves(register_refs[i][...])
            for k in range(4):
                to_x = jnp.bitwise_and(x + k, 3)
                mine = jnp.broadcast_to(jnp.where(owner == (to_x * 4 + y) * 2 + c, 1.0, 0.0).astype(bf16), (S, WIDE))
                rows_ref[2 * S * k : 2 * S * k + S, i * WIDE : (i + 1) * WIDE] = high * mine
                rows_ref[2 * S * k + S : 2 * S * (k + 1), i * WIDE : (i + 1) * WIDE] = low * mine

        def block(start, width):
            marks = [ones_where(cell_ref[...] == lane + (start + 128 * t)) for t in range(width // 128)]
            return sums_of(mm(rows_ref[...], jnp.concatenate(marks, axis=1)), 4)

        def body(i, carry):
            start = pl.multiple_of(i * 256, 256)
            for out, part in zip(outs, block(start, 256)):
                out[:, pl.ds(start, 256)] = part
            return carry

        lax.fori_loop(0, 4, body, 0)
        for out, part in zip(outs, block(1024, 128)):
            out[:, 1024:CELLS] = part

    return call(
        kernel,
        [sds(S, CELLS)] * 4,
        [VMEM] * 11,
        *requests,
        cells,
        *registers,
        scratch=[pltpu.VMEM((8 * S, total), bf16)],
        name="scatter_columns",
    )


def box_facts(levels_ref):
    box = lax.axis_index("box")
    last = 7
    own = levels_ref[0, box]
    use_low = (box > 0) & (levels_ref[0, jnp.maximum(box - 1, 0)] == own)
    use_high = (box < last) & (levels_ref[0, jnp.minimum(box + 1, last)] == own)
    factor = lax.shift_left(1, own).astype(f32)
    return use_low, use_high, factor


def laplacian(planes, lower, upper, y_ghosts):
    rows = planes[0].shape[0]
    z = jnp.bitwise_and(lax.broadcasted_iota(i32, (rows, PLANE), 1), 31)
    wide = lax.broadcasted_iota(i32, (rows, 128), 1)
    result = []
    for x in range(X):
        v = planes[x]
        ghost = y_ghosts[x // 2]
        before_y = pltpu.roll(v, 32, 1)
        after_y = pltpu.roll(v, PLANE - 32, 1)
        before_y = jnp.concatenate(
            [jnp.where(wide < 32, ghost[:, :128], before_y[:, :128]), before_y[:, 128:]], axis=1
        )
        after_y = jnp.concatenate(
            [after_y[:, :896], jnp.where(wide >= 96, ghost[:, 128:], after_y[:, 896:])], axis=1
        )
        before_z = jnp.where(z == 0, v, pltpu.roll(v, 1, 1))
        after_z = jnp.where(z == 31, v, pltpu.roll(v, PLANE - 1, 1))
        before_x = planes[x - 1] if x > 0 else lower
        after_x = planes[x + 1] if x < X - 1 else upper
        result.append(before_x + after_x + before_y + after_y + before_z + after_z - 6.0 * v)
    return result


def y_code(shape, lane_dim, row_dim, half):
    lane = lax.broadcasted_iota(i32, shape, lane_dim)
    row = lax.broadcasted_iota(i32, shape, row_dim)
    fine = jnp.where(lane < 32, lane, lane - 192)
    code = jnp.where(lane < 32, half * 16 + (lane >> 1), 32 + half * 16 + ((lane - 224) >> 1))
    return ones_where((code == row) & ((lane < 32) | (lane >= 224)))


def x_code(shape, lane_dim, row_dim):
    lane = lax.broadcasted_iota(i32, shape, lane_dim)
    row = lax.broadcasted_iota(i32, shape, row_dim)
    return ones_where((((lane >> 6) << 4) | ((lane >> 1) & 15)) == row)


def first_stage(levels, diffusion, planes, growth, strips, below_plane, above_plane):
    def kernel(levels_ref, diffusion_ref, *refs):
        plane_refs, growth_refs, strip_refs = refs[:4], refs[4:8], refs[8:12]
        lower_ref, upper_ref = refs[12:14]
        middle_refs, base_refs = refs[14:18], refs[18:22]
        registers_ref, x_low_ref, x_high_ref = refs[22:25]
        y_refs = refs[25:27]
        use_low, use_high, factor = box_facts(levels_ref)
        diffusion_column = diffusion_ref[...]
        strip = strip_refs[0][...] + strip_refs[1][...] + strip_refs[2][...] + strip_refs[3][...]
        x_low, x_high = sums_of(mm(rows_of([strip[:, :256], strip[:, 256:512]]), x_code((256, PLANE), 1, 0)), 2)
        y_rows = rows_of([strip[:, 512:640]])
        y_ghosts = [sums_of(mm(y_rows, y_code((128, 256), 1, 0, half)), 1)[0] for half in range(2)]
        x_low_ref[...] = x_low
        x_high_ref[...] = x_high
        for ref, ghost in zip(y_refs, y_ghosts):
            ref[...] = ghost
        lower = jnp.where(use_low, lower_ref[...], x_low)
        upper = jnp.where(use_high, upper_ref[...], x_high)
        values = [ref[...] for ref in plane_refs]
        spread = laplacian(values, lower, upper, y_ghosts)
        means = []
        for x in range(X):
            rate = (factor * diffusion_column) * spread[x] + STEP * growth_refs[x][...]
            middle = values[x] + rate
            middle_refs[x][...] = middle
            base_refs[x][...] = values[x] + 0.5 * rate
            means.append(0.5 * (values[x] + middle))
        x_below = sums_of(mm(rows_of([means[0], means[3]]), x_code((PLANE, 256), 0, 1)), 2)
        y_below = jnp.zeros((S, 128), f32)
        for half in range(2):
            both = means[2 * half] + means[2 * half + 1]
            ends = jnp.concatenate([both[:, :128], both[:, 896:]], axis=1)
            y_below = y_below + sums_of(mm(rows_of([ends]), y_code((256, 128), 0, 1, half)), 1)[0]
        below = 0.25 * jnp.concatenate(x_below + [y_below], axis=1)
        column = lax.broadcasted_iota(i32, (1, WIDE), 1)
        keep_low = jnp.where(use_low, 0.0, 1.0)
        keep_high = jnp.where(use_high, 0.0, 1.0)
        keep = jnp.where(column < 256, keep_low, jnp.where(column < 512, keep_high, 1.0))
        registers_ref[...] = ((factor - 1.0) * diffusion_column) * (strip - below) * keep

    outs = call(
        kernel,
        [sds(S, PLANE)] * 8 + [sds(S, WIDE)] + [sds(S, PLANE)] * 2 + [sds(S, 256)] * 2,
        [SMEM] + [VMEM] * 15,
        levels,
        diffusion,
        *planes,
        *growth,
        *strips,
        below_plane,
        above_plane,
        name="first_stage",
    )
    return outs[:4], outs[4:8], outs[8], outs[9:11], outs[11:13]


def second_stage(levels, diffusion, middle, base, growth, x_ghosts, y_ghosts, below_plane, above_plane):
    rows = 8

    def kernel(levels_ref, diffusion_ref, *refs):
        middle_refs, base_refs, growth_refs = refs[:4], refs[4:8], refs[8:12]
        x_low_ref, x_high_ref, y_a, y_b, lower_ref, upper_ref, out_ref, held_ref, sems = refs[12:]
        use_low, use_high, factor = box_facts(levels_ref)
        copies = []
        for i in range(S // rows):
            part = slice(i * rows, (i + 1) * rows)
            lower = jnp.where(use_low, lower_ref[part], x_low_ref[part])
            upper = jnp.where(use_high, upper_ref[part], x_high_ref[part])
            spread = laplacian([ref[part] for ref in middle_refs], lower, upper, [y_a[part], y_b[part]])
            for x in range(X):
                rate = (factor * diffusion_ref[part]) * spread[x] + STEP * growth_refs[x][part]
                held_ref[part, x, :] = base_refs[x][part] + 0.5 * rate
            copies.append(pltpu.make_async_copy(held_ref.at[part], out_ref.at[part], sems.at[i]))
            copies[-1].start()
        for copy in copies:
            copy.wait()

    return pl.pallas_call(
        kernel,
        out_shape=sds(S, X, PLANE),
        in_specs=[SMEM] + [VMEM] * 19,
        out_specs=pl.BlockSpec(memory_space=pl.ANY),
        scratch_shapes=[pltpu.VMEM((S, X, PLANE), f32), pltpu.SemaphoreType.DMA((S // rows,))],
        compiler_params=pltpu.CompilerParams(vmem_limit_bytes=40 * MIB),
        cost_estimate=COST,
        name="second_stage",
    )(levels, diffusion, *middle, *base, *growth, *x_ghosts, *y_ghosts, below_plane, above_plane)


def finish_coarse(coarse, growth, parts):
    def kernel(coarse_ref, growth_ref, a, b, c, d, out_ref):
        total = (a[...] + b[...]) + (c[...] + d[...])
        out_ref[...] = coarse_ref[...] + STEP * growth_ref[...] - total

    return call(kernel, sds(S, CELLS), [VMEM] * 6, coarse, growth, *parts, name="finish_coarse")


def shifted(value, axis, shift):
    size = lax.axis_size(axis)
    return lax.ppermute(value, axis, [(i, (i + shift) % size) for i in range(size)])


def after(value, before):
    return lax.optimization_barrier((value, before))[0]


def on_device(fine_state, coarse_state, coag_kernel, diffusion, levels, ghost_src):
    fine = fine_state[0, 0]
    coarse = coarse_state[0, 0]
    column = diffusion.reshape(S, 1)
    source = ghost_src[0]
    y_count = GHOSTS - 512
    own_request = jnp.concatenate(
        [source[:, y_count:], source[:, :y_count], jnp.full((1, WIDE - GHOSTS), -1, i32)], axis=1
    )

    far = {k: shifted(coarse, "x", k) for k in (2, 1, 3)}
    mate = shifted(coarse, "core", 1)
    near = jnp.concatenate([own_request, shifted(own_request, "y", 1)], axis=0)
    requests = [near, shifted(near, "y", 2)]
    planes = split_planes(fine)
    below_plane, above_plane = shifted(planes[3], "box", 1), shifted(planes[0], "box", 7)
    far, requests, below_plane, above_plane = lax.optimization_barrier((far, requests, below_plane, above_plane))

    sources, shifts = [coarse, mate], [(0, False), (0, True)]
    for k in (1, 3, 2):
        sources += [far[k], shifted(far[k], "core", 1)]
        shifts += [(k, False), (k, True)]
    part = gather_columns(requests, sources, shifts)
    strips = [part[0]] + [shifted(part[k], "y", 4 - k) for k in (2, 1, 3)]
    growth = coagulate(after(coag_kernel, part[0]), planes, "coagulate_fine")
    request_rows = jnp.concatenate(requests, axis=0)
    mate_rows = shifted(request_rows, "core", 1)
    strips, growth, mate_rows = lax.optimization_barrier((strips, growth, mate_rows))

    middle, base, registers, x_ghosts, y_ghosts = first_stage(
        levels, column, planes, growth, strips, below_plane, above_plane
    )

    held = {k: shifted(registers, "y", k) for k in (2, 1, 3)}
    held[0] = registers
    cells = cells_by_row([request_rows, after(mate_rows, registers)])
    mates = [shifted(after(held[k], cells), "core", 1) for k in range(4)]
    parts = scatter_columns([request_rows, mate_rows], cells, [held[k] for k in range(4)] + mates)
    sent = [parts[0]] + [shifted(parts[k], "x", k) for k in (2, 1, 3)]
    middle, _ = lax.optimization_barrier((middle, parts[0]))
    below_plane, above_plane = shifted(middle[3], "box", 1), shifted(middle[0], "box", 7)
    growth = coagulate(coag_kernel, middle, "coagulate_middle")
    fine_out = second_stage(levels, column, middle, base, growth, x_ghosts, y_ghosts, below_plane, above_plane)
    coarse_growth = coagulate(after(coag_kernel, growth[0]), [coarse], "coagulate_coarse")[0]
    sent, fine_out, coarse_growth = lax.optimization_barrier((sent, fine_out, coarse_growth))
    coarse_out = finish_coarse(coarse, coarse_growth, sent)
    return fine_out[None, None], coarse_out[None, None]


def solution(mesh):
    group = ("x", "y", "core")
    split = Mesh(mesh.devices.reshape(4, 4, 2, 8), group + ("box",))
    return jax.shard_map(
        on_device,
        mesh=split,
        in_specs=(
            P(group, "box", None, None, None),
            P(group, "box", None, None),
            P(),
            P(),
            P(group, None),
            P(group, "box", None),
        ),
        out_specs=(P(group, "box", None, None, None), P(group, "box", None, None)),
        check_vma=False,
    )
```

```python
import jax
import jax.numpy as jnp
from jax import lax
from jax.experimental import pallas as pl
from jax.experimental.pallas import tpu as pltpu
from jax.sharding import Mesh, PartitionSpec as P

S = 48
X = 4
PLANE = 1024
CELLS = 1152
GHOSTS = 576
WIDE = 640
STEP = 0.25
MIB = 1024 * 1024
COST = pl.CostEstimate(flops=0, bytes_accessed=0, transcendentals=0)

f32 = jnp.float32
bf16 = jnp.bfloat16
i32 = jnp.int32
VMEM = pl.BlockSpec(memory_space=pltpu.VMEM)
SMEM = pl.BlockSpec(memory_space=pltpu.SMEM)


def sds(*shape):
    return jax.ShapeDtypeStruct(shape, f32)


def call(kernel, out_shape, in_specs, *operands, scratch=(), name=None):
    many = isinstance(out_shape, list)
    return pl.pallas_call(
        kernel,
        out_shape=out_shape,
        in_specs=in_specs,
        out_specs=[VMEM] * len(out_shape) if many else VMEM,
        scratch_shapes=list(scratch),
        compiler_params=pltpu.CompilerParams(vmem_limit_bytes=40 * MIB),
        cost_estimate=COST,
        name=name,
    )(*operands)


def mm(a, b):
    return jnp.dot(a, b, preferred_element_type=f32)


def halves(value):
    high = value.astype(bf16)
    return high, (value - high.astype(f32)).astype(bf16)


def rows_of(values):
    parts = []
    for value in values:
        parts.extend(halves(value))
    return jnp.concatenate(parts, axis=0)


def sums_of(product, count):
    return [product[2 * S * i : 2 * S * i + S] + product[2 * S * i + S : 2 * S * (i + 1)] for i in range(count)]


def ones_where(mask):
    return jnp.where(mask, 1.0, 0.0).astype(bf16)


def split_planes(fine, coarse):
    def kernel(fine_ref, coarse_ref, *outs):
        for x in range(X):
            outs[x][...] = fine_ref[:, x, :]
        outs[X][...] = coarse_ref[...]

    outs = call(kernel, [sds(S, PLANE)] * X + [sds(S, CELLS)], [VMEM] * 2, fine, coarse, name="split_planes")
    return outs[:X], outs[X]


def coagulate(kernel_matrix, fields, name):
    count = len(fields)

    def kernel(matrix_ref, *refs):
        for field_ref, out_ref in zip(refs[:count], refs[count:]):
            width = field_ref.shape[1]
            for start in range(0, width, 1024):
                stop = min(start + 1024, width)
                v = field_ref[:, start:stop]
                pairs = jnp.concatenate([(v[j : j + 1] * v).astype(bf16) for j in range(S)], axis=0)
                out_ref[:, start:stop] = mm(matrix_ref[...], pairs)

    return call(
        kernel,
        [sds(*f.shape) for f in fields],
        [VMEM] * (count + 1),
        kernel_matrix,
        *fields,
        name=name,
    )


def owner_and_cell(request):
    y_count = GHOSTS - 512
    none = jnp.full((1, WIDE - GHOSTS), -1, i32)
    request = jnp.concatenate([request[:, y_count:], request[:, :y_count], none], axis=1)
    owner = jnp.floor((request.astype(f32) + 0.5) * (1.0 / CELLS)).astype(i32)
    return owner, jnp.where(request < 0, -1, request - owner * CELLS)


def column_of(row):
    same = lax.broadcasted_iota(i32, (S, S), 0) == lax.broadcasted_iota(i32, (S, S), 1)
    return jnp.sum(jnp.where(same, jnp.broadcast_to(row, (S, S)), 0.0), axis=1, keepdims=True)


def pick(rows, request, shifts):
    x, y, c = lax.axis_index("x"), lax.axis_index("y"), lax.axis_index("core")
    owner, cell = owner_and_cell(request)
    cell_id = lax.broadcasted_iota(i32, (CELLS, WIDE), 0)
    product = mm(rows, ones_where(jnp.broadcast_to(cell, (CELLS, WIDE)) == cell_id))
    total = jnp.zeros((S, WIDE), f32)
    for part, (shift, mate) in zip(sums_of(product, len(shifts)), shifts):
        from_x = jnp.bitwise_and(x - shift, 3)
        source_owner = (from_x * 4 + y) * 2 + (1 - c if mate else c)
        total = total + jnp.where(owner == source_owner, part, 0.0)
    return total


def gather_first(requests, sources, shifts, row):
    count = len(sources)

    def kernel(request_ref, *refs):
        source_refs, (out_ref, rows_ref) = refs[:count], refs[count:]
        for i, ref in enumerate(source_refs):
            high, low = halves(ref[...])
            rows_ref[2 * S * i : 2 * S * i + S] = high
            rows_ref[2 * S * i + S : 2 * S * (i + 1)] = low
        out_ref[...] = pick(rows_ref[...], request_ref[row : row + 1, :], shifts)

    return call(
        kernel,
        [sds(S, WIDE), jax.ShapeDtypeStruct((2 * S * count, CELLS), bf16)],
        [VMEM] * (1 + count),
        requests,
        *sources,
        name="gather_first",
    )


def gather_next(requests, rows, shifts, row, name):
    def kernel(request_ref, rows_ref, out_ref):
        out_ref[...] = pick(rows_ref[...], request_ref[row : row + 1, :], shifts)

    return call(kernel, sds(S, WIDE), [VMEM] * 2, requests, rows, name=name)


def cells_by_row(requests):
    def kernel(request_a, request_b, out_ref):
        for i in range(8):
            cell = owner_and_cell((request_a if i < 4 else request_b)[i % 4 : i % 4 + 1, :])[1].astype(f32)
            for t in range(WIDE // 128):
                block = jnp.broadcast_to(cell[:, t * 128 : (t + 1) * 128], (128, 128))
                out_ref[i * WIDE + t * 128 : i * WIDE + (t + 1) * 128, :] = block.T.astype(i32)

    out = jax.ShapeDtypeStruct((8 * WIDE, 128), i32)
    return call(kernel, out, [VMEM] * 2, *requests, name="cells_by_row")


def scatter_columns(requests, cells, registers, steps, name):
    total = 8 * WIDE

    def kernel(request_a, request_b, cell_ref, *refs):
        register_refs, outs, rows_ref = refs[:8], refs[8:-1], refs[-1]
        x, y, c = lax.axis_index("x"), lax.axis_index("y"), lax.axis_index("core")
        lane = lax.broadcasted_iota(i32, (1, 128), 1)
        for i in range(8):
            request = (request_a if i < 4 else request_b)[i % 4 : i % 4 + 1, :]
            owner, _ = owner_and_cell(request)
            high, low = halves(register_refs[i][...])
            for k, step in enumerate(steps):
                to_x = jnp.bitwise_and(x + step, 3)
                mine = jnp.broadcast_to(jnp.where(owner == (to_x * 4 + y) * 2 + c, 1.0, 0.0).astype(bf16), (S, WIDE))
                rows_ref[2 * S * k : 2 * S * k + S, i * WIDE : (i + 1) * WIDE] = high * mine
                rows_ref[2 * S * k + S : 2 * S * (k + 1), i * WIDE : (i + 1) * WIDE] = low * mine

        def block(start, width):
            marks = [ones_where(cell_ref[...] == lane + (start + 128 * t)) for t in range(width // 128)]
            return sums_of(mm(rows_ref[...], jnp.concatenate(marks, axis=1)), len(steps))

        def body(i, carry):
            start = pl.multiple_of(i * 256, 256)
            for out, part in zip(outs, block(start, 256)):
                out[:, pl.ds(start, 256)] = part
            return carry

        lax.fori_loop(0, 4, body, 0)
        for out, part in zip(outs, block(1024, 128)):
            out[:, 1024:CELLS] = part

    return call(
        kernel,
        [sds(S, CELLS)] * len(steps),
        [VMEM] * 11,
        *requests,
        cells,
        *registers,
        scratch=[pltpu.VMEM((2 * S * len(steps), total), bf16)],
        name=name,
    )


def box_facts(levels_ref):
    box = lax.axis_index("box")
    last = 7
    own = levels_ref[0, box]
    use_low = (box > 0) & (levels_ref[0, jnp.maximum(box - 1, 0)] == own)
    use_high = (box < last) & (levels_ref[0, jnp.minimum(box + 1, last)] == own)
    factor = lax.shift_left(1, own).astype(f32)
    return use_low, use_high, factor


def laplacian(planes, lower, upper, y_ghosts):
    rows = planes[0].shape[0]
    z = jnp.bitwise_and(lax.broadcasted_iota(i32, (rows, PLANE), 1), 31)
    wide = lax.broadcasted_iota(i32, (rows, 128), 1)
    result = []
    for x in range(X):
        v = planes[x]
        ghost = y_ghosts[x // 2]
        before_y = pltpu.roll(v, 32, 1)
        after_y = pltpu.roll(v, PLANE - 32, 1)
        before_y = jnp.concatenate(
            [jnp.where(wide < 32, ghost[:, :128], before_y[:, :128]), before_y[:, 128:]], axis=1
        )
        after_y = jnp.concatenate(
            [after_y[:, :896], jnp.where(wide >= 96, ghost[:, 128:], after_y[:, 896:])], axis=1
        )
        before_z = jnp.where(z == 0, v, pltpu.roll(v, 1, 1))
        after_z = jnp.where(z == 31, v, pltpu.roll(v, PLANE - 1, 1))
        before_x = planes[x - 1] if x > 0 else lower
        after_x = planes[x + 1] if x < X - 1 else upper
        result.append(before_x + after_x + before_y + after_y + before_z + after_z - 6.0 * v)
    return result


def y_code(shape, lane_dim, row_dim, half):
    lane = lax.broadcasted_iota(i32, shape, lane_dim)
    row = lax.broadcasted_iota(i32, shape, row_dim)
    fine = jnp.where(lane < 32, lane, lane - 192)
    code = jnp.where(lane < 32, half * 16 + (lane >> 1), 32 + half * 16 + ((lane - 224) >> 1))
    return ones_where((code == row) & ((lane < 32) | (lane >= 224)))


def x_code(shape, lane_dim, row_dim):
    lane = lax.broadcasted_iota(i32, shape, lane_dim)
    row = lax.broadcasted_iota(i32, shape, row_dim)
    return ones_where((((lane >> 6) << 4) | ((lane >> 1) & 15)) == row)


def first_stage(levels, diffusion, planes, growth, strips, below_plane, above_plane):
    def kernel(levels_ref, diffusion_ref, *refs):
        plane_refs, growth_refs, strip_refs = refs[:4], refs[4:8], refs[8:12]
        lower_ref, upper_ref = refs[12:14]
        middle_refs, base_refs = refs[14:18], refs[18:22]
        registers_ref, x_low_ref, x_high_ref = refs[22:25]
        y_refs = refs[25:27]
        use_low, use_high, factor = box_facts(levels_ref)
        diffusion_column = column_of(diffusion_ref[...])
        strip = strip_refs[0][...] + strip_refs[1][...] + strip_refs[2][...] + strip_refs[3][...]
        x_low, x_high = sums_of(mm(rows_of([strip[:, :256], strip[:, 256:512]]), x_code((256, PLANE), 1, 0)), 2)
        y_rows = rows_of([strip[:, 512:640]])
        y_ghosts = [sums_of(mm(y_rows, y_code((128, 256), 1, 0, half)), 1)[0] for half in range(2)]
        x_low_ref[...] = x_low
        x_high_ref[...] = x_high
        for ref, ghost in zip(y_refs, y_ghosts):
            ref[...] = ghost
        lower = jnp.where(use_low, lower_ref[...], x_low)
        upper = jnp.where(use_high, upper_ref[...], x_high)
        values = [ref[...] for ref in plane_refs]
        spread = laplacian(values, lower, upper, y_ghosts)
        means = []
        for x in range(X):
            rate = (factor * diffusion_column) * spread[x] + STEP * growth_refs[x][...]
            middle = values[x] + rate
            middle_refs[x][...] = middle
            base_refs[x][...] = values[x] + 0.5 * rate
            means.append(0.5 * (values[x] + middle))
        x_below = sums_of(mm(rows_of([means[0], means[3]]), x_code((PLANE, 256), 0, 1)), 2)
        y_below = jnp.zeros((S, 128), f32)
        for half in range(2):
            both = means[2 * half] + means[2 * half + 1]
            ends = jnp.concatenate([both[:, :128], both[:, 896:]], axis=1)
            y_below = y_below + sums_of(mm(rows_of([ends]), y_code((256, 128), 0, 1, half)), 1)[0]
        below = 0.25 * jnp.concatenate(x_below + [y_below], axis=1)
        column = lax.broadcasted_iota(i32, (1, WIDE), 1)
        keep_low = jnp.where(use_low, 0.0, 1.0)
        keep_high = jnp.where(use_high, 0.0, 1.0)
        keep = jnp.where(column < 256, keep_low, jnp.where(column < 512, keep_high, 1.0))
        registers_ref[...] = ((factor - 1.0) * diffusion_column) * (strip - below) * keep

    outs = call(
        kernel,
        [sds(S, PLANE)] * 8 + [sds(S, WIDE)] + [sds(S, PLANE)] * 2 + [sds(S, 256)] * 2,
        [SMEM] + [VMEM] * 15,
        levels,
        diffusion,
        *planes,
        *growth,
        *strips,
        below_plane,
        above_plane,
        name="first_stage",
    )
    return outs[:4], outs[4:8], outs[8], outs[9:11], outs[11:13]


def second_stage(levels, diffusion, middle, base, growth, x_ghosts, y_ghosts, below_plane, above_plane):
    rows = 8

    def kernel(levels_ref, diffusion_ref, *refs):
        middle_refs, base_refs, growth_refs = refs[:4], refs[4:8], refs[8:12]
        x_low_ref, x_high_ref, y_a, y_b, lower_ref, upper_ref, out_ref, held_ref, sems = refs[12:]
        use_low, use_high, factor = box_facts(levels_ref)
        scale = factor * column_of(diffusion_ref[...])
        copies = []
        for i in range(S // rows):
            part = slice(i * rows, (i + 1) * rows)
            lower = jnp.where(use_low, lower_ref[part], x_low_ref[part])
            upper = jnp.where(use_high, upper_ref[part], x_high_ref[part])
            spread = laplacian([ref[part] for ref in middle_refs], lower, upper, [y_a[part], y_b[part]])
            for x in range(X):
                rate = scale[part] * spread[x] + STEP * growth_refs[x][part]
                held_ref[part, x, :] = base_refs[x][part] + 0.5 * rate
            copies.append(pltpu.make_async_copy(held_ref.at[part], out_ref.at[part], sems.at[i]))
            copies[-1].start()
        for copy in copies:
            copy.wait()

    return pl.pallas_call(
        kernel,
        out_shape=sds(S, X, PLANE),
        in_specs=[SMEM] + [VMEM] * 19,
        out_specs=pl.BlockSpec(memory_space=pl.ANY),
        scratch_shapes=[pltpu.VMEM((S, X, PLANE), f32), pltpu.SemaphoreType.DMA((S // rows,))],
        compiler_params=pltpu.CompilerParams(vmem_limit_bytes=40 * MIB),
        cost_estimate=COST,
        name="second_stage",
    )(levels, diffusion, *middle, *base, *growth, *x_ghosts, *y_ghosts, below_plane, above_plane)


def finish_coarse(coarse, growth, parts):
    def kernel(coarse_ref, growth_ref, a, b, c, d, out_ref):
        total = (a[...] + b[...]) + (c[...] + d[...])
        out_ref[...] = coarse_ref[...] + STEP * growth_ref[...] - total

    return call(kernel, sds(S, CELLS), [VMEM] * 6, coarse, growth, *parts, name="finish_coarse")


def shifted(value, axis, shift):
    size = lax.axis_size(axis)
    return lax.ppermute(value, axis, [(i, (i + shift) % size) for i in range(size)])


def after(value, before):
    return lax.optimization_barrier((value, before))[0]


def on_device(fine_state, coarse_state, coag_kernel, diffusion, levels, ghost_src):
    fine = fine_state[0, 0]
    coarse = coarse_state[0, 0]
    row = diffusion.reshape(1, S)
    request = ghost_src[0]

    near = shifted(request, "y", 1)
    far = {k: shifted(coarse, "x", k) for k in (2, 1, 3)}
    mate = shifted(coarse, "core", 1)
    near = jnp.concatenate([request, near], axis=0)
    away = shifted(near, "y", 2)
    planes, held_coarse = split_planes(fine, coarse)
    below_plane, above_plane = shifted(planes[3], "box", 1), shifted(planes[0], "box", 7)
    far, near, away, below_plane, above_plane = lax.optimization_barrier((far, near, away, below_plane, above_plane))

    sources, shifts = [held_coarse, mate], [(0, False), (0, True)]
    for k in (1, 3, 2):
        sources += [far[k], shifted(far[k], "core", 1)]
        shifts += [(k, False), (k, True)]
    part, strips = {}, {}
    part[2], rows = gather_first(away, sources, shifts, 0)
    strips[2] = shifted(part[2], "y", 2)
    part[1] = gather_next(after(near, part[2]), rows, shifts, 1, "gather_one")
    strips[1] = shifted(part[1], "y", 3)
    part[3] = gather_next(after(away, part[1]), rows, shifts, 1, "gather_three")
    strips[3] = shifted(part[3], "y", 1)
    strips[0] = gather_next(after(near, (part[3], strips[2])), rows, shifts, 0, "gather_own")
    growth = coagulate(after(coag_kernel, (strips[0], strips[1])), planes, "coagulate_fine")
    request_rows = jnp.concatenate([near, away], axis=0)
    mate_rows = shifted(request_rows, "core", 1)
    strips, growth, mate_rows = lax.optimization_barrier((strips, growth, mate_rows))
    strips = [strips[k] for k in range(4)]

    middle, base, registers, x_ghosts, y_ghosts = first_stage(
        levels, row, planes, growth, strips, below_plane, above_plane
    )

    held = {k: shifted(registers, "y", k) for k in (2, 1, 3)}
    held[0] = registers
    cells = cells_by_row([request_rows, after(mate_rows, registers)])
    growth = coagulate(after(coag_kernel, cells), middle, "coagulate_middle")
    held = [after(held[k], growth[0]) for k in range(4)]
    held += [shifted(value, "core", 1) for value in held]
    parts, sent = {}, {}
    parts[2], parts[1] = scatter_columns([request_rows, mate_rows], cells, held, (2, 1), "scatter_far")
    for k in (2, 1):
        sent[k] = shifted(parts[k], "x", k)
    parts[3], sent[0] = scatter_columns([request_rows, mate_rows], after(cells, parts[2]), held, (3, 0), "scatter_near")
    sent[3] = shifted(parts[3], "x", 3)
    middle, _ = lax.optimization_barrier((middle, (parts[3], sent[2])))
    below_plane, above_plane = shifted(middle[3], "box", 1), shifted(middle[0], "box", 7)
    coarse_growth = coagulate(after(coag_kernel, (parts[3], sent[1])), [held_coarse], "coagulate_coarse")[0]
    fine_out = second_stage(levels, row, middle, base, growth, x_ghosts, y_ghosts, below_plane, above_plane)
    sent, fine_out, coarse_growth = lax.optimization_barrier((sent, fine_out, coarse_growth))
    coarse_out = finish_coarse(held_coarse, coarse_growth, [sent[k] for k in range(4)])
    return fine_out[None, None], coarse_out[None, None]


def solution(mesh):
    group = ("x", "y", "core")
    split = Mesh(mesh.devices.reshape(4, 4, 2, 8), group + ("box",))
    return jax.shard_map(
        on_device,
        mesh=split,
        in_specs=(
            P(group, "box", None, None, None),
            P(group, "box", None, None),
            P(),
            P(),
            P(group, None),
            P(group, "box", None),
        ),
        out_specs=(P(group, "box", None, None, None), P(group, "box", None, None)),
        check_vma=False,
    )
```

```python
import jax
import jax.numpy as jnp
from jax import lax
from jax.experimental import pallas as pl
from jax.experimental.pallas import tpu as pltpu
from jax.sharding import Mesh, PartitionSpec as P

S = 48
X = 4
PLANE = 1024
CELLS = 1152
GHOSTS = 576
WIDE = 640
STEP = 0.25
FOLDED = 1280
MIB = 1024 * 1024
COST = pl.CostEstimate(flops=0, bytes_accessed=0, transcendentals=0)

f32 = jnp.float32
bf16 = jnp.bfloat16
i32 = jnp.int32
VMEM = pl.BlockSpec(memory_space=pltpu.VMEM)
SMEM = pl.BlockSpec(memory_space=pltpu.SMEM)


def sds(*shape):
    return jax.ShapeDtypeStruct(shape, f32)


def call(kernel, out_shape, in_specs, *operands, scratch=(), name=None):
    many = isinstance(out_shape, list)
    return pl.pallas_call(
        kernel,
        out_shape=out_shape,
        in_specs=in_specs,
        out_specs=[VMEM] * len(out_shape) if many else VMEM,
        scratch_shapes=list(scratch),
        compiler_params=pltpu.CompilerParams(vmem_limit_bytes=40 * MIB),
        cost_estimate=COST,
        name=name,
    )(*operands)


def mm(a, b):
    return jnp.dot(a, b, preferred_element_type=f32)


def halves(value):
    high = value.astype(bf16)
    return high, (value - high.astype(f32)).astype(bf16)


def rows_of(values):
    parts = []
    for value in values:
        parts.extend(halves(value))
    return jnp.concatenate(parts, axis=0)


def sums_of(product, count):
    return [product[2 * S * i : 2 * S * i + S] + product[2 * S * i + S : 2 * S * (i + 1)] for i in range(count)]


def ones_where(mask):
    return jnp.where(mask, 1.0, 0.0).astype(bf16)


def split_planes(fine, coarse):
    def kernel(fine_ref, coarse_ref, *outs):
        for x in range(X):
            outs[x][...] = fine_ref[:, x, :]
        outs[X][...] = coarse_ref[...]

    outs = call(kernel, [sds(S, PLANE)] * X + [sds(S, CELLS)], [VMEM] * 2, fine, coarse, name="split_planes")
    return outs[:X], outs[X]


def fold_kernel(kernel_matrix):
    pairs = S * S

    def kernel(matrix_ref, out_ref):
        pair = lax.broadcasted_iota(i32, (pairs, 128), 0)
        first = (pair * 43691) >> 21
        second = pair - first * S
        gap = second - first
        gap = jnp.where(gap < 0, gap + S, gap)
        place = jnp.where(gap <= S // 2, gap * S + first, (S - gap) * S + second)
        lane = lax.broadcasted_iota(i32, (1, 128), 1)
        for start in range(0, FOLDED, 256):
            marks = [ones_where(place == lane + (start + t)) for t in (0, 128)]
            sums = mm(matrix_ref[...], jnp.concatenate(marks, axis=1))
            high, low = halves(sums)
            out_ref[:S, start : start + 256] = high
            out_ref[S:, start : start + 256] = low

    out = jax.ShapeDtypeStruct((2 * S, FOLDED), bf16)
    return call(kernel, out, [VMEM], kernel_matrix, name="fold_kernel")


def coagulate(folded, fields, name):
    count = len(fields)

    def kernel(matrix_ref, *refs):
        for field_ref, out_ref in zip(refs[:count], refs[count:]):
            width = field_ref.shape[1]
            for start in range(0, width, 1024):
                stop = min(start + 1024, width)
                v = field_ref[:, start:stop]
                twice = jnp.concatenate([v, v], axis=0)
                turned = [twice] + [pltpu.roll(twice, 2 * S - b, 0) for b in range(1, 8)]
                pairs = [
                    (v * turned[d % 8][d - d % 8 : d - d % 8 + S]).astype(bf16) for d in range(S // 2 + 1)
                ]
                pairs.append(jnp.zeros((FOLDED - S * (S // 2 + 1), stop - start), bf16))
                product = mm(matrix_ref[...], jnp.concatenate(pairs, axis=0))
                out_ref[:, start:stop] = product[:S] + product[S:]

    return call(
        kernel,
        [sds(*f.shape) for f in fields],
        [VMEM] * (count + 1),
        folded,
        *fields,
        name=name,
    )


def owner_and_cell(request):
    y_count = GHOSTS - 512
    none = jnp.full((1, WIDE - GHOSTS), -1, i32)
    request = jnp.concatenate([request[:, y_count:], request[:, :y_count], none], axis=1)
    owner = jnp.floor((request.astype(f32) + 0.5) * (1.0 / CELLS)).astype(i32)
    return owner, jnp.where(request < 0, -1, request - owner * CELLS)


def column_of(row):
    same = lax.broadcasted_iota(i32, (S, S), 0) == lax.broadcasted_iota(i32, (S, S), 1)
    return jnp.sum(jnp.where(same, jnp.broadcast_to(row, (S, S)), 0.0), axis=1, keepdims=True)


def pick(rows, request, shifts):
    x, y, c = lax.axis_index("x"), lax.axis_index("y"), lax.axis_index("core")
    owner, cell = owner_and_cell(request)
    cell_id = lax.broadcasted_iota(i32, (CELLS, WIDE), 0)
    product = mm(rows, ones_where(jnp.broadcast_to(cell, (CELLS, WIDE)) == cell_id))
    total = jnp.zeros((S, WIDE), f32)
    for part, (shift, mate) in zip(sums_of(product, len(shifts)), shifts):
        from_x = jnp.bitwise_and(x - shift, 3)
        source_owner = (from_x * 4 + y) * 2 + (1 - c if mate else c)
        total = total + jnp.where(owner == source_owner, part, 0.0)
    return total


def gather_first(requests, sources, shifts, row):
    count = len(sources)

    def kernel(request_ref, *refs):
        source_refs, (out_ref, rows_ref) = refs[:count], refs[count:]
        for i, ref in enumerate(source_refs):
            high, low = halves(ref[...])
            rows_ref[2 * S * i : 2 * S * i + S] = high
            rows_ref[2 * S * i + S : 2 * S * (i + 1)] = low
        out_ref[...] = pick(rows_ref[...], request_ref[row : row + 1, :], shifts)

    return call(
        kernel,
        [sds(S, WIDE), jax.ShapeDtypeStruct((2 * S * count, CELLS), bf16)],
        [VMEM] * (1 + count),
        requests,
        *sources,
        name="gather_first",
    )


def gather_next(requests, rows, shifts, row, name):
    def kernel(request_ref, rows_ref, out_ref):
        out_ref[...] = pick(rows_ref[...], request_ref[row : row + 1, :], shifts)

    return call(kernel, sds(S, WIDE), [VMEM] * 2, requests, rows, name=name)


def cells_by_row(requests):
    def kernel(request_a, request_b, out_ref):
        for i in range(8):
            cell = owner_and_cell((request_a if i < 4 else request_b)[i % 4 : i % 4 + 1, :])[1].astype(f32)
            for t in range(WIDE // 128):
                block = jnp.broadcast_to(cell[:, t * 128 : (t + 1) * 128], (128, 128))
                out_ref[i * WIDE + t * 128 : i * WIDE + (t + 1) * 128, :] = block.T.astype(i32)

    out = jax.ShapeDtypeStruct((8 * WIDE, 128), i32)
    return call(kernel, out, [VMEM] * 2, *requests, name="cells_by_row")


def scatter_columns(requests, cells, registers, steps, name):
    total = 8 * WIDE

    def kernel(request_a, request_b, cell_ref, *refs):
        register_refs, outs, rows_ref = refs[:8], refs[8:-1], refs[-1]
        x, y, c = lax.axis_index("x"), lax.axis_index("y"), lax.axis_index("core")
        lane = lax.broadcasted_iota(i32, (1, 128), 1)
        for i in range(8):
            request = (request_a if i < 4 else request_b)[i % 4 : i % 4 + 1, :]
            owner, _ = owner_and_cell(request)
            high, low = halves(register_refs[i][...])
            for k, step in enumerate(steps):
                to_x = jnp.bitwise_and(x + step, 3)
                mine = jnp.broadcast_to(jnp.where(owner == (to_x * 4 + y) * 2 + c, 1.0, 0.0).astype(bf16), (S, WIDE))
                rows_ref[2 * S * k : 2 * S * k + S, i * WIDE : (i + 1) * WIDE] = high * mine
                rows_ref[2 * S * k + S : 2 * S * (k + 1), i * WIDE : (i + 1) * WIDE] = low * mine

        def block(start, width):
            marks = [ones_where(cell_ref[...] == lane + (start + 128 * t)) for t in range(width // 128)]
            return sums_of(mm(rows_ref[...], jnp.concatenate(marks, axis=1)), len(steps))

        def body(i, carry):
            start = pl.multiple_of(i * 256, 256)
            for out, part in zip(outs, block(start, 256)):
                out[:, pl.ds(start, 256)] = part
            return carry

        lax.fori_loop(0, 4, body, 0)
        for out, part in zip(outs, block(1024, 128)):
            out[:, 1024:CELLS] = part

    return call(
        kernel,
        [sds(S, CELLS)] * len(steps),
        [VMEM] * 11,
        *requests,
        cells,
        *registers,
        scratch=[pltpu.VMEM((2 * S * len(steps), total), bf16)],
        name=name,
    )


def box_facts(levels_ref):
    box = lax.axis_index("box")
    last = 7
    own = levels_ref[0, box]
    use_low = (box > 0) & (levels_ref[0, jnp.maximum(box - 1, 0)] == own)
    use_high = (box < last) & (levels_ref[0, jnp.minimum(box + 1, last)] == own)
    factor = lax.shift_left(1, own).astype(f32)
    return use_low, use_high, factor


def laplacian(planes, lower, upper, y_ghosts):
    rows = planes[0].shape[0]
    z = jnp.bitwise_and(lax.broadcasted_iota(i32, (rows, PLANE), 1), 31)
    wide = lax.broadcasted_iota(i32, (rows, 128), 1)
    result = []
    for x in range(X):
        v = planes[x]
        ghost = y_ghosts[x // 2]
        before_y = pltpu.roll(v, 32, 1)
        after_y = pltpu.roll(v, PLANE - 32, 1)
        before_y = jnp.concatenate(
            [jnp.where(wide < 32, ghost[:, :128], before_y[:, :128]), before_y[:, 128:]], axis=1
        )
        after_y = jnp.concatenate(
            [after_y[:, :896], jnp.where(wide >= 96, ghost[:, 128:], after_y[:, 896:])], axis=1
        )
        before_z = jnp.where(z == 0, v, pltpu.roll(v, 1, 1))
        after_z = jnp.where(z == 31, v, pltpu.roll(v, PLANE - 1, 1))
        before_x = planes[x - 1] if x > 0 else lower
        after_x = planes[x + 1] if x < X - 1 else upper
        result.append(before_x + after_x + before_y + after_y + before_z + after_z - 6.0 * v)
    return result


def y_code(shape, lane_dim, row_dim, half):
    lane = lax.broadcasted_iota(i32, shape, lane_dim)
    row = lax.broadcasted_iota(i32, shape, row_dim)
    fine = jnp.where(lane < 32, lane, lane - 192)
    code = jnp.where(lane < 32, half * 16 + (lane >> 1), 32 + half * 16 + ((lane - 224) >> 1))
    return ones_where((code == row) & ((lane < 32) | (lane >= 224)))


def x_code(shape, lane_dim, row_dim):
    lane = lax.broadcasted_iota(i32, shape, lane_dim)
    row = lax.broadcasted_iota(i32, shape, row_dim)
    return ones_where((((lane >> 6) << 4) | ((lane >> 1) & 15)) == row)


def first_stage(levels, diffusion, planes, growth, strips, below_plane, above_plane):
    def kernel(levels_ref, diffusion_ref, *refs):
        plane_refs, growth_refs, strip_refs = refs[:4], refs[4:8], refs[8:12]
        lower_ref, upper_ref = refs[12:14]
        middle_refs, base_refs = refs[14:18], refs[18:22]
        registers_ref, x_low_ref, x_high_ref = refs[22:25]
        y_refs = refs[25:27]
        use_low, use_high, factor = box_facts(levels_ref)
        diffusion_column = column_of(diffusion_ref[...])
        strip = strip_refs[0][...] + strip_refs[1][...] + strip_refs[2][...] + strip_refs[3][...]
        x_low, x_high = sums_of(mm(rows_of([strip[:, :256], strip[:, 256:512]]), x_code((256, PLANE), 1, 0)), 2)
        y_rows = rows_of([strip[:, 512:640]])
        y_ghosts = [sums_of(mm(y_rows, y_code((128, 256), 1, 0, half)), 1)[0] for half in range(2)]
        x_low_ref[...] = x_low
        x_high_ref[...] = x_high
        for ref, ghost in zip(y_refs, y_ghosts):
            ref[...] = ghost
        lower = jnp.where(use_low, lower_ref[...], x_low)
        upper = jnp.where(use_high, upper_ref[...], x_high)
        values = [ref[...] for ref in plane_refs]
        spread = laplacian(values, lower, upper, y_ghosts)
        means = []
        for x in range(X):
            rate = (factor * diffusion_column) * spread[x] + STEP * growth_refs[x][...]
            middle = values[x] + rate
            middle_refs[x][...] = middle
            base_refs[x][...] = values[x] + 0.5 * rate
            means.append(0.5 * (values[x] + middle))
        x_below = sums_of(mm(rows_of([means[0], means[3]]), x_code((PLANE, 256), 0, 1)), 2)
        y_below = jnp.zeros((S, 128), f32)
        for half in range(2):
            both = means[2 * half] + means[2 * half + 1]
            ends = jnp.concatenate([both[:, :128], both[:, 896:]], axis=1)
            y_below = y_below + sums_of(mm(rows_of([ends]), y_code((256, 128), 0, 1, half)), 1)[0]
        below = 0.25 * jnp.concatenate(x_below + [y_below], axis=1)
        column = lax.broadcasted_iota(i32, (1, WIDE), 1)
        keep_low = jnp.where(use_low, 0.0, 1.0)
        keep_high = jnp.where(use_high, 0.0, 1.0)
        keep = jnp.where(column < 256, keep_low, jnp.where(column < 512, keep_high, 1.0))
        registers_ref[...] = ((factor - 1.0) * diffusion_column) * (strip - below) * keep

    outs = call(
        kernel,
        [sds(S, PLANE)] * 8 + [sds(S, WIDE)] + [sds(S, PLANE)] * 2 + [sds(S, 256)] * 2,
        [SMEM] + [VMEM] * 15,
        levels,
        diffusion,
        *planes,
        *growth,
        *strips,
        below_plane,
        above_plane,
        name="first_stage",
    )
    return outs[:4], outs[4:8], outs[8], outs[9:11], outs[11:13]


def second_stage(levels, diffusion, middle, base, growth, x_ghosts, y_ghosts, below_plane, above_plane):
    rows = 8

    def kernel(levels_ref, diffusion_ref, *refs):
        middle_refs, base_refs, growth_refs = refs[:4], refs[4:8], refs[8:12]
        x_low_ref, x_high_ref, y_a, y_b, lower_ref, upper_ref, out_ref, held_ref, sems = refs[12:]
        use_low, use_high, factor = box_facts(levels_ref)
        scale = factor * column_of(diffusion_ref[...])
        copies = []
        for i in range(S // rows):
            part = slice(i * rows, (i + 1) * rows)
            lower = jnp.where(use_low, lower_ref[part], x_low_ref[part])
            upper = jnp.where(use_high, upper_ref[part], x_high_ref[part])
            spread = laplacian([ref[part] for ref in middle_refs], lower, upper, [y_a[part], y_b[part]])
            for x in range(X):
                rate = scale[part] * spread[x] + STEP * growth_refs[x][part]
                held_ref[part, x, :] = base_refs[x][part] + 0.5 * rate
            copies.append(pltpu.make_async_copy(held_ref.at[part], out_ref.at[part], sems.at[i]))
            copies[-1].start()
        for copy in copies:
            copy.wait()

    return pl.pallas_call(
        kernel,
        out_shape=sds(S, X, PLANE),
        in_specs=[SMEM] + [VMEM] * 19,
        out_specs=pl.BlockSpec(memory_space=pl.ANY),
        scratch_shapes=[pltpu.VMEM((S, X, PLANE), f32), pltpu.SemaphoreType.DMA((S // rows,))],
        compiler_params=pltpu.CompilerParams(vmem_limit_bytes=40 * MIB),
        cost_estimate=COST,
        name="second_stage",
    )(levels, diffusion, *middle, *base, *growth, *x_ghosts, *y_ghosts, below_plane, above_plane)


def finish_coarse(coarse, growth, parts):
    def kernel(coarse_ref, growth_ref, a, b, c, d, out_ref):
        total = (a[...] + b[...]) + (c[...] + d[...])
        out_ref[...] = coarse_ref[...] + STEP * growth_ref[...] - total

    return call(kernel, sds(S, CELLS), [VMEM] * 6, coarse, growth, *parts, name="finish_coarse")


def shifted(value, axis, shift):
    size = lax.axis_size(axis)
    return lax.ppermute(value, axis, [(i, (i + shift) % size) for i in range(size)])


def after(value, before):
    return lax.optimization_barrier((value, before))[0]


def on_device(fine_state, coarse_state, coag_kernel, diffusion, levels, ghost_src):
    fine = fine_state[0, 0]
    coarse = coarse_state[0, 0]
    row = diffusion.reshape(1, S)
    request = ghost_src[0]

    near = shifted(request, "y", 1)
    far = {k: shifted(coarse, "x", k) for k in (2, 1, 3)}
    mate = shifted(coarse, "core", 1)
    near = jnp.concatenate([request, near], axis=0)
    away = shifted(near, "y", 2)
    planes, held_coarse = split_planes(fine, coarse)
    folded = fold_kernel(after(coag_kernel, held_coarse))
    below_plane, above_plane = shifted(planes[3], "box", 1), shifted(planes[0], "box", 7)
    far, near, away, folded = lax.optimization_barrier((far, near, away, folded))

    sources, shifts = [held_coarse, mate], [(0, False), (0, True)]
    for k in (1, 3, 2):
        sources += [far[k], shifted(far[k], "core", 1)]
        shifts += [(k, False), (k, True)]
    part, strips = {}, {}
    part[2], rows = gather_first(away, sources, shifts, 0)
    strips[2] = shifted(part[2], "y", 2)
    below_plane, above_plane, _ = lax.optimization_barrier((below_plane, above_plane, part[2]))
    part[1] = gather_next(after(near, (part[2], below_plane, above_plane)), rows, shifts, 1, "gather_one")
    strips[1] = shifted(part[1], "y", 3)
    part[3] = gather_next(after(away, part[1]), rows, shifts, 1, "gather_three")
    strips[3] = shifted(part[3], "y", 1)
    strips[0] = gather_next(after(near, (part[3], strips[2])), rows, shifts, 0, "gather_own")
    growth = coagulate(after(folded, (strips[0], strips[1])), planes, "coagulate_fine")
    request_rows = jnp.concatenate([near, away], axis=0)
    mate_rows = shifted(request_rows, "core", 1)
    strips, growth, mate_rows = lax.optimization_barrier((strips, growth, mate_rows))
    strips = [strips[k] for k in range(4)]

    middle, base, registers, x_ghosts, y_ghosts = first_stage(
        levels, row, planes, growth, strips, below_plane, above_plane
    )

    held = {k: shifted(registers, "y", k) for k in (2, 1, 3)}
    held[0] = registers
    cells = cells_by_row([request_rows, after(mate_rows, registers)])
    growth = coagulate(after(folded, cells), middle, "coagulate_middle")
    held = [after(held[k], growth[0]) for k in range(4)]
    held += [shifted(value, "core", 1) for value in held]
    parts = scatter_columns([request_rows, mate_rows], cells, held, (2, 1, 3, 0), "scatter_columns")
    sent = [shifted(part, "x", k) for part, k in zip(parts, (2, 1, 3))] + [parts[3]]
    middle, _ = lax.optimization_barrier((middle, parts[3]))
    below_plane, above_plane = shifted(middle[3], "box", 1), shifted(middle[0], "box", 7)
    coarse_growth = coagulate(after(folded, parts[3]), [held_coarse], "coagulate_coarse")[0]
    fine_out = second_stage(levels, row, middle, base, growth, x_ghosts, y_ghosts, below_plane, above_plane)
    sent, fine_out, coarse_growth = lax.optimization_barrier((sent, fine_out, coarse_growth))
    coarse_out = finish_coarse(held_coarse, coarse_growth, sent)
    return fine_out[None, None], coarse_out[None, None]


def solution(mesh):
    group = ("x", "y", "core")
    split = Mesh(mesh.devices.reshape(4, 4, 2, 8), group + ("box",))
    return jax.shard_map(
        on_device,
        mesh=split,
        in_specs=(
            P(group, "box", None, None, None),
            P(group, "box", None, None),
            P(),
            P(),
            P(group, None),
            P(group, "box", None),
        ),
        out_specs=(P(group, "box", None, None, None), P(group, "box", None, None)),
        check_vma=False,
    )
```

```python
import jax
import jax.numpy as jnp
from jax import lax
from jax.experimental import pallas as pl
from jax.experimental.pallas import tpu as pltpu
from jax.sharding import Mesh, PartitionSpec as P

S = 48
X = 4
PLANE = 1024
CELLS = 1152
GHOSTS = 576
WIDE = 640
STEP = 0.25
FOLDED = 1280
MIB = 1024 * 1024
LIMIT = 52
SPREAD = 24
COST = pl.CostEstimate(flops=0, bytes_accessed=0, transcendentals=0)

f32 = jnp.float32
bf16 = jnp.bfloat16
i32 = jnp.int32
VMEM = pl.BlockSpec(memory_space=pltpu.VMEM)
SMEM = pl.BlockSpec(memory_space=pltpu.SMEM)


def sds(*shape):
    return jax.ShapeDtypeStruct(shape, f32)


def call(kernel, out_shape, in_specs, *operands, scratch=(), name=None):
    many = isinstance(out_shape, list)
    return pl.pallas_call(
        kernel,
        out_shape=out_shape,
        in_specs=in_specs,
        out_specs=[VMEM] * len(out_shape) if many else VMEM,
        scratch_shapes=list(scratch),
        compiler_params=pltpu.CompilerParams(vmem_limit_bytes=40 * MIB),
        cost_estimate=COST,
        name=name,
    )(*operands)


def mm(a, b):
    return jnp.dot(a, b, preferred_element_type=f32)


def halves(value):
    high = value.astype(bf16)
    return high, (value - high.astype(f32)).astype(bf16)


def rows_of(values):
    parts = []
    for value in values:
        parts.extend(halves(value))
    return jnp.concatenate(parts, axis=0)


def sums_of(product, count):
    return [product[2 * S * i : 2 * S * i + S] + product[2 * S * i + S : 2 * S * (i + 1)] for i in range(count)]


def ones_where(mask):
    return jnp.where(mask, 1.0, 0.0).astype(bf16)


def prepare(fine, coarse, kernel_matrix):
    pairs, rows = S * S, 8

    def kernel(fine_ref, coarse_ref, matrix_ref, *refs):
        planes, coarse_out, folded_ref = refs[:X], refs[X], refs[X + 1]
        fine_held, matrix_held, sems = refs[X + 2 :]
        parts = [slice(i * rows, (i + 1) * rows) for i in range(S // rows)]
        copies = [pltpu.make_async_copy(matrix_ref, matrix_held, sems.at[0])]
        copies += [pltpu.make_async_copy(fine_ref.at[p], fine_held.at[p], sems.at[2 + i]) for i, p in enumerate(parts)]
        copies.append(pltpu.make_async_copy(coarse_ref, coarse_out, sems.at[1]))
        for copy in copies:
            copy.start()
        pair = lax.broadcasted_iota(i32, (pairs, 128), 0)
        first = (pair * 43691) >> 21
        second = pair - first * S
        gap = second - first
        gap = jnp.where(gap < 0, gap + S, gap)
        place = jnp.where(gap <= S // 2, gap * S + first, (S - gap) * S + second)
        lane = lax.broadcasted_iota(i32, (1, 128), 1)
        copies[0].wait()
        for start in range(0, FOLDED, 256):
            marks = [ones_where(place == lane + (start + t)) for t in (0, 128)]
            high, low = halves(mm(matrix_held[...], jnp.concatenate(marks, axis=1)))
            folded_ref[:S, start : start + 256] = high
            folded_ref[S:, start : start + 256] = low
        for part, copy in zip(parts, copies[1:-1]):
            copy.wait()
            for x in range(X):
                planes[x][part] = fine_held[part, x, :]
        copies[-1].wait()

    outs = pl.pallas_call(
        kernel,
        out_shape=[sds(S, PLANE)] * X + [sds(S, CELLS), jax.ShapeDtypeStruct((2 * S, FOLDED), bf16)],
        in_specs=[pl.BlockSpec(memory_space=pl.ANY)] * 3,
        out_specs=[VMEM] * (X + 2),
        scratch_shapes=[
            pltpu.VMEM((S, X, PLANE), f32),
            pltpu.VMEM((S, pairs), bf16),
            pltpu.SemaphoreType.DMA((2 + S // rows,)),
        ],
        compiler_params=pltpu.CompilerParams(vmem_limit_bytes=LIMIT * MIB),
        cost_estimate=COST,
        name="prepare",
    )(fine, coarse, kernel_matrix)
    return outs[:X], outs[X], outs[X + 1]


def coagulate(folded, fields, name):
    count = len(fields)

    def kernel(matrix_ref, *refs):
        for field_ref, out_ref in zip(refs[:count], refs[count:]):
            width = field_ref.shape[1]
            for start in range(0, width, 1024):
                stop = min(start + 1024, width)
                v = field_ref[:, start:stop]
                twice = jnp.concatenate([v, v], axis=0)
                turned = [twice] + [pltpu.roll(twice, 2 * S - b, 0) for b in range(1, 8)]
                pairs = [
                    (v * turned[d % 8][d - d % 8 : d - d % 8 + S]).astype(bf16) for d in range(S // 2 + 1)
                ]
                pairs.append(jnp.zeros((FOLDED - S * (S // 2 + 1), stop - start), bf16))
                product = mm(matrix_ref[...], jnp.concatenate(pairs, axis=0))
                out_ref[:, start:stop] = product[:S] + product[S:]

    return call(
        kernel,
        [sds(*f.shape) for f in fields],
        [VMEM] * (count + 1),
        folded,
        *fields,
        name=name,
    )


def owner_and_cell(request):
    y_count = GHOSTS - 512
    none = jnp.full((1, WIDE - GHOSTS), -1, i32)
    request = jnp.concatenate([request[:, y_count:], request[:, :y_count], none], axis=1)
    owner = jnp.floor((request.astype(f32) + 0.5) * (1.0 / CELLS)).astype(i32)
    return owner, jnp.where(request < 0, -1, request - owner * CELLS)


def column_of(row):
    same = lax.broadcasted_iota(i32, (S, S), 0) == lax.broadcasted_iota(i32, (S, S), 1)
    return jnp.sum(jnp.where(same, jnp.broadcast_to(row, (S, S)), 0.0), axis=1, keepdims=True)


def pick(rows, request, shifts):
    x, y, c = lax.axis_index("x"), lax.axis_index("y"), lax.axis_index("core")
    owner, cell = owner_and_cell(request)
    cell_id = lax.broadcasted_iota(i32, (CELLS, WIDE), 0)
    product = mm(rows, ones_where(jnp.broadcast_to(cell, (CELLS, WIDE)) == cell_id))
    total = jnp.zeros((S, WIDE), f32)
    for part, (shift, mate) in zip(sums_of(product, len(shifts)), shifts):
        from_x = jnp.bitwise_and(x - shift, 3)
        source_owner = (from_x * 4 + y) * 2 + (1 - c if mate else c)
        total = total + jnp.where(owner == source_owner, part, 0.0)
    return total


def gather_first(requests, sources, shifts, row):
    count = len(sources)

    def kernel(*refs):
        request_refs, source_refs, (out_ref, rows_ref, request_out) = refs[:2], refs[2 : 2 + count], refs[2 + count :]
        for i in range(4):
            at = i % 2 * (SPREAD // 2)
            request_out[i : i + 1, :] = request_refs[i // 2][at : at + 1, :]
        for i, ref in enumerate(source_refs):
            high, low = halves(ref[...])
            rows_ref[2 * S * i : 2 * S * i + S] = high
            rows_ref[2 * S * i + S : 2 * S * (i + 1)] = low
        out_ref[...] = pick(rows_ref[...], request_out[row : row + 1, :], shifts)

    return call(
        kernel,
        [
            sds(S, WIDE),
            jax.ShapeDtypeStruct((2 * S * count, CELLS), bf16),
            jax.ShapeDtypeStruct((4, GHOSTS), i32),
        ],
        [VMEM] * (2 + count),
        *requests,
        *sources,
        name="gather_first",
    )


def gather_next(requests, rows, shifts, row, name):
    def kernel(request_ref, rows_ref, out_ref):
        out_ref[...] = pick(rows_ref[...], request_ref[row : row + 1, :], shifts)

    return call(kernel, sds(S, WIDE), [VMEM] * 2, requests, rows, name=name)


def cells_by_row(requests):
    def kernel(request_a, request_b, out_ref):
        for i in range(8):
            cell = owner_and_cell((request_a if i < 4 else request_b)[i % 4 : i % 4 + 1, :])[1].astype(f32)
            for t in range(WIDE // 128):
                block = jnp.broadcast_to(cell[:, t * 128 : (t + 1) * 128], (128, 128))
                out_ref[i * WIDE + t * 128 : i * WIDE + (t + 1) * 128, :] = block.T.astype(i32)

    out = jax.ShapeDtypeStruct((8 * WIDE, 128), i32)
    return call(kernel, out, [VMEM] * 2, *requests, name="cells_by_row")


def scatter_columns(requests, cells, registers, steps, name):
    total = 8 * WIDE

    def kernel(request_a, request_b, cell_ref, *refs):
        register_refs, outs, rows_ref = refs[:8], refs[8:-1], refs[-1]
        x, y, c = lax.axis_index("x"), lax.axis_index("y"), lax.axis_index("core")
        lane = lax.broadcasted_iota(i32, (1, 128), 1)
        for i in range(8):
            request = (request_a if i < 4 else request_b)[i % 4 : i % 4 + 1, :]
            owner, _ = owner_and_cell(request)
            high, low = halves(register_refs[i][...])
            for k, step in enumerate(steps):
                to_x = jnp.bitwise_and(x + step, 3)
                mine = jnp.broadcast_to(jnp.where(owner == (to_x * 4 + y) * 2 + c, 1.0, 0.0).astype(bf16), (S, WIDE))
                rows_ref[2 * S * k : 2 * S * k + S, i * WIDE : (i + 1) * WIDE] = high * mine
                rows_ref[2 * S * k + S : 2 * S * (k + 1), i * WIDE : (i + 1) * WIDE] = low * mine

        def block(start, width):
            marks = [ones_where(cell_ref[...] == lane + (start + 128 * t)) for t in range(width // 128)]
            return sums_of(mm(rows_ref[...], jnp.concatenate(marks, axis=1)), len(steps))

        def body(i, carry):
            start = pl.multiple_of(i * 256, 256)
            for out, part in zip(outs, block(start, 256)):
                out[:, pl.ds(start, 256)] = part
            return carry

        lax.fori_loop(0, 4, body, 0)
        for out, part in zip(outs, block(1024, 128)):
            out[:, 1024:CELLS] = part

    return call(
        kernel,
        [sds(S, CELLS)] * len(steps),
        [VMEM] * 11,
        *requests,
        cells,
        *registers,
        scratch=[pltpu.VMEM((2 * S * len(steps), total), bf16)],
        name=name,
    )


def box_facts(levels_ref):
    box = lax.axis_index("box")
    last = 7
    own = levels_ref[0, box]
    use_low = (box > 0) & (levels_ref[0, jnp.maximum(box - 1, 0)] == own)
    use_high = (box < last) & (levels_ref[0, jnp.minimum(box + 1, last)] == own)
    factor = lax.shift_left(1, own).astype(f32)
    return use_low, use_high, factor


def laplacian(planes, lower, upper, y_ghosts):
    rows = planes[0].shape[0]
    z = jnp.bitwise_and(lax.broadcasted_iota(i32, (rows, PLANE), 1), 31)
    wide = lax.broadcasted_iota(i32, (rows, 128), 1)
    result = []
    for x in range(X):
        v = planes[x]
        ghost = y_ghosts[x // 2]
        before_y = pltpu.roll(v, 32, 1)
        after_y = pltpu.roll(v, PLANE - 32, 1)
        before_y = jnp.concatenate(
            [jnp.where(wide < 32, ghost[:, :128], before_y[:, :128]), before_y[:, 128:]], axis=1
        )
        after_y = jnp.concatenate(
            [after_y[:, :896], jnp.where(wide >= 96, ghost[:, 128:], after_y[:, 896:])], axis=1
        )
        before_z = jnp.where(z == 0, v, pltpu.roll(v, 1, 1))
        after_z = jnp.where(z == 31, v, pltpu.roll(v, PLANE - 1, 1))
        before_x = planes[x - 1] if x > 0 else lower
        after_x = planes[x + 1] if x < X - 1 else upper
        result.append(before_x + after_x + before_y + after_y + before_z + after_z - 6.0 * v)
    return result


def y_code(shape, lane_dim, row_dim, half):
    lane = lax.broadcasted_iota(i32, shape, lane_dim)
    row = lax.broadcasted_iota(i32, shape, row_dim)
    fine = jnp.where(lane < 32, lane, lane - 192)
    code = jnp.where(lane < 32, half * 16 + (lane >> 1), 32 + half * 16 + ((lane - 224) >> 1))
    return ones_where((code == row) & ((lane < 32) | (lane >= 224)))


def x_code(shape, lane_dim, row_dim):
    lane = lax.broadcasted_iota(i32, shape, lane_dim)
    row = lax.broadcasted_iota(i32, shape, row_dim)
    return ones_where((((lane >> 6) << 4) | ((lane >> 1) & 15)) == row)


def first_stage(levels, diffusion, planes, growth, strips, below_plane, above_plane):
    def kernel(levels_ref, diffusion_ref, *refs):
        plane_refs, growth_refs, strip_refs = refs[:4], refs[4:8], refs[8:12]
        lower_ref, upper_ref = refs[12:14]
        middle_refs, base_refs = refs[14:18], refs[18:22]
        registers_ref, x_low_ref, x_high_ref = refs[22:25]
        y_refs = refs[25:27]
        use_low, use_high, factor = box_facts(levels_ref)
        diffusion_column = column_of(diffusion_ref[...])
        strip = strip_refs[0][...] + strip_refs[1][...] + strip_refs[2][...] + strip_refs[3][...]
        x_low, x_high = sums_of(mm(rows_of([strip[:, :256], strip[:, 256:512]]), x_code((256, PLANE), 1, 0)), 2)
        y_rows = rows_of([strip[:, 512:640]])
        y_ghosts = [sums_of(mm(y_rows, y_code((128, 256), 1, 0, half)), 1)[0] for half in range(2)]
        x_low_ref[...] = x_low
        x_high_ref[...] = x_high
        for ref, ghost in zip(y_refs, y_ghosts):
            ref[...] = ghost
        lower = jnp.where(use_low, lower_ref[...], x_low)
        upper = jnp.where(use_high, upper_ref[...], x_high)
        values = [ref[...] for ref in plane_refs]
        spread = laplacian(values, lower, upper, y_ghosts)
        means = []
        for x in range(X):
            rate = (factor * diffusion_column) * spread[x] + STEP * growth_refs[x][...]
            middle = values[x] + rate
            middle_refs[x][...] = middle
            base_refs[x][...] = values[x] + 0.5 * rate
            means.append(0.5 * (values[x] + middle))
        x_below = sums_of(mm(rows_of([means[0], means[3]]), x_code((PLANE, 256), 0, 1)), 2)
        y_below = jnp.zeros((S, 128), f32)
        for half in range(2):
            both = means[2 * half] + means[2 * half + 1]
            ends = jnp.concatenate([both[:, :128], both[:, 896:]], axis=1)
            y_below = y_below + sums_of(mm(rows_of([ends]), y_code((256, 128), 0, 1, half)), 1)[0]
        below = 0.25 * jnp.concatenate(x_below + [y_below], axis=1)
        column = lax.broadcasted_iota(i32, (1, WIDE), 1)
        keep_low = jnp.where(use_low, 0.0, 1.0)
        keep_high = jnp.where(use_high, 0.0, 1.0)
        keep = jnp.where(column < 256, keep_low, jnp.where(column < 512, keep_high, 1.0))
        registers_ref[...] = ((factor - 1.0) * diffusion_column) * (strip - below) * keep

    outs = call(
        kernel,
        [sds(S, PLANE)] * 8 + [sds(S, WIDE)] + [sds(S, PLANE)] * 2 + [sds(S, 256)] * 2,
        [SMEM] + [VMEM] * 15,
        levels,
        diffusion,
        *planes,
        *growth,
        *strips,
        below_plane,
        above_plane,
        name="first_stage",
    )
    return outs[:4], outs[4:8], outs[8], outs[9:11], outs[11:13]


def second_stage(levels, diffusion, middle, base, growth, x_ghosts, y_ghosts, below_plane, above_plane):
    rows = 8

    def kernel(levels_ref, diffusion_ref, *refs):
        middle_refs, base_refs, growth_refs = refs[:4], refs[4:8], refs[8:12]
        x_low_ref, x_high_ref, y_a, y_b, lower_ref, upper_ref, out_ref, held_ref, sems = refs[12:]
        use_low, use_high, factor = box_facts(levels_ref)
        scale = factor * column_of(diffusion_ref[...])
        copies = []
        for i in range(S // rows):
            part = slice(i * rows, (i + 1) * rows)
            lower = jnp.where(use_low, lower_ref[part], x_low_ref[part])
            upper = jnp.where(use_high, upper_ref[part], x_high_ref[part])
            spread = laplacian([ref[part] for ref in middle_refs], lower, upper, [y_a[part], y_b[part]])
            for x in range(X):
                rate = scale[part] * spread[x] + STEP * growth_refs[x][part]
                held_ref[part, x, :] = base_refs[x][part] + 0.5 * rate
            copies.append(pltpu.make_async_copy(held_ref.at[part], out_ref.at[part], sems.at[i]))
            copies[-1].start()
        for copy in copies:
            copy.wait()

    return pl.pallas_call(
        kernel,
        out_shape=sds(S, X, PLANE),
        in_specs=[SMEM] + [VMEM] * 19,
        out_specs=pl.BlockSpec(memory_space=pl.ANY),
        scratch_shapes=[pltpu.VMEM((S, X, PLANE), f32), pltpu.SemaphoreType.DMA((S // rows,))],
        compiler_params=pltpu.CompilerParams(vmem_limit_bytes=40 * MIB),
        cost_estimate=COST,
        name="second_stage",
    )(levels, diffusion, *middle, *base, *growth, *x_ghosts, *y_ghosts, below_plane, above_plane)


def finish_coarse(coarse, growth, parts):
    def kernel(coarse_ref, growth_ref, a, b, c, d, out_ref):
        total = (a[...] + b[...]) + (c[...] + d[...])
        out_ref[...] = coarse_ref[...] + STEP * growth_ref[...] - total

    return call(kernel, sds(S, CELLS), [VMEM] * 6, coarse, growth, *parts, name="finish_coarse")


def shifted(value, axis, shift):
    size = lax.axis_size(axis)
    return lax.ppermute(value, axis, [(i, (i + shift) % size) for i in range(size)])


def after(value, before):
    return lax.optimization_barrier((value, before))[0]


def on_device(fine_state, coarse_state, coag_kernel, diffusion, levels, ghost_src):
    fine = fine_state[0, 0]
    coarse = coarse_state[0, 0]
    row = diffusion.reshape(1, S)
    request = ghost_src[0]

    far = {k: shifted(coarse, "x", k) for k in (2, 1, 3)}
    spread = jnp.broadcast_to(request, (SPREAD, GHOSTS))
    near = shifted(spread, "y", 1)
    mate = shifted(coarse, "core", 1)
    planes, held_coarse, folded = prepare(fine, coarse, coag_kernel)
    below_plane, above_plane = shifted(planes[3], "box", 1), shifted(planes[0], "box", 7)
    near, held_coarse = lax.optimization_barrier((near, held_coarse))
    requests = jnp.concatenate([spread[: SPREAD // 2], near[: SPREAD // 2]], axis=0)
    far, requests = lax.optimization_barrier((far, requests))
    requests = [requests, shifted(requests, "y", 2)]

    sources, shifts = [held_coarse, mate], [(0, False), (0, True)]
    for k in (1, 3, 2):
        sources += [far[k], shifted(far[k], "core", 1)]
        shifts += [(k, False), (k, True)]
    part, strips = {}, {}
    part[2], rows, request_rows = gather_first(requests, sources, shifts, 2)
    strips[2] = shifted(part[2], "y", 2)
    part[1] = gather_next(request_rows, rows, shifts, 1, "gather_one")
    strips[1] = shifted(part[1], "y", 3)
    part[3] = gather_next(after(request_rows, part[1]), rows, shifts, 3, "gather_three")
    strips[3] = shifted(part[3], "y", 1)
    strips[0] = gather_next(after(request_rows, (part[3], strips[2])), rows, shifts, 0, "gather_own")
    growth = coagulate(after(folded, (strips[0], strips[1], below_plane, above_plane)), planes, "coagulate_fine")
    mate_rows = shifted(request_rows, "core", 1)
    strips, growth, mate_rows = lax.optimization_barrier((strips, growth, mate_rows))
    strips = [strips[k] for k in range(4)]

    middle, base, registers, x_ghosts, y_ghosts = first_stage(
        levels, row, planes, growth, strips, below_plane, above_plane
    )

    held = {k: shifted(registers, "y", k) for k in (2, 1, 3)}
    held[0] = registers
    cells = cells_by_row([request_rows, after(mate_rows, registers)])
    below_plane, above_plane = shifted(middle[3], "box", 1), shifted(middle[0], "box", 7)
    growth = coagulate(after(folded, cells), middle, "coagulate_middle")
    held = [after(held[k], growth[0]) for k in range(4)]
    held += [shifted(value, "core", 1) for value in held]
    parts = scatter_columns([request_rows, mate_rows], after(cells, (below_plane, above_plane)), held, (2, 1, 3, 0), "scatter_columns")
    sent = [shifted(part, "x", k) for part, k in zip(parts, (2, 1, 3))] + [parts[3]]
    coarse_growth = coagulate(after(folded, parts[3]), [held_coarse], "coagulate_coarse")[0]
    fine_out = second_stage(levels, row, middle, base, growth, x_ghosts, y_ghosts, below_plane, above_plane)
    sent, fine_out, coarse_growth = lax.optimization_barrier((sent, fine_out, coarse_growth))
    coarse_out = finish_coarse(held_coarse, coarse_growth, sent)
    return fine_out[None, None], coarse_out[None, None]


def solution(mesh):
    group = ("x", "y", "core")
    split = Mesh(mesh.devices.reshape(4, 4, 2, 8), group + ("box",))
    return jax.shard_map(
        on_device,
        mesh=split,
        in_specs=(
            P(group, "box", None, None, None),
            P(group, "box", None, None),
            P(),
            P(),
            P(group, None),
            P(group, "box", None),
        ),
        out_specs=(P(group, "box", None, None, None), P(group, "box", None, None)),
        check_vma=False,
    )
```

```python
import jax
import jax.numpy as jnp
from jax import lax
from jax.experimental import pallas as pl
from jax.experimental.pallas import tpu as pltpu
from jax.sharding import Mesh, PartitionSpec as P

S = 48
X = 4
PLANE = 1024
CELLS = 1152
GHOSTS = 576
WIDE = 640
STEP = 0.25
FOLDED = 1280
MIB = 1024 * 1024
LIMIT = 52
SPREAD = 24
COST = pl.CostEstimate(flops=0, bytes_accessed=0, transcendentals=0)

f32 = jnp.float32
bf16 = jnp.bfloat16
i32 = jnp.int32
VMEM = pl.BlockSpec(memory_space=pltpu.VMEM)
SMEM = pl.BlockSpec(memory_space=pltpu.SMEM)


def sds(*shape):
    return jax.ShapeDtypeStruct(shape, f32)


def call(kernel, out_shape, in_specs, *operands, scratch=(), name=None):
    many = isinstance(out_shape, list)
    return pl.pallas_call(
        kernel,
        out_shape=out_shape,
        in_specs=in_specs,
        out_specs=[VMEM] * len(out_shape) if many else VMEM,
        scratch_shapes=list(scratch),
        compiler_params=pltpu.CompilerParams(vmem_limit_bytes=40 * MIB),
        cost_estimate=COST,
        name=name,
    )(*operands)


def mm(a, b):
    return jnp.dot(a, b, preferred_element_type=f32)


def halves(value):
    high = value.astype(bf16)
    return high, (value - high.astype(f32)).astype(bf16)


def rows_of(values):
    parts = []
    for value in values:
        parts.extend(halves(value))
    return jnp.concatenate(parts, axis=0)


def sums_of(product, count):
    return [product[2 * S * i : 2 * S * i + S] + product[2 * S * i + S : 2 * S * (i + 1)] for i in range(count)]


def ones_where(mask):
    return jnp.where(mask, 1.0, 0.0).astype(bf16)


def fold_kernel(kernel_matrix):
    pairs = S * S

    def kernel(matrix_ref, folded_ref):
        pair = lax.broadcasted_iota(i32, (pairs, 128), 0)
        first = (pair * 43691) >> 21
        second = pair - first * S
        gap = second - first
        gap = jnp.where(gap < 0, gap + S, gap)
        place = jnp.where(gap <= S // 2, gap * S + first, (S - gap) * S + second)
        lane = lax.broadcasted_iota(i32, (1, 128), 1)
        for start in range(0, FOLDED, 256):
            marks = [ones_where(place == lane + (start + t)) for t in (0, 128)]
            high, low = halves(mm(matrix_ref[...], jnp.concatenate(marks, axis=1)))
            folded_ref[:S, start : start + 256] = high
            folded_ref[S:, start : start + 256] = low

    out = jax.ShapeDtypeStruct((2 * S, FOLDED), bf16)
    return call(kernel, out, [VMEM], kernel_matrix, name="fold_kernel")


def split_planes(fine, coarse):
    rows = 8

    def kernel(fine_ref, coarse_ref, *refs):
        planes, coarse_out, fine_held, sems = refs[:X], refs[X], refs[X + 1], refs[X + 2]
        parts = [slice(i * rows, (i + 1) * rows) for i in range(S // rows)]
        copies = [pltpu.make_async_copy(fine_ref.at[p], fine_held.at[p], sems.at[i]) for i, p in enumerate(parts)]
        copies.append(pltpu.make_async_copy(coarse_ref, coarse_out, sems.at[len(parts)]))
        for copy in copies:
            copy.start()
        for part, copy in zip(parts, copies):
            copy.wait()
            for x in range(X):
                planes[x][part] = fine_held[part, x, :]
        copies[-1].wait()

    outs = pl.pallas_call(
        kernel,
        out_shape=[sds(S, PLANE)] * X + [sds(S, CELLS)],
        in_specs=[pl.BlockSpec(memory_space=pl.ANY)] * 2,
        out_specs=[VMEM] * (X + 1),
        scratch_shapes=[pltpu.VMEM((S, X, PLANE), f32), pltpu.SemaphoreType.DMA((1 + S // rows,))],
        compiler_params=pltpu.CompilerParams(vmem_limit_bytes=LIMIT * MIB),
        cost_estimate=COST,
        name="split_planes",
    )(fine, coarse)
    return outs[:X], outs[X]


def coagulate(folded, fields, name):
    count = len(fields)

    def kernel(matrix_ref, *refs):
        for field_ref, out_ref in zip(refs[:count], refs[count:]):
            width = field_ref.shape[1]
            for start in range(0, width, 1024):
                stop = min(start + 1024, width)
                v = field_ref[:, start:stop]
                twice = jnp.concatenate([v, v], axis=0)
                turned = [twice] + [pltpu.roll(twice, 2 * S - b, 0) for b in range(1, 8)]
                pairs = [
                    (v * turned[d % 8][d - d % 8 : d - d % 8 + S]).astype(bf16) for d in range(S // 2 + 1)
                ]
                pairs.append(jnp.zeros((FOLDED - S * (S // 2 + 1), stop - start), bf16))
                product = mm(matrix_ref[...], jnp.concatenate(pairs, axis=0))
                out_ref[:, start:stop] = product[:S] + product[S:]

    return call(
        kernel,
        [sds(*f.shape) for f in fields],
        [VMEM] * (count + 1),
        folded,
        *fields,
        name=name,
    )


def owner_and_cell(request):
    y_count = GHOSTS - 512
    none = jnp.full((1, WIDE - GHOSTS), -1, i32)
    request = jnp.concatenate([request[:, y_count:], request[:, :y_count], none], axis=1)
    owner = jnp.floor((request.astype(f32) + 0.5) * (1.0 / CELLS)).astype(i32)
    return owner, jnp.where(request < 0, -1, request - owner * CELLS)


def column_of(row):
    same = lax.broadcasted_iota(i32, (S, S), 0) == lax.broadcasted_iota(i32, (S, S), 1)
    return jnp.sum(jnp.where(same, jnp.broadcast_to(row, (S, S)), 0.0), axis=1, keepdims=True)


def pick(rows, request, shifts):
    x, y, c = lax.axis_index("x"), lax.axis_index("y"), lax.axis_index("core")
    owner, cell = owner_and_cell(request)
    cell_id = lax.broadcasted_iota(i32, (CELLS, WIDE), 0)
    product = mm(rows, ones_where(jnp.broadcast_to(cell, (CELLS, WIDE)) == cell_id))
    total = jnp.zeros((S, WIDE), f32)
    for part, (shift, mate) in zip(sums_of(product, len(shifts)), shifts):
        from_x = jnp.bitwise_and(x - shift, 3)
        source_owner = (from_x * 4 + y) * 2 + (1 - c if mate else c)
        total = total + jnp.where(owner == source_owner, part, 0.0)
    return total


def gather_first(requests, sources, shifts, row):
    count = len(sources)

    def kernel(*refs):
        request_refs, source_refs, (out_ref, rows_ref, request_out) = refs[:2], refs[2 : 2 + count], refs[2 + count :]
        for i in range(4):
            at = i % 2 * (SPREAD // 2)
            request_out[i : i + 1, :] = request_refs[i // 2][at : at + 1, :]
        for i, ref in enumerate(source_refs):
            high, low = halves(ref[...])
            rows_ref[2 * S * i : 2 * S * i + S] = high
            rows_ref[2 * S * i + S : 2 * S * (i + 1)] = low
        out_ref[...] = pick(rows_ref[...], request_out[row : row + 1, :], shifts)

    return call(
        kernel,
        [
            sds(S, WIDE),
            jax.ShapeDtypeStruct((2 * S * count, CELLS), bf16),
            jax.ShapeDtypeStruct((4, GHOSTS), i32),
        ],
        [VMEM] * (2 + count),
        *requests,
        *sources,
        name="gather_first",
    )


def gather_next(requests, rows, shifts, row, name):
    def kernel(request_ref, rows_ref, out_ref):
        out_ref[...] = pick(rows_ref[...], request_ref[row : row + 1, :], shifts)

    return call(kernel, sds(S, WIDE), [VMEM] * 2, requests, rows, name=name)


def cells_by_row(requests):
    def kernel(request_a, request_b, out_ref):
        for i in range(8):
            cell = owner_and_cell((request_a if i < 4 else request_b)[i % 4 : i % 4 + 1, :])[1].astype(f32)
            for t in range(WIDE // 128):
                block = jnp.broadcast_to(cell[:, t * 128 : (t + 1) * 128], (128, 128))
                out_ref[i * WIDE + t * 128 : i * WIDE + (t + 1) * 128, :] = block.T.astype(i32)

    out = jax.ShapeDtypeStruct((8 * WIDE, 128), i32)
    return call(kernel, out, [VMEM] * 2, *requests, name="cells_by_row")


def scatter_columns(requests, cells, registers, steps, name):
    total = 8 * WIDE

    def kernel(request_a, request_b, cell_ref, *refs):
        register_refs, outs, rows_ref = refs[:8], refs[8:-1], refs[-1]
        x, y, c = lax.axis_index("x"), lax.axis_index("y"), lax.axis_index("core")
        lane = lax.broadcasted_iota(i32, (1, 128), 1)
        for i in range(8):
            request = (request_a if i < 4 else request_b)[i % 4 : i % 4 + 1, :]
            owner, _ = owner_and_cell(request)
            high, low = halves(register_refs[i][...])
            for k, step in enumerate(steps):
                to_x = jnp.bitwise_and(x + step, 3)
                mine = jnp.broadcast_to(jnp.where(owner == (to_x * 4 + y) * 2 + c, 1.0, 0.0).astype(bf16), (S, WIDE))
                rows_ref[2 * S * k : 2 * S * k + S, i * WIDE : (i + 1) * WIDE] = high * mine
                rows_ref[2 * S * k + S : 2 * S * (k + 1), i * WIDE : (i + 1) * WIDE] = low * mine

        def block(start, width):
            marks = [ones_where(cell_ref[...] == lane + (start + 128 * t)) for t in range(width // 128)]
            return sums_of(mm(rows_ref[...], jnp.concatenate(marks, axis=1)), len(steps))

        def body(i, carry):
            start = pl.multiple_of(i * 256, 256)
            for out, part in zip(outs, block(start, 256)):
                out[:, pl.ds(start, 256)] = part
            return carry

        lax.fori_loop(0, 4, body, 0)
        for out, part in zip(outs, block(1024, 128)):
            out[:, 1024:CELLS] = part

    return call(
        kernel,
        [sds(S, CELLS)] * len(steps),
        [VMEM] * 11,
        *requests,
        cells,
        *registers,
        scratch=[pltpu.VMEM((2 * S * len(steps), total), bf16)],
        name=name,
    )


def box_facts(levels_ref):
    box = lax.axis_index("box")
    last = 7
    own = levels_ref[0, box]
    use_low = (box > 0) & (levels_ref[0, jnp.maximum(box - 1, 0)] == own)
    use_high = (box < last) & (levels_ref[0, jnp.minimum(box + 1, last)] == own)
    factor = lax.shift_left(1, own).astype(f32)
    return use_low, use_high, factor


def laplacian(planes, lower, upper, y_ghosts):
    rows = planes[0].shape[0]
    z = jnp.bitwise_and(lax.broadcasted_iota(i32, (rows, PLANE), 1), 31)
    wide = lax.broadcasted_iota(i32, (rows, 128), 1)
    result = []
    for x in range(X):
        v = planes[x]
        ghost = y_ghosts[x // 2]
        before_y = pltpu.roll(v, 32, 1)
        after_y = pltpu.roll(v, PLANE - 32, 1)
        before_y = jnp.concatenate(
            [jnp.where(wide < 32, ghost[:, :128], before_y[:, :128]), before_y[:, 128:]], axis=1
        )
        after_y = jnp.concatenate(
            [after_y[:, :896], jnp.where(wide >= 96, ghost[:, 128:], after_y[:, 896:])], axis=1
        )
        before_z = jnp.where(z == 0, v, pltpu.roll(v, 1, 1))
        after_z = jnp.where(z == 31, v, pltpu.roll(v, PLANE - 1, 1))
        before_x = planes[x - 1] if x > 0 else lower
        after_x = planes[x + 1] if x < X - 1 else upper
        result.append(before_x + after_x + before_y + after_y + before_z + after_z - 6.0 * v)
    return result


def y_code(shape, lane_dim, row_dim, half):
    lane = lax.broadcasted_iota(i32, shape, lane_dim)
    row = lax.broadcasted_iota(i32, shape, row_dim)
    fine = jnp.where(lane < 32, lane, lane - 192)
    code = jnp.where(lane < 32, half * 16 + (lane >> 1), 32 + half * 16 + ((lane - 224) >> 1))
    return ones_where((code == row) & ((lane < 32) | (lane >= 224)))


def x_code(shape, lane_dim, row_dim):
    lane = lax.broadcasted_iota(i32, shape, lane_dim)
    row = lax.broadcasted_iota(i32, shape, row_dim)
    return ones_where((((lane >> 6) << 4) | ((lane >> 1) & 15)) == row)


def first_stage(levels, diffusion, planes, growth, strips, below_plane, above_plane):
    def kernel(levels_ref, diffusion_ref, *refs):
        plane_refs, growth_refs, strip_refs = refs[:4], refs[4:8], refs[8:12]
        lower_ref, upper_ref = refs[12:14]
        middle_refs, base_refs = refs[14:18], refs[18:22]
        registers_ref, x_low_ref, x_high_ref = refs[22:25]
        y_refs = refs[25:27]
        use_low, use_high, factor = box_facts(levels_ref)
        diffusion_column = column_of(diffusion_ref[...])
        strip = strip_refs[0][...] + strip_refs[1][...] + strip_refs[2][...] + strip_refs[3][...]
        x_low, x_high = sums_of(mm(rows_of([strip[:, :256], strip[:, 256:512]]), x_code((256, PLANE), 1, 0)), 2)
        y_rows = rows_of([strip[:, 512:640]])
        y_ghosts = [sums_of(mm(y_rows, y_code((128, 256), 1, 0, half)), 1)[0] for half in range(2)]
        x_low_ref[...] = x_low
        x_high_ref[...] = x_high
        for ref, ghost in zip(y_refs, y_ghosts):
            ref[...] = ghost
        lower = jnp.where(use_low, lower_ref[...], x_low)
        upper = jnp.where(use_high, upper_ref[...], x_high)
        values = [ref[...] for ref in plane_refs]
        spread = laplacian(values, lower, upper, y_ghosts)
        means = []
        for x in range(X):
            rate = (factor * diffusion_column) * spread[x] + STEP * growth_refs[x][...]
            middle = values[x] + rate
            middle_refs[x][...] = middle
            base_refs[x][...] = values[x] + 0.5 * rate
            means.append(0.5 * (values[x] + middle))
        x_below = sums_of(mm(rows_of([means[0], means[3]]), x_code((PLANE, 256), 0, 1)), 2)
        y_below = jnp.zeros((S, 128), f32)
        for half in range(2):
            both = means[2 * half] + means[2 * half + 1]
            ends = jnp.concatenate([both[:, :128], both[:, 896:]], axis=1)
            y_below = y_below + sums_of(mm(rows_of([ends]), y_code((256, 128), 0, 1, half)), 1)[0]
        below = 0.25 * jnp.concatenate(x_below + [y_below], axis=1)
        column = lax.broadcasted_iota(i32, (1, WIDE), 1)
        keep_low = jnp.where(use_low, 0.0, 1.0)
        keep_high = jnp.where(use_high, 0.0, 1.0)
        keep = jnp.where(column < 256, keep_low, jnp.where(column < 512, keep_high, 1.0))
        registers_ref[...] = ((factor - 1.0) * diffusion_column) * (strip - below) * keep

    outs = call(
        kernel,
        [sds(S, PLANE)] * 8 + [sds(S, WIDE)] + [sds(S, PLANE)] * 2 + [sds(S, 256)] * 2,
        [SMEM] + [VMEM] * 15,
        levels,
        diffusion,
        *planes,
        *growth,
        *strips,
        below_plane,
        above_plane,
        name="first_stage",
    )
    return outs[:4], outs[4:8], outs[8], outs[9:11], outs[11:13]


def second_stage(levels, diffusion, middle, base, growth, x_ghosts, y_ghosts, below_plane, above_plane):
    rows = 8

    def kernel(levels_ref, diffusion_ref, *refs):
        middle_refs, base_refs, growth_refs = refs[:4], refs[4:8], refs[8:12]
        x_low_ref, x_high_ref, y_a, y_b, lower_ref, upper_ref, out_ref, held_ref, sems = refs[12:]
        use_low, use_high, factor = box_facts(levels_ref)
        scale = factor * column_of(diffusion_ref[...])
        copies = []
        for i in range(S // rows):
            part = slice(i * rows, (i + 1) * rows)
            lower = jnp.where(use_low, lower_ref[part], x_low_ref[part])
            upper = jnp.where(use_high, upper_ref[part], x_high_ref[part])
            spread = laplacian([ref[part] for ref in middle_refs], lower, upper, [y_a[part], y_b[part]])
            for x in range(X):
                rate = scale[part] * spread[x] + STEP * growth_refs[x][part]
                held_ref[part, x, :] = base_refs[x][part] + 0.5 * rate
            copies.append(pltpu.make_async_copy(held_ref.at[part], out_ref.at[part], sems.at[i]))
            copies[-1].start()
        for copy in copies:
            copy.wait()

    return pl.pallas_call(
        kernel,
        out_shape=sds(S, X, PLANE),
        in_specs=[SMEM] + [VMEM] * 19,
        out_specs=pl.BlockSpec(memory_space=pl.ANY),
        scratch_shapes=[pltpu.VMEM((S, X, PLANE), f32), pltpu.SemaphoreType.DMA((S // rows,))],
        compiler_params=pltpu.CompilerParams(vmem_limit_bytes=40 * MIB),
        cost_estimate=COST,
        name="second_stage",
    )(levels, diffusion, *middle, *base, *growth, *x_ghosts, *y_ghosts, below_plane, above_plane)


def finish_coarse(coarse, growth, parts):
    def kernel(coarse_ref, growth_ref, a, b, c, d, out_ref):
        total = (a[...] + b[...]) + (c[...] + d[...])
        out_ref[...] = coarse_ref[...] + STEP * growth_ref[...] - total

    return call(kernel, sds(S, CELLS), [VMEM] * 6, coarse, growth, *parts, name="finish_coarse")


def shifted(value, axis, shift):
    size = lax.axis_size(axis)
    return lax.ppermute(value, axis, [(i, (i + shift) % size) for i in range(size)])


def after(value, before):
    return lax.optimization_barrier((value, before))[0]


def on_device(fine_state, coarse_state, coag_kernel, diffusion, levels, ghost_src):
    fine = fine_state[0, 0]
    coarse = coarse_state[0, 0]
    row = diffusion.reshape(1, S)
    request = ghost_src[0]

    far = {k: shifted(coarse, "x", k) for k in (2, 1, 3)}
    spread = request + jnp.zeros((SPREAD, 1), i32)
    near = shifted(spread, "y", 1)
    mate = shifted(coarse, "core", 1)
    folded = fold_kernel(coag_kernel)
    near, folded = lax.optimization_barrier((near, folded))
    requests = jnp.concatenate([spread[: SPREAD // 2], near[: SPREAD // 2]], axis=0)
    requests = [requests, shifted(requests, "y", 2)]
    planes, held_coarse = split_planes(fine, after(coarse, (folded, requests[0])))
    below_plane, above_plane = shifted(planes[3], "box", 1), shifted(planes[0], "box", 7)
    far, requests, held_coarse = lax.optimization_barrier((far, requests, held_coarse))

    sources, shifts = [held_coarse, mate], [(0, False), (0, True)]
    for k in (1, 3, 2):
        sources += [far[k], shifted(far[k], "core", 1)]
        shifts += [(k, False), (k, True)]
    part, strips = {}, {}
    part[2], rows, request_rows = gather_first(requests, sources, shifts, 2)
    strips[2] = shifted(part[2], "y", 2)
    part[1] = gather_next(request_rows, rows, shifts, 1, "gather_one")
    strips[1] = shifted(part[1], "y", 3)
    part[3] = gather_next(after(request_rows, part[1]), rows, shifts, 3, "gather_three")
    strips[3] = shifted(part[3], "y", 1)
    strips[0] = gather_next(after(request_rows, (part[3], strips[2])), rows, shifts, 0, "gather_own")
    growth = coagulate(after(folded, (strips[0], strips[1], below_plane, above_plane)), planes, "coagulate_fine")
    mate_rows = shifted(request_rows, "core", 1)
    strips, growth, mate_rows = lax.optimization_barrier((strips, growth, mate_rows))
    strips = [strips[k] for k in range(4)]

    middle, base, registers, x_ghosts, y_ghosts = first_stage(
        levels, row, planes, growth, strips, below_plane, above_plane
    )

    held = {k: shifted(registers, "y", k) for k in (2, 1, 3)}
    held[0] = registers
    cells = cells_by_row([request_rows, after(mate_rows, registers)])
    below_plane, above_plane = shifted(middle[3], "box", 1), shifted(middle[0], "box", 7)
    growth = coagulate(after(folded, cells), middle, "coagulate_middle")
    held = [after(held[k], growth[0]) for k in range(4)]
    held += [shifted(value, "core", 1) for value in held]
    cells = after(cells, (below_plane, above_plane))
    sent = {}
    both = scatter_columns([request_rows, mate_rows], cells, held, (2, 1), "scatter_far")
    sent[2], sent[1] = shifted(both[0], "x", 2), shifted(both[1], "x", 1)
    both = scatter_columns([request_rows, mate_rows], after(cells, both[0]), held, (3, 0), "scatter_near")
    sent[3], sent[0] = shifted(both[0], "x", 3), both[1]
    base = after(base, (both[0], sent[1], sent[2]))
    fine_out = second_stage(levels, row, middle, base, growth, x_ghosts, y_ghosts, below_plane, above_plane)
    coarse_growth = coagulate(after(folded, fine_out), [held_coarse], "coagulate_coarse")[0]
    sent = [sent[k] for k in range(4)]
    sent, fine_out, coarse_growth = lax.optimization_barrier((sent, fine_out, coarse_growth))
    coarse_out = finish_coarse(held_coarse, coarse_growth, sent)
    return fine_out[None, None], coarse_out[None, None]


def solution(mesh):
    group = ("x", "y", "core")
    split = Mesh(mesh.devices.reshape(4, 4, 2, 8), group + ("box",))
    return jax.shard_map(
        on_device,
        mesh=split,
        in_specs=(
            P(group, "box", None, None, None),
            P(group, "box", None, None),
            P(),
            P(),
            P(group, None),
            P(group, "box", None),
        ),
        out_specs=(P(group, "box", None, None, None), P(group, "box", None, None)),
        check_vma=False,
    )
```

```python
import jax
import jax.numpy as jnp
from jax import lax
from jax.experimental import pallas as pl
from jax.experimental.pallas import tpu as pltpu
from jax.sharding import Mesh, PartitionSpec as P

S = 48
X = 4
PLANE = 1024
CELLS = 1152
GHOSTS = 576
WIDE = 640
STEP = 0.25
FOLDED = 1280
MIB = 1024 * 1024
LIMIT = 60
SPREAD = 24
COST = pl.CostEstimate(flops=0, bytes_accessed=0, transcendentals=0)

f32 = jnp.float32
bf16 = jnp.bfloat16
i32 = jnp.int32
VMEM = pl.BlockSpec(memory_space=pltpu.VMEM)
SMEM = pl.BlockSpec(memory_space=pltpu.SMEM)


def sds(*shape):
    return jax.ShapeDtypeStruct(shape, f32)


def call(kernel, out_shape, in_specs, *operands, scratch=(), name=None):
    many = isinstance(out_shape, list)
    return pl.pallas_call(
        kernel,
        out_shape=out_shape,
        in_specs=in_specs,
        out_specs=[VMEM] * len(out_shape) if many else VMEM,
        scratch_shapes=list(scratch),
        compiler_params=pltpu.CompilerParams(vmem_limit_bytes=40 * MIB),
        cost_estimate=COST,
        name=name,
    )(*operands)


def mm(a, b):
    return jnp.dot(a, b, preferred_element_type=f32)


def halves(value):
    high = value.astype(bf16)
    return high, (value - high.astype(f32)).astype(bf16)


def rows_of(values):
    parts = []
    for value in values:
        parts.extend(halves(value))
    return jnp.concatenate(parts, axis=0)


def sums_of(product, count):
    return [product[2 * S * i : 2 * S * i + S] + product[2 * S * i + S : 2 * S * (i + 1)] for i in range(count)]


def ones_where(mask):
    return jnp.where(mask, 1.0, 0.0).astype(bf16)


def fold_kernel(kernel_matrix):
    pairs = S * S

    def kernel(matrix_ref, folded_ref):
        pair = lax.broadcasted_iota(i32, (pairs, 128), 0)
        first = (pair * 43691) >> 21
        second = pair - first * S
        gap = second - first
        gap = jnp.where(gap < 0, gap + S, gap)
        place = jnp.where(gap <= S // 2, gap * S + first, (S - gap) * S + second)
        lane = lax.broadcasted_iota(i32, (1, 128), 1)
        for start in range(0, FOLDED, 256):
            marks = [ones_where(place == lane + (start + t)) for t in (0, 128)]
            high, low = halves(mm(matrix_ref[...], jnp.concatenate(marks, axis=1)))
            folded_ref[:S, start : start + 256] = high
            folded_ref[S:, start : start + 256] = low

    out = jax.ShapeDtypeStruct((2 * S, FOLDED), bf16)
    return call(kernel, out, [VMEM], kernel_matrix, name="fold_kernel")


def split_planes(fine, coarse):
    rows = 8

    def kernel(fine_ref, coarse_ref, *refs):
        planes, coarse_out, fine_held, sems = refs[:X], refs[X], refs[X + 1], refs[X + 2]
        parts = [slice(i * rows, (i + 1) * rows) for i in range(S // rows)]
        copies = [pltpu.make_async_copy(fine_ref.at[p], fine_held.at[p], sems.at[i]) for i, p in enumerate(parts)]
        copies.append(pltpu.make_async_copy(coarse_ref, coarse_out, sems.at[len(parts)]))
        for copy in copies:
            copy.start()
        for part, copy in zip(parts, copies):
            copy.wait()
            for x in range(X):
                planes[x][part] = fine_held[part, x, :]
        copies[-1].wait()

    outs = pl.pallas_call(
        kernel,
        out_shape=[sds(S, PLANE)] * X + [sds(S, CELLS)],
        in_specs=[pl.BlockSpec(memory_space=pl.ANY)] * 2,
        out_specs=[VMEM] * (X + 1),
        scratch_shapes=[pltpu.VMEM((S, X, PLANE), f32), pltpu.SemaphoreType.DMA((1 + S // rows,))],
        compiler_params=pltpu.CompilerParams(vmem_limit_bytes=LIMIT * MIB),
        cost_estimate=COST,
        name="split_planes",
    )(fine, coarse)
    return outs[:X], outs[X]


def coagulate(folded, fields, name):
    count = len(fields)

    def kernel(matrix_ref, *refs):
        for field_ref, out_ref in zip(refs[:count], refs[count:]):
            width = field_ref.shape[1]
            for start in range(0, width, 1024):
                stop = min(start + 1024, width)
                v = field_ref[:, start:stop]
                twice = jnp.concatenate([v, v], axis=0)
                turned = [twice] + [pltpu.roll(twice, 2 * S - b, 0) for b in range(1, 8)]
                pairs = [
                    (v * turned[d % 8][d - d % 8 : d - d % 8 + S]).astype(bf16) for d in range(S // 2 + 1)
                ]
                pairs.append(jnp.zeros((FOLDED - S * (S // 2 + 1), stop - start), bf16))
                product = mm(matrix_ref[...], jnp.concatenate(pairs, axis=0))
                out_ref[:, start:stop] = product[:S] + product[S:]

    return call(
        kernel,
        [sds(*f.shape) for f in fields],
        [VMEM] * (count + 1),
        folded,
        *fields,
        name=name,
    )


def owner_and_cell(request):
    y_count = GHOSTS - 512
    none = jnp.full((1, WIDE - GHOSTS), -1, i32)
    request = jnp.concatenate([request[:, y_count:], request[:, :y_count], none], axis=1)
    owner = jnp.floor((request.astype(f32) + 0.5) * (1.0 / CELLS)).astype(i32)
    return owner, jnp.where(request < 0, -1, request - owner * CELLS)


def column_of(row):
    same = lax.broadcasted_iota(i32, (S, S), 0) == lax.broadcasted_iota(i32, (S, S), 1)
    return jnp.sum(jnp.where(same, jnp.broadcast_to(row, (S, S)), 0.0), axis=1, keepdims=True)


def pick(rows, request, shifts):
    x, y, c = lax.axis_index("x"), lax.axis_index("y"), lax.axis_index("core")
    owner, cell = owner_and_cell(request)
    cell_id = lax.broadcasted_iota(i32, (CELLS, WIDE), 0)
    product = mm(rows, ones_where(jnp.broadcast_to(cell, (CELLS, WIDE)) == cell_id))
    total = jnp.zeros((S, WIDE), f32)
    for part, (shift, mate) in zip(sums_of(product, len(shifts)), shifts):
        from_x = jnp.bitwise_and(x - shift, 3)
        source_owner = (from_x * 4 + y) * 2 + (1 - c if mate else c)
        total = total + jnp.where(owner == source_owner, part, 0.0)
    return total


def gather_first(requests, sources, shifts, row):
    count = len(sources)

    def kernel(*refs):
        request_refs, source_refs, (out_ref, rows_ref, request_out) = refs[:2], refs[2 : 2 + count], refs[2 + count :]
        for i in range(4):
            at = i % 2 * (SPREAD // 2)
            request_out[i : i + 1, :] = request_refs[i // 2][at : at + 1, :]
        for i, ref in enumerate(source_refs):
            high, low = halves(ref[...])
            rows_ref[2 * S * i : 2 * S * i + S] = high
            rows_ref[2 * S * i + S : 2 * S * (i + 1)] = low
        out_ref[...] = pick(rows_ref[...], request_out[row : row + 1, :], shifts)

    return call(
        kernel,
        [
            sds(S, WIDE),
            jax.ShapeDtypeStruct((2 * S * count, CELLS), bf16),
            jax.ShapeDtypeStruct((4, GHOSTS), i32),
        ],
        [VMEM] * (2 + count),
        *requests,
        *sources,
        name="gather_first",
    )


def gather_next(requests, rows, shifts, row, name):
    def kernel(request_ref, rows_ref, out_ref):
        out_ref[...] = pick(rows_ref[...], request_ref[row : row + 1, :], shifts)

    return call(kernel, sds(S, WIDE), [VMEM] * 2, requests, rows, name=name)


def cells_by_row(requests):
    def kernel(request_a, request_b, out_ref):
        for i in range(8):
            cell = owner_and_cell((request_a if i < 4 else request_b)[i % 4 : i % 4 + 1, :])[1].astype(f32)
            for t in range(WIDE // 128):
                block = jnp.broadcast_to(cell[:, t * 128 : (t + 1) * 128], (128, 128))
                out_ref[i * WIDE + t * 128 : i * WIDE + (t + 1) * 128, :] = block.T.astype(i32)

    out = jax.ShapeDtypeStruct((8 * WIDE, 128), i32)
    return call(kernel, out, [VMEM] * 2, *requests, name="cells_by_row")


def scatter_columns(requests, cells, registers, steps, name):
    total = 8 * WIDE

    def kernel(request_a, request_b, cell_ref, *refs):
        register_refs, outs, rows_ref = refs[:8], refs[8:-1], refs[-1]
        x, y, c = lax.axis_index("x"), lax.axis_index("y"), lax.axis_index("core")
        lane = lax.broadcasted_iota(i32, (1, 128), 1)
        for i in range(8):
            request = (request_a if i < 4 else request_b)[i % 4 : i % 4 + 1, :]
            owner, _ = owner_and_cell(request)
            high, low = halves(register_refs[i][...])
            for k, step in enumerate(steps):
                to_x = jnp.bitwise_and(x + step, 3)
                mine = jnp.broadcast_to(jnp.where(owner == (to_x * 4 + y) * 2 + c, 1.0, 0.0).astype(bf16), (S, WIDE))
                rows_ref[2 * S * k : 2 * S * k + S, i * WIDE : (i + 1) * WIDE] = high * mine
                rows_ref[2 * S * k + S : 2 * S * (k + 1), i * WIDE : (i + 1) * WIDE] = low * mine

        def block(start, width):
            marks = [ones_where(cell_ref[...] == lane + (start + 128 * t)) for t in range(width // 128)]
            return sums_of(mm(rows_ref[...], jnp.concatenate(marks, axis=1)), len(steps))

        def body(i, carry):
            start = pl.multiple_of(i * 256, 256)
            for out, part in zip(outs, block(start, 256)):
                out[:, pl.ds(start, 256)] = part
            return carry

        lax.fori_loop(0, 4, body, 0)
        for out, part in zip(outs, block(1024, 128)):
            out[:, 1024:CELLS] = part

    return call(
        kernel,
        [sds(S, CELLS)] * len(steps),
        [VMEM] * 11,
        *requests,
        cells,
        *registers,
        scratch=[pltpu.VMEM((2 * S * len(steps), total), bf16)],
        name=name,
    )


def box_facts(levels_ref):
    box = lax.axis_index("box")
    last = 7
    own = levels_ref[0, box]
    use_low = (box > 0) & (levels_ref[0, jnp.maximum(box - 1, 0)] == own)
    use_high = (box < last) & (levels_ref[0, jnp.minimum(box + 1, last)] == own)
    factor = lax.shift_left(1, own).astype(f32)
    return use_low, use_high, factor


def laplacian(planes, lower, upper, y_ghosts):
    rows = planes[0].shape[0]
    z = jnp.bitwise_and(lax.broadcasted_iota(i32, (rows, PLANE), 1), 31)
    wide = lax.broadcasted_iota(i32, (rows, 128), 1)
    result = []
    for x in range(X):
        v = planes[x]
        ghost = y_ghosts[x // 2]
        before_y = pltpu.roll(v, 32, 1)
        after_y = pltpu.roll(v, PLANE - 32, 1)
        before_y = jnp.concatenate(
            [jnp.where(wide < 32, ghost[:, :128], before_y[:, :128]), before_y[:, 128:]], axis=1
        )
        after_y = jnp.concatenate(
            [after_y[:, :896], jnp.where(wide >= 96, ghost[:, 128:], after_y[:, 896:])], axis=1
        )
        before_z = jnp.where(z == 0, v, pltpu.roll(v, 1, 1))
        after_z = jnp.where(z == 31, v, pltpu.roll(v, PLANE - 1, 1))
        before_x = planes[x - 1] if x > 0 else lower
        after_x = planes[x + 1] if x < X - 1 else upper
        result.append(before_x + after_x + before_y + after_y + before_z + after_z - 6.0 * v)
    return result


def y_code(shape, lane_dim, row_dim, half):
    lane = lax.broadcasted_iota(i32, shape, lane_dim)
    row = lax.broadcasted_iota(i32, shape, row_dim)
    fine = jnp.where(lane < 32, lane, lane - 192)
    code = jnp.where(lane < 32, half * 16 + (lane >> 1), 32 + half * 16 + ((lane - 224) >> 1))
    return ones_where((code == row) & ((lane < 32) | (lane >= 224)))


def x_code(shape, lane_dim, row_dim):
    lane = lax.broadcasted_iota(i32, shape, lane_dim)
    row = lax.broadcasted_iota(i32, shape, row_dim)
    return ones_where((((lane >> 6) << 4) | ((lane >> 1) & 15)) == row)


def first_stage(levels, diffusion, planes, growth, strips, below_plane, above_plane):
    def kernel(levels_ref, diffusion_ref, *refs):
        plane_refs, growth_refs, strip_refs = refs[:4], refs[4:8], refs[8:12]
        lower_ref, upper_ref = refs[12:14]
        middle_refs, base_refs = refs[14:18], refs[18:22]
        registers_ref, x_low_ref, x_high_ref = refs[22:25]
        y_refs = refs[25:27]
        use_low, use_high, factor = box_facts(levels_ref)
        diffusion_column = column_of(diffusion_ref[...])
        strip = strip_refs[0][...] + strip_refs[1][...] + strip_refs[2][...] + strip_refs[3][...]
        x_low, x_high = sums_of(mm(rows_of([strip[:, :256], strip[:, 256:512]]), x_code((256, PLANE), 1, 0)), 2)
        y_rows = rows_of([strip[:, 512:640]])
        y_ghosts = [sums_of(mm(y_rows, y_code((128, 256), 1, 0, half)), 1)[0] for half in range(2)]
        x_low_ref[...] = x_low
        x_high_ref[...] = x_high
        for ref, ghost in zip(y_refs, y_ghosts):
            ref[...] = ghost
        lower = jnp.where(use_low, lower_ref[...], x_low)
        upper = jnp.where(use_high, upper_ref[...], x_high)
        values = [ref[...] for ref in plane_refs]
        spread = laplacian(values, lower, upper, y_ghosts)
        means = []
        for x in range(X):
            rate = (factor * diffusion_column) * spread[x] + STEP * growth_refs[x][...]
            middle = values[x] + rate
            middle_refs[x][...] = middle
            base_refs[x][...] = values[x] + 0.5 * rate
            means.append(0.5 * (values[x] + middle))
        x_below = sums_of(mm(rows_of([means[0], means[3]]), x_code((PLANE, 256), 0, 1)), 2)
        y_below = jnp.zeros((S, 128), f32)
        for half in range(2):
            both = means[2 * half] + means[2 * half + 1]
            ends = jnp.concatenate([both[:, :128], both[:, 896:]], axis=1)
            y_below = y_below + sums_of(mm(rows_of([ends]), y_code((256, 128), 0, 1, half)), 1)[0]
        below = 0.25 * jnp.concatenate(x_below + [y_below], axis=1)
        column = lax.broadcasted_iota(i32, (1, WIDE), 1)
        keep_low = jnp.where(use_low, 0.0, 1.0)
        keep_high = jnp.where(use_high, 0.0, 1.0)
        keep = jnp.where(column < 256, keep_low, jnp.where(column < 512, keep_high, 1.0))
        registers_ref[...] = ((factor - 1.0) * diffusion_column) * (strip - below) * keep

    outs = call(
        kernel,
        [sds(S, PLANE)] * 8 + [sds(S, WIDE)] + [sds(S, PLANE)] * 2 + [sds(S, 256)] * 2,
        [SMEM] + [VMEM] * 15,
        levels,
        diffusion,
        *planes,
        *growth,
        *strips,
        below_plane,
        above_plane,
        name="first_stage",
    )
    return outs[:4], outs[4:8], outs[8], outs[9:11], outs[11:13]


def second_stage(levels, diffusion, middle, base, growth, x_ghosts, y_ghosts, below_plane, above_plane):
    rows = 8

    def kernel(levels_ref, diffusion_ref, *refs):
        middle_refs, base_refs, growth_refs = refs[:4], refs[4:8], refs[8:12]
        x_low_ref, x_high_ref, y_a, y_b, lower_ref, upper_ref, out_ref, held_ref, sems = refs[12:]
        use_low, use_high, factor = box_facts(levels_ref)
        scale = factor * column_of(diffusion_ref[...])
        copies = []
        for i in range(S // rows):
            part = slice(i * rows, (i + 1) * rows)
            lower = jnp.where(use_low, lower_ref[part], x_low_ref[part])
            upper = jnp.where(use_high, upper_ref[part], x_high_ref[part])
            spread = laplacian([ref[part] for ref in middle_refs], lower, upper, [y_a[part], y_b[part]])
            for x in range(X):
                rate = scale[part] * spread[x] + STEP * growth_refs[x][part]
                held_ref[part, x, :] = base_refs[x][part] + 0.5 * rate
            copies.append(pltpu.make_async_copy(held_ref.at[part], out_ref.at[part], sems.at[i]))
            copies[-1].start()
        for copy in copies:
            copy.wait()

    return pl.pallas_call(
        kernel,
        out_shape=sds(S, X, PLANE),
        in_specs=[SMEM] + [VMEM] * 19,
        out_specs=pl.BlockSpec(memory_space=pl.ANY),
        scratch_shapes=[pltpu.VMEM((S, X, PLANE), f32), pltpu.SemaphoreType.DMA((S // rows,))],
        compiler_params=pltpu.CompilerParams(vmem_limit_bytes=40 * MIB),
        cost_estimate=COST,
        name="second_stage",
    )(levels, diffusion, *middle, *base, *growth, *x_ghosts, *y_ghosts, below_plane, above_plane)


def finish_coarse(coarse, growth, parts):
    def kernel(coarse_ref, growth_ref, a, b, c, d, out_ref):
        total = (a[...] + b[...]) + (c[...] + d[...])
        out_ref[...] = coarse_ref[...] + STEP * growth_ref[...] - total

    return call(kernel, sds(S, CELLS), [VMEM] * 6, coarse, growth, *parts, name="finish_coarse")


def shifted(value, axis, shift):
    size = lax.axis_size(axis)
    return lax.ppermute(value, axis, [(i, (i + shift) % size) for i in range(size)])


def after(value, before):
    return lax.optimization_barrier((value, before))[0]


def on_device(fine_state, coarse_state, coag_kernel, diffusion, levels, ghost_src):
    fine = fine_state[0, 0]
    coarse = coarse_state[0, 0]
    row = diffusion.reshape(1, S)
    request = ghost_src[0]

    far = {k: shifted(coarse, "x", k) for k in (2, 1, 3)}
    spread = request + jnp.zeros((SPREAD, 1), i32)
    near = shifted(spread, "y", 1)
    mate = shifted(coarse, "core", 1)
    folded = fold_kernel(coag_kernel)
    near, folded = lax.optimization_barrier((near, folded))
    requests = jnp.concatenate([spread[: SPREAD // 2], near[: SPREAD // 2]], axis=0)
    requests = [requests, shifted(requests, "y", 2)]
    planes, held_coarse = split_planes(fine, after(coarse, (folded, requests[0])))
    below_plane, above_plane = shifted(planes[3], "box", 1), shifted(planes[0], "box", 7)
    far, requests, held_coarse = lax.optimization_barrier((far, requests, held_coarse))

    sources, shifts = [held_coarse, mate], [(0, False), (0, True)]
    for k in (1, 3, 2):
        sources += [far[k], shifted(far[k], "core", 1)]
        shifts += [(k, False), (k, True)]
    part, strips = {}, {}
    part[2], rows, request_rows = gather_first(requests, sources, shifts, 2)
    strips[2] = shifted(part[2], "y", 2)
    part[1] = gather_next(request_rows, rows, shifts, 1, "gather_one")
    strips[1] = shifted(part[1], "y", 3)
    part[3] = gather_next(after(request_rows, part[1]), rows, shifts, 3, "gather_three")
    strips[3] = shifted(part[3], "y", 1)
    strips[0] = gather_next(after(request_rows, (part[3], strips[2])), rows, shifts, 0, "gather_own")
    growth = coagulate(after(folded, (strips[0], strips[1], below_plane, above_plane)), planes, "coagulate_fine")
    mate_rows = shifted(request_rows, "core", 1)
    strips, growth, mate_rows = lax.optimization_barrier((strips, growth, mate_rows))
    strips = [strips[k] for k in range(4)]

    middle, base, registers, x_ghosts, y_ghosts = first_stage(
        levels, row, planes, growth, strips, below_plane, above_plane
    )

    held = {k: shifted(registers, "y", k) for k in (2, 1, 3)}
    held[0] = registers
    cells = cells_by_row([request_rows, after(mate_rows, registers)])
    below_plane, above_plane = shifted(middle[3], "box", 1), shifted(middle[0], "box", 7)
    growth = coagulate(after(folded, cells), middle, "coagulate_middle")
    held = [after(held[k], growth[0]) for k in range(4)]
    held += [shifted(value, "core", 1) for value in held]
    cells = after(cells, (below_plane, above_plane))
    sent = {}
    (part,) = scatter_columns([request_rows, mate_rows], cells, held, (2,), "scatter_far")
    sent[2] = shifted(part, "x", 2)
    parts = scatter_columns([request_rows, mate_rows], after(cells, part), held, (1, 3, 0), "scatter_near")
    sent[1], sent[3], sent[0] = shifted(parts[0], "x", 1), shifted(parts[1], "x", 3), parts[2]
    base = after(base, parts[0])
    fine_out = second_stage(levels, row, middle, base, growth, x_ghosts, y_ghosts, below_plane, above_plane)
    coarse_growth = coagulate(after(folded, (fine_out, sent[2])), [held_coarse], "coagulate_coarse")[0]
    sent = [sent[k] for k in range(4)]
    sent, fine_out, coarse_growth = lax.optimization_barrier((sent, fine_out, coarse_growth))
    coarse_out = finish_coarse(held_coarse, coarse_growth, sent)
    return fine_out[None, None], coarse_out[None, None]


def solution(mesh):
    group = ("x", "y", "core")
    split = Mesh(mesh.devices.reshape(4, 4, 2, 8), group + ("box",))
    return jax.shard_map(
        on_device,
        mesh=split,
        in_specs=(
            P(group, "box", None, None, None),
            P(group, "box", None, None),
            P(),
            P(),
            P(group, None),
            P(group, "box", None),
        ),
        out_specs=(P(group, "box", None, None, None), P(group, "box", None, None)),
        check_vma=False,
    )
```

```python
import jax
import jax.numpy as jnp
from jax import lax
from jax.experimental import pallas as pl
from jax.experimental.pallas import tpu as pltpu
from jax.sharding import Mesh, PartitionSpec as P

S = 48
X = 4
PLANE = 1024
CELLS = 1152
GHOSTS = 576
WIDE = 640
STEP = 0.25
FOLDED = 1280
MIB = 1024 * 1024
LIMIT = 53
SPREAD = 24
COST = pl.CostEstimate(flops=0, bytes_accessed=0, transcendentals=0)

f32 = jnp.float32
bf16 = jnp.bfloat16
i32 = jnp.int32
VMEM = pl.BlockSpec(memory_space=pltpu.VMEM)
SMEM = pl.BlockSpec(memory_space=pltpu.SMEM)


def sds(*shape):
    return jax.ShapeDtypeStruct(shape, f32)


def call(kernel, out_shape, in_specs, *operands, scratch=(), name=None):
    many = isinstance(out_shape, list)
    return pl.pallas_call(
        kernel,
        out_shape=out_shape,
        in_specs=in_specs,
        out_specs=[VMEM] * len(out_shape) if many else VMEM,
        scratch_shapes=list(scratch),
        compiler_params=pltpu.CompilerParams(vmem_limit_bytes=40 * MIB),
        cost_estimate=COST,
        name=name,
    )(*operands)


def mm(a, b):
    return jnp.dot(a, b, preferred_element_type=f32)


def halves(value):
    high = value.astype(bf16)
    return high, (value - high.astype(f32)).astype(bf16)


def rows_of(values):
    parts = []
    for value in values:
        parts.extend(halves(value))
    return jnp.concatenate(parts, axis=0)


def sums_of(product, count):
    return [product[2 * S * i : 2 * S * i + S] + product[2 * S * i + S : 2 * S * (i + 1)] for i in range(count)]


def ones_where(mask):
    return jnp.where(mask, 1.0, 0.0).astype(bf16)


def fold_kernel(kernel_matrix):
    pairs = S * S

    def kernel(matrix_ref, folded_ref):
        pair = lax.broadcasted_iota(i32, (pairs, 128), 0)
        first = (pair * 43691) >> 21
        second = pair - first * S
        gap = second - first
        gap = jnp.where(gap < 0, gap + S, gap)
        place = jnp.where(gap <= S // 2, gap * S + first, (S - gap) * S + second)
        lane = lax.broadcasted_iota(i32, (1, 128), 1)
        for start in range(0, FOLDED, 256):
            marks = [ones_where(place == lane + (start + t)) for t in (0, 128)]
            high, low = halves(mm(matrix_ref[...], jnp.concatenate(marks, axis=1)))
            folded_ref[:S, start : start + 256] = high
            folded_ref[S:, start : start + 256] = low

    out = jax.ShapeDtypeStruct((2 * S, FOLDED), bf16)
    return call(kernel, out, [VMEM], kernel_matrix, name="fold_kernel")


def split_planes(fine, coarse):
    rows = 8

    def kernel(fine_ref, coarse_ref, *refs):
        planes, coarse_out, fine_held, sems = refs[:X], refs[X], refs[X + 1], refs[X + 2]
        parts = [slice(i * rows, (i + 1) * rows) for i in range(S // rows)]
        copies = [pltpu.make_async_copy(fine_ref.at[p], fine_held.at[p], sems.at[i]) for i, p in enumerate(parts)]
        copies.append(pltpu.make_async_copy(coarse_ref, coarse_out, sems.at[len(parts)]))
        for copy in copies:
            copy.start()
        for part, copy in zip(parts, copies):
            copy.wait()
            for x in range(X):
                planes[x][part] = fine_held[part, x, :]
        copies[-1].wait()

    outs = pl.pallas_call(
        kernel,
        out_shape=[sds(S, PLANE)] * X + [sds(S, CELLS)],
        in_specs=[pl.BlockSpec(memory_space=pl.ANY)] * 2,
        out_specs=[VMEM] * (X + 1),
        scratch_shapes=[pltpu.VMEM((S, X, PLANE), f32), pltpu.SemaphoreType.DMA((1 + S // rows,))],
        compiler_params=pltpu.CompilerParams(vmem_limit_bytes=LIMIT * MIB),
        cost_estimate=COST,
        name="split_planes",
    )(fine, coarse)
    return outs[:X], outs[X]


def coagulate(folded, fields, name):
    count = len(fields)

    def kernel(matrix_ref, *refs):
        for field_ref, out_ref in zip(refs[:count], refs[count:]):
            width = field_ref.shape[1]
            for start in range(0, width, 1024):
                stop = min(start + 1024, width)
                v = field_ref[:, start:stop]
                twice = jnp.concatenate([v, v], axis=0)
                turned = [twice] + [pltpu.roll(twice, 2 * S - b, 0) for b in range(1, 8)]
                pairs = [
                    (v * turned[d % 8][d - d % 8 : d - d % 8 + S]).astype(bf16) for d in range(S // 2 + 1)
                ]
                pairs.append(jnp.zeros((FOLDED - S * (S // 2 + 1), stop - start), bf16))
                product = mm(matrix_ref[...], jnp.concatenate(pairs, axis=0))
                out_ref[:, start:stop] = product[:S] + product[S:]

    return call(
        kernel,
        [sds(*f.shape) for f in fields],
        [VMEM] * (count + 1),
        folded,
        *fields,
        name=name,
    )


def owner_and_cell(request):
    y_count = GHOSTS - 512
    none = jnp.full((1, WIDE - GHOSTS), -1, i32)
    request = jnp.concatenate([request[:, y_count:], request[:, :y_count], none], axis=1)
    owner = jnp.floor((request.astype(f32) + 0.5) * (1.0 / CELLS)).astype(i32)
    return owner, jnp.where(request < 0, -1, request - owner * CELLS)


def column_of(row):
    same = lax.broadcasted_iota(i32, (S, S), 0) == lax.broadcasted_iota(i32, (S, S), 1)
    return jnp.sum(jnp.where(same, jnp.broadcast_to(row, (S, S)), 0.0), axis=1, keepdims=True)


def pick(rows, request, shifts):
    x, y, c = lax.axis_index("x"), lax.axis_index("y"), lax.axis_index("core")
    owner, cell = owner_and_cell(request)
    cell_id = lax.broadcasted_iota(i32, (CELLS, WIDE), 0)
    product = mm(rows, ones_where(jnp.broadcast_to(cell, (CELLS, WIDE)) == cell_id))
    total = jnp.zeros((S, WIDE), f32)
    for part, (shift, mate) in zip(sums_of(product, len(shifts)), shifts):
        from_x = jnp.bitwise_and(x - shift, 3)
        source_owner = (from_x * 4 + y) * 2 + (1 - c if mate else c)
        total = total + jnp.where(owner == source_owner, part, 0.0)
    return total


def gather_first(requests, sources, shifts, row):
    count = len(sources)

    def kernel(*refs):
        request_refs, source_refs, (out_ref, rows_ref, request_out) = refs[:2], refs[2 : 2 + count], refs[2 + count :]
        for i in range(4):
            at = i % 2 * (SPREAD // 2)
            request_out[i : i + 1, :] = request_refs[i // 2][at : at + 1, :]
        for i, ref in enumerate(source_refs):
            high, low = halves(ref[...])
            rows_ref[2 * S * i : 2 * S * i + S] = high
            rows_ref[2 * S * i + S : 2 * S * (i + 1)] = low
        out_ref[...] = pick(rows_ref[...], request_out[row : row + 1, :], shifts)

    return call(
        kernel,
        [
            sds(S, WIDE),
            jax.ShapeDtypeStruct((2 * S * count, CELLS), bf16),
            jax.ShapeDtypeStruct((4, GHOSTS), i32),
        ],
        [VMEM] * (2 + count),
        *requests,
        *sources,
        name="gather_first",
    )


def gather_next(requests, rows, shifts, row, name):
    def kernel(request_ref, rows_ref, out_ref):
        out_ref[...] = pick(rows_ref[...], request_ref[row : row + 1, :], shifts)

    return call(kernel, sds(S, WIDE), [VMEM] * 2, requests, rows, name=name)


def cells_by_row(requests):
    def kernel(request_a, request_b, out_ref):
        for i in range(8):
            cell = owner_and_cell((request_a if i < 4 else request_b)[i % 4 : i % 4 + 1, :])[1].astype(f32)
            for t in range(WIDE // 128):
                block = jnp.broadcast_to(cell[:, t * 128 : (t + 1) * 128], (128, 128))
                out_ref[i * WIDE + t * 128 : i * WIDE + (t + 1) * 128, :] = block.T.astype(i32)

    out = jax.ShapeDtypeStruct((8 * WIDE, 128), i32)
    return call(kernel, out, [VMEM] * 2, *requests, name="cells_by_row")


def scatter_columns(requests, cells, registers, steps, name):
    total = 8 * WIDE

    def kernel(request_a, request_b, cell_ref, *refs):
        register_refs, outs, rows_ref = refs[:8], refs[8:-1], refs[-1]
        x, y, c = lax.axis_index("x"), lax.axis_index("y"), lax.axis_index("core")
        lane = lax.broadcasted_iota(i32, (1, 128), 1)
        for i in range(8):
            request = (request_a if i < 4 else request_b)[i % 4 : i % 4 + 1, :]
            owner, _ = owner_and_cell(request)
            high, low = halves(register_refs[i][...])
            for k, step in enumerate(steps):
                to_x = jnp.bitwise_and(x + step, 3)
                mine = jnp.broadcast_to(jnp.where(owner == (to_x * 4 + y) * 2 + c, 1.0, 0.0).astype(bf16), (S, WIDE))
                rows_ref[2 * S * k : 2 * S * k + S, i * WIDE : (i + 1) * WIDE] = high * mine
                rows_ref[2 * S * k + S : 2 * S * (k + 1), i * WIDE : (i + 1) * WIDE] = low * mine

        def block(start, width):
            marks = [ones_where(cell_ref[...] == lane + (start + 128 * t)) for t in range(width // 128)]
            return sums_of(mm(rows_ref[...], jnp.concatenate(marks, axis=1)), len(steps))

        def body(i, carry):
            start = pl.multiple_of(i * 256, 256)
            for out, part in zip(outs, block(start, 256)):
                out[:, pl.ds(start, 256)] = part
            return carry

        lax.fori_loop(0, 4, body, 0)
        for out, part in zip(outs, block(1024, 128)):
            out[:, 1024:CELLS] = part

    return call(
        kernel,
        [sds(S, CELLS)] * len(steps),
        [VMEM] * 11,
        *requests,
        cells,
        *registers,
        scratch=[pltpu.VMEM((2 * S * len(steps), total), bf16)],
        name=name,
    )


def box_facts(levels_ref):
    box = lax.axis_index("box")
    last = 7
    own = levels_ref[0, box]
    use_low = (box > 0) & (levels_ref[0, jnp.maximum(box - 1, 0)] == own)
    use_high = (box < last) & (levels_ref[0, jnp.minimum(box + 1, last)] == own)
    factor = lax.shift_left(1, own).astype(f32)
    return use_low, use_high, factor


def laplacian(planes, lower, upper, y_ghosts):
    rows = planes[0].shape[0]
    z = jnp.bitwise_and(lax.broadcasted_iota(i32, (rows, PLANE), 1), 31)
    wide = lax.broadcasted_iota(i32, (rows, 128), 1)
    result = []
    for x in range(X):
        v = planes[x]
        ghost = y_ghosts[x // 2]
        before_y = pltpu.roll(v, 32, 1)
        after_y = pltpu.roll(v, PLANE - 32, 1)
        before_y = jnp.concatenate(
            [jnp.where(wide < 32, ghost[:, :128], before_y[:, :128]), before_y[:, 128:]], axis=1
        )
        after_y = jnp.concatenate(
            [after_y[:, :896], jnp.where(wide >= 96, ghost[:, 128:], after_y[:, 896:])], axis=1
        )
        before_z = jnp.where(z == 0, v, pltpu.roll(v, 1, 1))
        after_z = jnp.where(z == 31, v, pltpu.roll(v, PLANE - 1, 1))
        before_x = planes[x - 1] if x > 0 else lower
        after_x = planes[x + 1] if x < X - 1 else upper
        result.append(before_x + after_x + before_y + after_y + before_z + after_z - 6.0 * v)
    return result


def y_code(shape, lane_dim, row_dim, half):
    lane = lax.broadcasted_iota(i32, shape, lane_dim)
    row = lax.broadcasted_iota(i32, shape, row_dim)
    fine = jnp.where(lane < 32, lane, lane - 192)
    code = jnp.where(lane < 32, half * 16 + (lane >> 1), 32 + half * 16 + ((lane - 224) >> 1))
    return ones_where((code == row) & ((lane < 32) | (lane >= 224)))


def x_code(shape, lane_dim, row_dim):
    lane = lax.broadcasted_iota(i32, shape, lane_dim)
    row = lax.broadcasted_iota(i32, shape, row_dim)
    return ones_where((((lane >> 6) << 4) | ((lane >> 1) & 15)) == row)


def first_stage(levels, diffusion, planes, growth, strips, below_plane, above_plane):
    def kernel(levels_ref, diffusion_ref, *refs):
        plane_refs, growth_refs, strip_refs = refs[:4], refs[4:8], refs[8:12]
        lower_ref, upper_ref = refs[12:14]
        middle_refs, base_refs = refs[14:18], refs[18:22]
        registers_ref, x_low_ref, x_high_ref = refs[22:25]
        y_refs = refs[25:27]
        use_low, use_high, factor = box_facts(levels_ref)
        diffusion_column = column_of(diffusion_ref[...])
        strip = strip_refs[0][...] + strip_refs[1][...] + strip_refs[2][...] + strip_refs[3][...]
        x_low, x_high = sums_of(mm(rows_of([strip[:, :256], strip[:, 256:512]]), x_code((256, PLANE), 1, 0)), 2)
        y_rows = rows_of([strip[:, 512:640]])
        y_ghosts = [sums_of(mm(y_rows, y_code((128, 256), 1, 0, half)), 1)[0] for half in range(2)]
        x_low_ref[...] = x_low
        x_high_ref[...] = x_high
        for ref, ghost in zip(y_refs, y_ghosts):
            ref[...] = ghost
        lower = jnp.where(use_low, lower_ref[...], x_low)
        upper = jnp.where(use_high, upper_ref[...], x_high)
        values = [ref[...] for ref in plane_refs]
        spread = laplacian(values, lower, upper, y_ghosts)
        means = []
        for x in range(X):
            rate = (factor * diffusion_column) * spread[x] + STEP * growth_refs[x][...]
            middle = values[x] + rate
            middle_refs[x][...] = middle
            base_refs[x][...] = values[x] + 0.5 * rate
            means.append(0.5 * (values[x] + middle))
        x_below = sums_of(mm(rows_of([means[0], means[3]]), x_code((PLANE, 256), 0, 1)), 2)
        y_below = jnp.zeros((S, 128), f32)
        for half in range(2):
            both = means[2 * half] + means[2 * half + 1]
            ends = jnp.concatenate([both[:, :128], both[:, 896:]], axis=1)
            y_below = y_below + sums_of(mm(rows_of([ends]), y_code((256, 128), 0, 1, half)), 1)[0]
        below = 0.25 * jnp.concatenate(x_below + [y_below], axis=1)
        column = lax.broadcasted_iota(i32, (1, WIDE), 1)
        keep_low = jnp.where(use_low, 0.0, 1.0)
        keep_high = jnp.where(use_high, 0.0, 1.0)
        keep = jnp.where(column < 256, keep_low, jnp.where(column < 512, keep_high, 1.0))
        registers_ref[...] = ((factor - 1.0) * diffusion_column) * (strip - below) * keep

    outs = call(
        kernel,
        [sds(S, PLANE)] * 8 + [sds(S, WIDE)] + [sds(S, PLANE)] * 2 + [sds(S, 256)] * 2,
        [SMEM] + [VMEM] * 15,
        levels,
        diffusion,
        *planes,
        *growth,
        *strips,
        below_plane,
        above_plane,
        name="first_stage",
    )
    return outs[:4], outs[4:8], outs[8], outs[9:11], outs[11:13]


def second_stage(levels, diffusion, middle, base, growth, x_ghosts, y_ghosts, below_plane, above_plane):
    rows = 8

    def kernel(levels_ref, diffusion_ref, *refs):
        middle_refs, base_refs, growth_refs = refs[:4], refs[4:8], refs[8:12]
        x_low_ref, x_high_ref, y_a, y_b, lower_ref, upper_ref, out_ref, held_ref, sems = refs[12:]
        use_low, use_high, factor = box_facts(levels_ref)
        scale = factor * column_of(diffusion_ref[...])
        copies = []
        for i in range(S // rows):
            part = slice(i * rows, (i + 1) * rows)
            lower = jnp.where(use_low, lower_ref[part], x_low_ref[part])
            upper = jnp.where(use_high, upper_ref[part], x_high_ref[part])
            spread = laplacian([ref[part] for ref in middle_refs], lower, upper, [y_a[part], y_b[part]])
            for x in range(X):
                rate = scale[part] * spread[x] + STEP * growth_refs[x][part]
                held_ref[part, x, :] = base_refs[x][part] + 0.5 * rate
            copies.append(pltpu.make_async_copy(held_ref.at[part], out_ref.at[part], sems.at[i]))
            copies[-1].start()
        for copy in copies:
            copy.wait()

    return pl.pallas_call(
        kernel,
        out_shape=sds(S, X, PLANE),
        in_specs=[SMEM] + [VMEM] * 19,
        out_specs=pl.BlockSpec(memory_space=pl.ANY),
        scratch_shapes=[pltpu.VMEM((S, X, PLANE), f32), pltpu.SemaphoreType.DMA((S // rows,))],
        compiler_params=pltpu.CompilerParams(vmem_limit_bytes=40 * MIB),
        cost_estimate=COST,
        name="second_stage",
    )(levels, diffusion, *middle, *base, *growth, *x_ghosts, *y_ghosts, below_plane, above_plane)


def finish_coarse(coarse, growth, parts):
    def kernel(coarse_ref, growth_ref, a, b, c, d, out_ref):
        total = (a[...] + b[...]) + (c[...] + d[...])
        out_ref[...] = coarse_ref[...] + STEP * growth_ref[...] - total

    return call(kernel, sds(S, CELLS), [VMEM] * 6, coarse, growth, *parts, name="finish_coarse")


def shifted(value, axis, shift):
    size = lax.axis_size(axis)
    return lax.ppermute(value, axis, [(i, (i + shift) % size) for i in range(size)])


def after(value, before):
    return lax.optimization_barrier((value, before))[0]


def on_device(fine_state, coarse_state, coag_kernel, diffusion, levels, ghost_src):
    fine = fine_state[0, 0]
    coarse = coarse_state[0, 0]
    row = diffusion.reshape(1, S)
    request = ghost_src[0]

    far = {k: shifted(coarse, "x", k) for k in (2, 1, 3)}
    spread = request + jnp.zeros((SPREAD, 1), i32)
    near = shifted(spread, "y", 1)
    mate = shifted(coarse, "core", 1)
    folded = fold_kernel(coag_kernel)
    near, folded = lax.optimization_barrier((near, folded))
    requests = jnp.concatenate([spread[: SPREAD // 2], near[: SPREAD // 2]], axis=0)
    requests = [requests, shifted(requests, "y", 2)]
    planes, held_coarse = split_planes(fine, after(coarse, (folded, requests[0])))
    below_plane, above_plane = shifted(planes[3], "box", 1), shifted(planes[0], "box", 7)
    growth = coagulate(after(folded, held_coarse), planes, "coagulate_fine")
    far, requests, growth = lax.optimization_barrier((far, requests, growth))

    sources, shifts = [held_coarse, mate], [(0, False), (0, True)]
    for k in (1, 3, 2):
        sources += [far[k], shifted(far[k], "core", 1)]
        shifts += [(k, False), (k, True)]
    part, strips = {}, {}
    part[2], rows, request_rows = gather_first(requests, sources, shifts, 2)
    strips[2] = shifted(part[2], "y", 2)
    part[1] = gather_next(request_rows, rows, shifts, 1, "gather_one")
    strips[1] = shifted(part[1], "y", 3)
    part[3] = gather_next(after(request_rows, part[1]), rows, shifts, 3, "gather_three")
    strips[3] = shifted(part[3], "y", 1)
    strips[0] = gather_next(after(request_rows, (part[3], strips[2])), rows, shifts, 0, "gather_own")
    coarse_growth = coagulate(after(folded, (strips[0], strips[1])), [held_coarse], "coagulate_coarse")[0]
    mate_rows = shifted(request_rows, "core", 1)
    strips, coarse_growth, mate_rows = lax.optimization_barrier((strips, coarse_growth, mate_rows))
    strips = [strips[k] for k in range(4)]

    middle, base, registers, x_ghosts, y_ghosts = first_stage(
        levels, row, planes, growth, strips, below_plane, above_plane
    )

    held = {k: shifted(registers, "y", k) for k in (2, 1, 3)}
    held[0] = registers
    cells = cells_by_row([request_rows, after(mate_rows, registers)])
    below_plane, above_plane = shifted(middle[3], "box", 1), shifted(middle[0], "box", 7)
    growth = coagulate(after(folded, cells), middle, "coagulate_middle")
    held = [after(held[k], growth[0]) for k in range(4)]
    held += [shifted(value, "core", 1) for value in held]
    cells = after(cells, (below_plane, above_plane))
    sent = {}
    (part,) = scatter_columns([request_rows, mate_rows], cells, held, (2,), "scatter_far")
    sent[2] = shifted(part, "x", 2)
    parts = scatter_columns([request_rows, mate_rows], after(cells, part), held, (1, 3, 0), "scatter_near")
    sent[1], sent[3], sent[0] = shifted(parts[0], "x", 1), shifted(parts[1], "x", 3), parts[2]
    base = after(base, (parts[0], sent[2]))
    fine_out = second_stage(levels, row, middle, base, growth, x_ghosts, y_ghosts, below_plane, above_plane)
    sent = [sent[k] for k in range(4)]
    sent, fine_out, coarse_growth = lax.optimization_barrier((sent, fine_out, coarse_growth))
    coarse_out = finish_coarse(held_coarse, coarse_growth, sent)
    return fine_out[None, None], coarse_out[None, None]


def solution(mesh):
    group = ("x", "y", "core")
    split = Mesh(mesh.devices.reshape(4, 4, 2, 8), group + ("box",))
    return jax.shard_map(
        on_device,
        mesh=split,
        in_specs=(
            P(group, "box", None, None, None),
            P(group, "box", None, None),
            P(),
            P(),
            P(group, None),
            P(group, "box", None),
        ),
        out_specs=(P(group, "box", None, None, None), P(group, "box", None, None)),
        check_vma=False,
    )
```

```python
import jax
import jax.numpy as jnp
from jax import lax
from jax.experimental import pallas as pl
from jax.experimental.pallas import tpu as pltpu
from jax.sharding import Mesh, PartitionSpec as P

S = 48
X = 4
PLANE = 1024
CELLS = 1152
GHOSTS = 576
WIDE = 640
STEP = 0.25
FOLDED = 1280
MIB = 1024 * 1024
LIMIT = 53
SPREAD = 24
COST = pl.CostEstimate(flops=0, bytes_accessed=0, transcendentals=0)

f32 = jnp.float32
bf16 = jnp.bfloat16
i32 = jnp.int32
VMEM = pl.BlockSpec(memory_space=pltpu.VMEM)
SMEM = pl.BlockSpec(memory_space=pltpu.SMEM)


def sds(*shape):
    return jax.ShapeDtypeStruct(shape, f32)


def call(kernel, out_shape, in_specs, *operands, scratch=(), name=None):
    many = isinstance(out_shape, list)
    return pl.pallas_call(
        kernel,
        out_shape=out_shape,
        in_specs=in_specs,
        out_specs=[VMEM] * len(out_shape) if many else VMEM,
        scratch_shapes=list(scratch),
        compiler_params=pltpu.CompilerParams(vmem_limit_bytes=40 * MIB),
        cost_estimate=COST,
        name=name,
    )(*operands)


def mm(a, b):
    return jnp.dot(a, b, preferred_element_type=f32)


def halves(value):
    high = value.astype(bf16)
    return high, (value - high.astype(f32)).astype(bf16)


def rows_of(values):
    parts = []
    for value in values:
        parts.extend(halves(value))
    return jnp.concatenate(parts, axis=0)


def sums_of(product, count):
    return [product[2 * S * i : 2 * S * i + S] + product[2 * S * i + S : 2 * S * (i + 1)] for i in range(count)]


def ones_where(mask):
    return jnp.where(mask, 1.0, 0.0).astype(bf16)


def fold_kernel(kernel_matrix):
    pairs = S * S

    def kernel(matrix_ref, folded_ref):
        pair = lax.broadcasted_iota(i32, (pairs, 128), 0)
        first = (pair * 43691) >> 21
        second = pair - first * S
        gap = second - first
        gap = jnp.where(gap < 0, gap + S, gap)
        place = jnp.where(gap <= S // 2, gap * S + first, (S - gap) * S + second)
        lane = lax.broadcasted_iota(i32, (1, 128), 1)
        for start in range(0, FOLDED, 256):
            marks = [ones_where(place == lane + (start + t)) for t in (0, 128)]
            high, low = halves(mm(matrix_ref[...], jnp.concatenate(marks, axis=1)))
            folded_ref[:S, start : start + 256] = high
            folded_ref[S:, start : start + 256] = low

    out = jax.ShapeDtypeStruct((2 * S, FOLDED), bf16)
    return call(kernel, out, [VMEM], kernel_matrix, name="fold_kernel")


def split_planes(fine, coarse):
    rows = 8

    def kernel(fine_ref, coarse_ref, *refs):
        planes, coarse_out, fine_held, sems = refs[:X], refs[X], refs[X + 1], refs[X + 2]
        parts = [slice(i * rows, (i + 1) * rows) for i in range(S // rows)]
        copies = [pltpu.make_async_copy(fine_ref.at[p], fine_held.at[p], sems.at[i]) for i, p in enumerate(parts)]
        copies.append(pltpu.make_async_copy(coarse_ref, coarse_out, sems.at[len(parts)]))
        for copy in copies:
            copy.start()
        for part, copy in zip(parts, copies):
            copy.wait()
            for x in range(X):
                planes[x][part] = fine_held[part, x, :]
        copies[-1].wait()

    outs = pl.pallas_call(
        kernel,
        out_shape=[sds(S, PLANE)] * X + [sds(S, CELLS)],
        in_specs=[pl.BlockSpec(memory_space=pl.ANY)] * 2,
        out_specs=[VMEM] * (X + 1),
        scratch_shapes=[pltpu.VMEM((S, X, PLANE), f32), pltpu.SemaphoreType.DMA((1 + S // rows,))],
        compiler_params=pltpu.CompilerParams(vmem_limit_bytes=LIMIT * MIB - MIB // 2),
        cost_estimate=COST,
        name="split_planes",
    )(fine, coarse)
    return outs[:X], outs[X]


def coagulate(folded, fields, name):
    count = len(fields)

    def kernel(matrix_ref, *refs):
        for field_ref, out_ref in zip(refs[:count], refs[count:]):
            width = field_ref.shape[1]
            for start in range(0, width, 1024):
                stop = min(start + 1024, width)
                v = field_ref[:, start:stop]
                twice = jnp.concatenate([v, v], axis=0)
                turned = [twice] + [pltpu.roll(twice, 2 * S - b, 0) for b in range(1, 8)]
                pairs = [
                    (v * turned[d % 8][d - d % 8 : d - d % 8 + S]).astype(bf16) for d in range(S // 2 + 1)
                ]
                pairs.append(jnp.zeros((FOLDED - S * (S // 2 + 1), stop - start), bf16))
                product = mm(matrix_ref[...], jnp.concatenate(pairs, axis=0))
                out_ref[:, start:stop] = product[:S] + product[S:]

    return call(
        kernel,
        [sds(*f.shape) for f in fields],
        [VMEM] * (count + 1),
        folded,
        *fields,
        name=name,
    )


def owner_and_cell(request):
    y_count = GHOSTS - 512
    none = jnp.full((1, WIDE - GHOSTS), -1, i32)
    request = jnp.concatenate([request[:, y_count:], request[:, :y_count], none], axis=1)
    owner = jnp.floor((request.astype(f32) + 0.5) * (1.0 / CELLS)).astype(i32)
    return owner, jnp.where(request < 0, -1, request - owner * CELLS)


def column_of(row):
    same = lax.broadcasted_iota(i32, (S, S), 0) == lax.broadcasted_iota(i32, (S, S), 1)
    return jnp.sum(jnp.where(same, jnp.broadcast_to(row, (S, S)), 0.0), axis=1, keepdims=True)


def pick(rows, request, shifts):
    x, y, c = lax.axis_index("x"), lax.axis_index("y"), lax.axis_index("core")
    owner, cell = owner_and_cell(request)
    cell_id = lax.broadcasted_iota(i32, (CELLS, WIDE), 0)
    product = mm(rows, ones_where(jnp.broadcast_to(cell, (CELLS, WIDE)) == cell_id))
    total = jnp.zeros((S, WIDE), f32)
    for part, (shift, mate) in zip(sums_of(product, len(shifts)), shifts):
        from_x = jnp.bitwise_and(x - shift, 3)
        source_owner = (from_x * 4 + y) * 2 + (1 - c if mate else c)
        total = total + jnp.where(owner == source_owner, part, 0.0)
    return total


def gather_first(requests, sources, shifts, row):
    count = len(sources)

    def kernel(*refs):
        request_refs, source_refs, (out_ref, rows_ref, request_out) = refs[:2], refs[2 : 2 + count], refs[2 + count :]
        for i in range(4):
            at = i % 2 * (SPREAD // 2)
            request_out[i : i + 1, :] = request_refs[i // 2][at : at + 1, :]
        for i, ref in enumerate(source_refs):
            high, low = halves(ref[...])
            rows_ref[2 * S * i : 2 * S * i + S] = high
            rows_ref[2 * S * i + S : 2 * S * (i + 1)] = low
        out_ref[...] = pick(rows_ref[...], request_out[row : row + 1, :], shifts)

    return call(
        kernel,
        [
            sds(S, WIDE),
            jax.ShapeDtypeStruct((2 * S * count, CELLS), bf16),
            jax.ShapeDtypeStruct((4, GHOSTS), i32),
        ],
        [VMEM] * (2 + count),
        *requests,
        *sources,
        name="gather_first",
    )


def gather_next(requests, rows, shifts, row, name):
    def kernel(request_ref, rows_ref, out_ref):
        out_ref[...] = pick(rows_ref[...], request_ref[row : row + 1, :], shifts)

    return call(kernel, sds(S, WIDE), [VMEM] * 2, requests, rows, name=name)


def side_by_side(boxes):
    columns = []
    for first, second in zip(boxes[::2], boxes[1::2]):
        both = jnp.concatenate([first[:, 512:GHOSTS], second[:, 512:GHOSTS]], axis=1)
        columns += [first[:, :512], both, second[:, :512]]
    return columns


def cells_by_row(requests):
    def kernel(request_a, request_b, out_ref):
        cells = [
            owner_and_cell((request_a if i < 4 else request_b)[i % 4 : i % 4 + 1, :])[1].astype(f32) for i in range(8)
        ]
        row = 0
        for part in side_by_side(cells):
            for t in range(part.shape[1] // 128):
                block = jnp.broadcast_to(part[:, t * 128 : (t + 1) * 128], (128, 128))
                out_ref[row : row + 128, :] = block.T.astype(i32)
                row += 128

    out = jax.ShapeDtypeStruct((8 * GHOSTS, 128), i32)
    return call(kernel, out, [VMEM] * 2, *requests, name="cells_by_row")


def scatter_columns(requests, cells, registers, steps, name):
    total = 8 * GHOSTS

    def kernel(request_a, request_b, cell_ref, *refs):
        register_refs, outs, rows_ref = refs[:8], refs[8:-1], refs[-1]
        x, y, c = lax.axis_index("x"), lax.axis_index("y"), lax.axis_index("core")
        lane = lax.broadcasted_iota(i32, (1, 128), 1)
        owners = side_by_side(
            [owner_and_cell((request_a if i < 4 else request_b)[i % 4 : i % 4 + 1, :])[0].astype(f32) for i in range(8)]
        )
        at = 0
        for owner, value in zip(owners, side_by_side([ref[...] for ref in register_refs])):
            width = value.shape[1]
            high, low = halves(value)
            for k, step in enumerate(steps):
                to = ((jnp.bitwise_and(x + step, 3) * 4 + y) * 2 + c).astype(f32)
                mine = jnp.broadcast_to(jnp.where(owner == to, 1.0, 0.0).astype(bf16), (S, width))
                rows_ref[2 * S * k : 2 * S * k + S, at : at + width] = high * mine
                rows_ref[2 * S * k + S : 2 * S * (k + 1), at : at + width] = low * mine
            at += width

        def block(start, width):
            marks = [ones_where(cell_ref[...] == lane + (start + 128 * t)) for t in range(width // 128)]
            return sums_of(mm(rows_ref[...], jnp.concatenate(marks, axis=1)), len(steps))

        def body(i, carry):
            start = pl.multiple_of(i * 256, 256)
            for out, part in zip(outs, block(start, 256)):
                out[:, pl.ds(start, 256)] = part
            return carry

        lax.fori_loop(0, 4, body, 0)
        for out, part in zip(outs, block(1024, 128)):
            out[:, 1024:CELLS] = part

    return call(
        kernel,
        [sds(S, CELLS)] * len(steps),
        [VMEM] * 11,
        *requests,
        cells,
        *registers,
        scratch=[pltpu.VMEM((2 * S * len(steps), total), bf16)],
        name=name,
    )


def box_facts(levels_ref):
    box = lax.axis_index("box")
    last = 7
    own = levels_ref[0, box]
    use_low = (box > 0) & (levels_ref[0, jnp.maximum(box - 1, 0)] == own)
    use_high = (box < last) & (levels_ref[0, jnp.minimum(box + 1, last)] == own)
    factor = lax.shift_left(1, own).astype(f32)
    return use_low, use_high, factor


def laplacian(planes, lower, upper, y_ghosts):
    rows = planes[0].shape[0]
    z = jnp.bitwise_and(lax.broadcasted_iota(i32, (rows, PLANE), 1), 31)
    wide = lax.broadcasted_iota(i32, (rows, 128), 1)
    result = []
    for x in range(X):
        v = planes[x]
        ghost = y_ghosts[x // 2]
        before_y = pltpu.roll(v, 32, 1)
        after_y = pltpu.roll(v, PLANE - 32, 1)
        before_y = jnp.concatenate(
            [jnp.where(wide < 32, ghost[:, :128], before_y[:, :128]), before_y[:, 128:]], axis=1
        )
        after_y = jnp.concatenate(
            [after_y[:, :896], jnp.where(wide >= 96, ghost[:, 128:], after_y[:, 896:])], axis=1
        )
        before_z = jnp.where(z == 0, v, pltpu.roll(v, 1, 1))
        after_z = jnp.where(z == 31, v, pltpu.roll(v, PLANE - 1, 1))
        before_x = planes[x - 1] if x > 0 else lower
        after_x = planes[x + 1] if x < X - 1 else upper
        result.append(before_x + after_x + before_y + after_y + before_z + after_z - 6.0 * v)
    return result


def y_code(shape, lane_dim, row_dim, half):
    lane = lax.broadcasted_iota(i32, shape, lane_dim)
    row = lax.broadcasted_iota(i32, shape, row_dim)
    fine = jnp.where(lane < 32, lane, lane - 192)
    code = jnp.where(lane < 32, half * 16 + (lane >> 1), 32 + half * 16 + ((lane - 224) >> 1))
    return ones_where((code == row) & ((lane < 32) | (lane >= 224)))


def x_code(shape, lane_dim, row_dim):
    lane = lax.broadcasted_iota(i32, shape, lane_dim)
    row = lax.broadcasted_iota(i32, shape, row_dim)
    return ones_where((((lane >> 6) << 4) | ((lane >> 1) & 15)) == row)


def first_stage(levels, diffusion, planes, growth, strips, below_plane, above_plane):
    def kernel(levels_ref, diffusion_ref, *refs):
        plane_refs, growth_refs, strip_refs = refs[:4], refs[4:8], refs[8:12]
        lower_ref, upper_ref = refs[12:14]
        middle_refs, base_refs = refs[14:18], refs[18:22]
        registers_ref, x_low_ref, x_high_ref = refs[22:25]
        y_refs = refs[25:27]
        use_low, use_high, factor = box_facts(levels_ref)
        diffusion_column = column_of(diffusion_ref[...])
        strip = strip_refs[0][...] + strip_refs[1][...] + strip_refs[2][...] + strip_refs[3][...]
        x_low, x_high = sums_of(mm(rows_of([strip[:, :256], strip[:, 256:512]]), x_code((256, PLANE), 1, 0)), 2)
        y_rows = rows_of([strip[:, 512:640]])
        y_ghosts = [sums_of(mm(y_rows, y_code((128, 256), 1, 0, half)), 1)[0] for half in range(2)]
        x_low_ref[...] = x_low
        x_high_ref[...] = x_high
        for ref, ghost in zip(y_refs, y_ghosts):
            ref[...] = ghost
        lower = jnp.where(use_low, lower_ref[...], x_low)
        upper = jnp.where(use_high, upper_ref[...], x_high)
        values = [ref[...] for ref in plane_refs]
        spread = laplacian(values, lower, upper, y_ghosts)
        means = []
        for x in range(X):
            rate = (factor * diffusion_column) * spread[x] + STEP * growth_refs[x][...]
            middle = values[x] + rate
            middle_refs[x][...] = middle
            base_refs[x][...] = values[x] + 0.5 * rate
            means.append(0.5 * (values[x] + middle))
        x_below = sums_of(mm(rows_of([means[0], means[3]]), x_code((PLANE, 256), 0, 1)), 2)
        y_below = jnp.zeros((S, 128), f32)
        for half in range(2):
            both = means[2 * half] + means[2 * half + 1]
            ends = jnp.concatenate([both[:, :128], both[:, 896:]], axis=1)
            y_below = y_below + sums_of(mm(rows_of([ends]), y_code((256, 128), 0, 1, half)), 1)[0]
        below = 0.25 * jnp.concatenate(x_below + [y_below], axis=1)
        column = lax.broadcasted_iota(i32, (1, WIDE), 1)
        keep_low = jnp.where(use_low, 0.0, 1.0)
        keep_high = jnp.where(use_high, 0.0, 1.0)
        keep = jnp.where(column < 256, keep_low, jnp.where(column < 512, keep_high, 1.0))
        registers_ref[...] = ((factor - 1.0) * diffusion_column) * (strip - below) * keep

    outs = call(
        kernel,
        [sds(S, PLANE)] * 8 + [sds(S, WIDE)] + [sds(S, PLANE)] * 2 + [sds(S, 256)] * 2,
        [SMEM] + [VMEM] * 15,
        levels,
        diffusion,
        *planes,
        *growth,
        *strips,
        below_plane,
        above_plane,
        name="first_stage",
    )
    return outs[:4], outs[4:8], outs[8], outs[9:11], outs[11:13]


def second_stage(levels, diffusion, middle, base, growth, x_ghosts, y_ghosts, below_plane, above_plane):
    rows = 8

    def kernel(levels_ref, diffusion_ref, *refs):
        middle_refs, base_refs, growth_refs = refs[:4], refs[4:8], refs[8:12]
        x_low_ref, x_high_ref, y_a, y_b, lower_ref, upper_ref, out_ref, held_ref, sems = refs[12:]
        use_low, use_high, factor = box_facts(levels_ref)
        scale = factor * column_of(diffusion_ref[...])
        copies = []
        for i in range(S // rows):
            part = slice(i * rows, (i + 1) * rows)
            lower = jnp.where(use_low, lower_ref[part], x_low_ref[part])
            upper = jnp.where(use_high, upper_ref[part], x_high_ref[part])
            spread = laplacian([ref[part] for ref in middle_refs], lower, upper, [y_a[part], y_b[part]])
            for x in range(X):
                rate = scale[part] * spread[x] + STEP * growth_refs[x][part]
                held_ref[part, x, :] = base_refs[x][part] + 0.5 * rate
            copies.append(pltpu.make_async_copy(held_ref.at[part], out_ref.at[part], sems.at[i]))
            copies[-1].start()
        for copy in copies:
            copy.wait()

    return pl.pallas_call(
        kernel,
        out_shape=sds(S, X, PLANE),
        in_specs=[SMEM] + [VMEM] * 19,
        out_specs=pl.BlockSpec(memory_space=pl.ANY),
        scratch_shapes=[pltpu.VMEM((S, X, PLANE), f32), pltpu.SemaphoreType.DMA((S // rows,))],
        compiler_params=pltpu.CompilerParams(vmem_limit_bytes=40 * MIB),
        cost_estimate=COST,
        name="second_stage",
    )(levels, diffusion, *middle, *base, *growth, *x_ghosts, *y_ghosts, below_plane, above_plane)


def finish_coarse(coarse, growth, parts):
    def kernel(coarse_ref, growth_ref, a, b, c, d, out_ref):
        total = (a[...] + b[...]) + (c[...] + d[...])
        out_ref[...] = coarse_ref[...] + STEP * growth_ref[...] - total

    return call(kernel, sds(S, CELLS), [VMEM] * 6, coarse, growth, *parts, name="finish_coarse")


def shifted(value, axis, shift):
    size = lax.axis_size(axis)
    return lax.ppermute(value, axis, [(i, (i + shift) % size) for i in range(size)])


def after(value, before):
    return lax.optimization_barrier((value, before))[0]


def on_device(fine_state, coarse_state, coag_kernel, diffusion, levels, ghost_src):
    fine = fine_state[0, 0]
    coarse = coarse_state[0, 0]
    row = diffusion.reshape(1, S)
    request = ghost_src[0]

    far = {k: shifted(coarse, "x", k) for k in (2, 1, 3)}
    spread = request + jnp.zeros((SPREAD, 1), i32)
    near = shifted(spread, "y", 1)
    mate = shifted(coarse, "core", 1)
    folded = fold_kernel(coag_kernel)
    near, folded = lax.optimization_barrier((near, folded))
    requests = jnp.concatenate([spread[: SPREAD // 2], near[: SPREAD // 2]], axis=0)
    requests = [requests, shifted(requests, "y", 2)]
    planes, held_coarse = split_planes(fine, after(coarse, (folded, requests[0])))
    below_plane, above_plane = shifted(planes[3], "box", 1), shifted(planes[0], "box", 7)
    growth = coagulate(after(folded, held_coarse), planes, "coagulate_fine")
    far, requests, growth = lax.optimization_barrier((far, requests, growth))

    sources, shifts = [held_coarse, mate], [(0, False), (0, True)]
    for k in (1, 3, 2):
        sources += [far[k], shifted(far[k], "core", 1)]
        shifts += [(k, False), (k, True)]
    part, strips = {}, {}
    part[2], rows, request_rows = gather_first(requests, sources, shifts, 2)
    strips[2] = shifted(part[2], "y", 2)
    part[1] = gather_next(request_rows, rows, shifts, 1, "gather_one")
    strips[1] = shifted(part[1], "y", 3)
    part[3] = gather_next(after(request_rows, part[1]), rows, shifts, 3, "gather_three")
    strips[3] = shifted(part[3], "y", 1)
    strips[0] = gather_next(after(request_rows, (part[3], strips[2])), rows, shifts, 0, "gather_own")
    coarse_growth = coagulate(after(folded, (strips[0], strips[1])), [held_coarse], "coagulate_coarse")[0]
    mate_rows = shifted(request_rows, "core", 1)
    strips, coarse_growth, mate_rows = lax.optimization_barrier((strips, coarse_growth, mate_rows))
    strips = [strips[k] for k in range(4)]

    middle, base, registers, x_ghosts, y_ghosts = first_stage(
        levels, row, planes, growth, strips, below_plane, above_plane
    )

    held = {k: shifted(registers, "y", k) for k in (2, 1, 3)}
    held[0] = registers
    cells = cells_by_row([request_rows, after(mate_rows, registers)])
    below_plane, above_plane = shifted(middle[3], "box", 1), shifted(middle[0], "box", 7)
    growth = coagulate(after(folded, cells), middle, "coagulate_middle")
    held = [after(held[k], growth[0]) for k in range(4)]
    held += [shifted(value, "core", 1) for value in held]
    cells = after(cells, (below_plane, above_plane))
    sent = {}
    (part,) = scatter_columns([request_rows, mate_rows], cells, held, (2,), "scatter_far")
    sent[2] = shifted(part, "x", 2)
    parts = scatter_columns([request_rows, mate_rows], after(cells, part), held, (1, 3), "scatter_near")
    sent[1], sent[3] = shifted(parts[0], "x", 1), shifted(parts[1], "x", 3)
    (sent[0],) = scatter_columns([request_rows, mate_rows], after(cells, parts[0]), held, (0,), "scatter_own")
    base = after(base, (sent[0], sent[2]))
    fine_out = second_stage(levels, row, middle, base, growth, x_ghosts, y_ghosts, below_plane, above_plane)
    sent = [sent[k] for k in range(4)]
    sent, fine_out, coarse_growth = lax.optimization_barrier((sent, fine_out, coarse_growth))
    coarse_out = finish_coarse(held_coarse, coarse_growth, sent)
    return fine_out[None, None], coarse_out[None, None]


def solution(mesh):
    group = ("x", "y", "core")
    split = Mesh(mesh.devices.reshape(4, 4, 2, 8), group + ("box",))
    return jax.shard_map(
        on_device,
        mesh=split,
        in_specs=(
            P(group, "box", None, None, None),
            P(group, "box", None, None),
            P(),
            P(),
            P(group, None),
            P(group, "box", None),
        ),
        out_specs=(P(group, "box", None, None, None), P(group, "box", None, None)),
        check_vma=False,
    )
```

```python
import jax
import jax.numpy as jnp
from jax import lax
from jax.experimental import pallas as pl
from jax.experimental.pallas import tpu as pltpu
from jax.sharding import Mesh, PartitionSpec as P

S = 48
X = 4
PLANE = 1024
CELLS = 1152
GHOSTS = 576
WIDE = 640
STEP = 0.25
FOLDED = 1280
MIB = 1024 * 1024
LIMIT = 53
SPREAD = 24
COST = pl.CostEstimate(flops=0, bytes_accessed=0, transcendentals=0)

f32 = jnp.float32
bf16 = jnp.bfloat16
i32 = jnp.int32
VMEM = pl.BlockSpec(memory_space=pltpu.VMEM)
SMEM = pl.BlockSpec(memory_space=pltpu.SMEM)


def sds(*shape):
    return jax.ShapeDtypeStruct(shape, f32)


def call(kernel, out_shape, in_specs, *operands, scratch=(), name=None):
    many = isinstance(out_shape, list)
    return pl.pallas_call(
        kernel,
        out_shape=out_shape,
        in_specs=in_specs,
        out_specs=[VMEM] * len(out_shape) if many else VMEM,
        scratch_shapes=list(scratch),
        compiler_params=pltpu.CompilerParams(vmem_limit_bytes=40 * MIB),
        cost_estimate=COST,
        name=name,
    )(*operands)


def mm(a, b):
    return jnp.dot(a, b, preferred_element_type=f32)


def halves(value):
    high = value.astype(bf16)
    return high, (value - high.astype(f32)).astype(bf16)


def rows_of(values):
    parts = []
    for value in values:
        parts.extend(halves(value))
    return jnp.concatenate(parts, axis=0)


def sums_of(product, count):
    return [product[2 * S * i : 2 * S * i + S] + product[2 * S * i + S : 2 * S * (i + 1)] for i in range(count)]


def ones_where(mask):
    return jnp.where(mask, 1.0, 0.0).astype(bf16)


def fold_kernel(kernel_matrix):
    pairs = S * S

    def kernel(matrix_ref, folded_ref):
        pair = lax.broadcasted_iota(i32, (pairs, 128), 0)
        first = (pair * 43691) >> 21
        second = pair - first * S
        gap = second - first
        gap = jnp.where(gap < 0, gap + S, gap)
        place = jnp.where(gap <= S // 2, gap * S + first, (S - gap) * S + second)
        lane = lax.broadcasted_iota(i32, (1, 128), 1)
        for start in range(0, FOLDED, 256):
            marks = [ones_where(place == lane + (start + t)) for t in (0, 128)]
            high, low = halves(mm(matrix_ref[...], jnp.concatenate(marks, axis=1)))
            folded_ref[:S, start : start + 256] = high
            folded_ref[S:, start : start + 256] = low

    out = jax.ShapeDtypeStruct((2 * S, FOLDED), bf16)
    return call(kernel, out, [VMEM], kernel_matrix, name="fold_kernel")


def split_planes(fine, coarse):
    rows = 8

    def kernel(fine_ref, coarse_ref, *refs):
        planes, coarse_out, fine_held, sems = refs[:X], refs[X], refs[X + 1], refs[X + 2]
        parts = [slice(i * rows, (i + 1) * rows) for i in range(S // rows)]
        copies = [pltpu.make_async_copy(fine_ref.at[p], fine_held.at[p], sems.at[i]) for i, p in enumerate(parts)]
        copies.append(pltpu.make_async_copy(coarse_ref, coarse_out, sems.at[len(parts)]))
        for copy in copies:
            copy.start()
        for part, copy in zip(parts, copies):
            copy.wait()
            for x in range(X):
                planes[x][part] = fine_held[part, x, :]
        copies[-1].wait()

    outs = pl.pallas_call(
        kernel,
        out_shape=[sds(S, PLANE)] * X + [sds(S, CELLS)],
        in_specs=[pl.BlockSpec(memory_space=pl.ANY)] * 2,
        out_specs=[VMEM] * (X + 1),
        scratch_shapes=[pltpu.VMEM((S, X, PLANE), f32), pltpu.SemaphoreType.DMA((1 + S // rows,))],
        compiler_params=pltpu.CompilerParams(vmem_limit_bytes=LIMIT * MIB - MIB // 2),
        cost_estimate=COST,
        name="split_planes",
    )(fine, coarse)
    return outs[:X], outs[X]


def coagulate(folded, fields, name):
    count = len(fields)

    def kernel(matrix_ref, *refs):
        for field_ref, out_ref in zip(refs[:count], refs[count:]):
            width = field_ref.shape[1]
            for start in range(0, width, 1024):
                stop = min(start + 1024, width)
                v = field_ref[:, start:stop]
                twice = jnp.concatenate([v, v], axis=0)
                turned = [twice] + [pltpu.roll(twice, 2 * S - b, 0) for b in range(1, 8)]
                pairs = [
                    (v * turned[d % 8][d - d % 8 : d - d % 8 + S]).astype(bf16) for d in range(S // 2 + 1)
                ]
                pairs.append(jnp.zeros((FOLDED - S * (S // 2 + 1), stop - start), bf16))
                product = mm(matrix_ref[...], jnp.concatenate(pairs, axis=0))
                out_ref[:, start:stop] = product[:S] + product[S:]

    return call(
        kernel,
        [sds(*f.shape) for f in fields],
        [VMEM] * (count + 1),
        folded,
        *fields,
        name=name,
    )


def owner_and_cell(request):
    y_count = GHOSTS - 512
    none = jnp.full((1, WIDE - GHOSTS), -1, i32)
    request = jnp.concatenate([request[:, y_count:], request[:, :y_count], none], axis=1)
    owner = jnp.floor((request.astype(f32) + 0.5) * (1.0 / CELLS)).astype(i32)
    return owner, jnp.where(request < 0, -1, request - owner * CELLS)


def column_of(row):
    same = lax.broadcasted_iota(i32, (S, S), 0) == lax.broadcasted_iota(i32, (S, S), 1)
    return jnp.sum(jnp.where(same, jnp.broadcast_to(row, (S, S)), 0.0), axis=1, keepdims=True)


def pick(rows, requests, shifts):
    x, y, c = lax.axis_index("x"), lax.axis_index("y"), lax.axis_index("core")
    owner, cell = [jnp.concatenate(both, axis=1) for both in zip(*map(owner_and_cell, requests))]
    cell_id = lax.broadcasted_iota(i32, (CELLS, cell.shape[1]), 0)
    product = mm(rows, ones_where(jnp.broadcast_to(cell, cell_id.shape) == cell_id))
    total = jnp.zeros((S, cell.shape[1]), f32)
    for part, (shift, mate) in zip(sums_of(product, len(shifts)), shifts):
        from_x = jnp.bitwise_and(x - shift, 3)
        source_owner = (from_x * 4 + y) * 2 + (1 - c if mate else c)
        total = total + jnp.where(owner == source_owner, part, 0.0)
    return total


def gather_first(requests, sources, shifts, row):
    count = len(sources)

    def kernel(*refs):
        request_refs, source_refs, (out_ref, rows_ref, request_out) = refs[:2], refs[2 : 2 + count], refs[2 + count :]
        for i in range(4):
            at = i % 2 * (SPREAD // 2)
            request_out[i : i + 1, :] = request_refs[i // 2][at : at + 1, :]
        for i, ref in enumerate(source_refs):
            high, low = halves(ref[...])
            rows_ref[2 * S * i : 2 * S * i + S] = high
            rows_ref[2 * S * i + S : 2 * S * (i + 1)] = low
        out_ref[...] = pick(rows_ref[...], [request_out[row : row + 1, :]], shifts)

    return call(
        kernel,
        [
            sds(S, WIDE),
            jax.ShapeDtypeStruct((2 * S * count, CELLS), bf16),
            jax.ShapeDtypeStruct((4, GHOSTS), i32),
        ],
        [VMEM] * (2 + count),
        *requests,
        *sources,
        name="gather_first",
    )


def gather_next(requests, rows, shifts, boxes, name):
    def kernel(request_ref, rows_ref, *outs):
        total = pick(rows_ref[...], [request_ref[i : i + 1, :] for i in boxes], shifts)
        for i, out in enumerate(outs):
            out[...] = total[:, i * WIDE : (i + 1) * WIDE]

    return call(kernel, [sds(S, WIDE)] * len(boxes), [VMEM] * 2, requests, rows, name=name)


def side_by_side(boxes):
    columns = []
    for first, second in zip(boxes[::2], boxes[1::2]):
        both = jnp.concatenate([first[:, 512:GHOSTS], second[:, 512:GHOSTS]], axis=1)
        columns += [first[:, :512], both, second[:, :512]]
    return columns


def cells_by_row(requests):
    def kernel(request_a, request_b, out_ref):
        cells = [
            owner_and_cell((request_a if i < 4 else request_b)[i % 4 : i % 4 + 1, :])[1].astype(f32) for i in range(8)
        ]
        row = 0
        for part in side_by_side(cells):
            for t in range(part.shape[1] // 128):
                block = jnp.broadcast_to(part[:, t * 128 : (t + 1) * 128], (128, 128))
                out_ref[row : row + 128, :] = block.T.astype(i32)
                row += 128

    out = jax.ShapeDtypeStruct((8 * GHOSTS, 128), i32)
    return call(kernel, out, [VMEM] * 2, *requests, name="cells_by_row")


def scatter_columns(requests, cells, registers, steps, name):
    total = 8 * GHOSTS

    def kernel(request_a, request_b, cell_ref, *refs):
        register_refs, outs, rows_ref = refs[:8], refs[8:-1], refs[-1]
        x, y, c = lax.axis_index("x"), lax.axis_index("y"), lax.axis_index("core")
        lane = lax.broadcasted_iota(i32, (1, 128), 1)
        owners = side_by_side(
            [owner_and_cell((request_a if i < 4 else request_b)[i % 4 : i % 4 + 1, :])[0].astype(f32) for i in range(8)]
        )
        at = 0
        for owner, value in zip(owners, side_by_side([ref[...] for ref in register_refs])):
            width = value.shape[1]
            high, low = halves(value)
            for k, step in enumerate(steps):
                to = ((jnp.bitwise_and(x + step, 3) * 4 + y) * 2 + c).astype(f32)
                mine = jnp.broadcast_to(jnp.where(owner == to, 1.0, 0.0).astype(bf16), (S, width))
                rows_ref[2 * S * k : 2 * S * k + S, at : at + width] = high * mine
                rows_ref[2 * S * k + S : 2 * S * (k + 1), at : at + width] = low * mine
            at += width

        def block(start, width):
            marks = [ones_where(cell_ref[...] == lane + (start + 128 * t)) for t in range(width // 128)]
            return sums_of(mm(rows_ref[...], jnp.concatenate(marks, axis=1)), len(steps))

        def body(i, carry):
            start = pl.multiple_of(i * 256, 256)
            for out, part in zip(outs, block(start, 256)):
                out[:, pl.ds(start, 256)] = part
            return carry

        lax.fori_loop(0, 4, body, 0)
        for out, part in zip(outs, block(1024, 128)):
            out[:, 1024:CELLS] = part

    return call(
        kernel,
        [sds(S, CELLS)] * len(steps),
        [VMEM] * 11,
        *requests,
        cells,
        *registers,
        scratch=[pltpu.VMEM((2 * S * len(steps), total), bf16)],
        name=name,
    )


def box_facts(levels_ref):
    box = lax.axis_index("box")
    last = 7
    own = levels_ref[0, box]
    use_low = (box > 0) & (levels_ref[0, jnp.maximum(box - 1, 0)] == own)
    use_high = (box < last) & (levels_ref[0, jnp.minimum(box + 1, last)] == own)
    factor = lax.shift_left(1, own).astype(f32)
    return use_low, use_high, factor


def laplacian(planes, lower, upper, y_ghosts):
    rows = planes[0].shape[0]
    z = jnp.bitwise_and(lax.broadcasted_iota(i32, (rows, PLANE), 1), 31)
    wide = lax.broadcasted_iota(i32, (rows, 128), 1)
    result = []
    for x in range(X):
        v = planes[x]
        ghost = y_ghosts[x // 2]
        before_y = pltpu.roll(v, 32, 1)
        after_y = pltpu.roll(v, PLANE - 32, 1)
        before_y = jnp.concatenate(
            [jnp.where(wide < 32, ghost[:, :128], before_y[:, :128]), before_y[:, 128:]], axis=1
        )
        after_y = jnp.concatenate(
            [after_y[:, :896], jnp.where(wide >= 96, ghost[:, 128:], after_y[:, 896:])], axis=1
        )
        before_z = jnp.where(z == 0, v, pltpu.roll(v, 1, 1))
        after_z = jnp.where(z == 31, v, pltpu.roll(v, PLANE - 1, 1))
        before_x = planes[x - 1] if x > 0 else lower
        after_x = planes[x + 1] if x < X - 1 else upper
        result.append(before_x + after_x + before_y + after_y + before_z + after_z - 6.0 * v)
    return result


def y_code(shape, lane_dim, row_dim, half):
    lane = lax.broadcasted_iota(i32, shape, lane_dim)
    row = lax.broadcasted_iota(i32, shape, row_dim)
    fine = jnp.where(lane < 32, lane, lane - 192)
    code = jnp.where(lane < 32, half * 16 + (lane >> 1), 32 + half * 16 + ((lane - 224) >> 1))
    return ones_where((code == row) & ((lane < 32) | (lane >= 224)))


def x_code(shape, lane_dim, row_dim):
    lane = lax.broadcasted_iota(i32, shape, lane_dim)
    row = lax.broadcasted_iota(i32, shape, row_dim)
    return ones_where((((lane >> 6) << 4) | ((lane >> 1) & 15)) == row)


def first_stage(levels, diffusion, planes, growth, strips, below_plane, above_plane):
    def kernel(levels_ref, diffusion_ref, *refs):
        plane_refs, growth_refs, strip_refs = refs[:4], refs[4:8], refs[8:12]
        lower_ref, upper_ref = refs[12:14]
        middle_refs, base_refs = refs[14:18], refs[18:22]
        registers_ref, x_low_ref, x_high_ref = refs[22:25]
        y_refs = refs[25:27]
        use_low, use_high, factor = box_facts(levels_ref)
        diffusion_column = column_of(diffusion_ref[...])
        strip = strip_refs[0][...] + strip_refs[1][...] + strip_refs[2][...] + strip_refs[3][...]
        x_low, x_high = sums_of(mm(rows_of([strip[:, :256], strip[:, 256:512]]), x_code((256, PLANE), 1, 0)), 2)
        y_rows = rows_of([strip[:, 512:640]])
        y_ghosts = [sums_of(mm(y_rows, y_code((128, 256), 1, 0, half)), 1)[0] for half in range(2)]
        x_low_ref[...] = x_low
        x_high_ref[...] = x_high
        for ref, ghost in zip(y_refs, y_ghosts):
            ref[...] = ghost
        lower = jnp.where(use_low, lower_ref[...], x_low)
        upper = jnp.where(use_high, upper_ref[...], x_high)
        values = [ref[...] for ref in plane_refs]
        spread = laplacian(values, lower, upper, y_ghosts)
        means = []
        for x in range(X):
            rate = (factor * diffusion_column) * spread[x] + STEP * growth_refs[x][...]
            middle = values[x] + rate
            middle_refs[x][...] = middle
            base_refs[x][...] = values[x] + 0.5 * rate
            means.append(0.5 * (values[x] + middle))
        x_below = sums_of(mm(rows_of([means[0], means[3]]), x_code((PLANE, 256), 0, 1)), 2)
        y_below = jnp.zeros((S, 128), f32)
        for half in range(2):
            both = means[2 * half] + means[2 * half + 1]
            ends = jnp.concatenate([both[:, :128], both[:, 896:]], axis=1)
            y_below = y_below + sums_of(mm(rows_of([ends]), y_code((256, 128), 0, 1, half)), 1)[0]
        below = 0.25 * jnp.concatenate(x_below + [y_below], axis=1)
        column = lax.broadcasted_iota(i32, (1, WIDE), 1)
        keep_low = jnp.where(use_low, 0.0, 1.0)
        keep_high = jnp.where(use_high, 0.0, 1.0)
        keep = jnp.where(column < 256, keep_low, jnp.where(column < 512, keep_high, 1.0))
        registers_ref[...] = ((factor - 1.0) * diffusion_column) * (strip - below) * keep

    outs = call(
        kernel,
        [sds(S, PLANE)] * 8 + [sds(S, WIDE)] + [sds(S, PLANE)] * 2 + [sds(S, 256)] * 2,
        [SMEM] + [VMEM] * 15,
        levels,
        diffusion,
        *planes,
        *growth,
        *strips,
        below_plane,
        above_plane,
        name="first_stage",
    )
    return outs[:4], outs[4:8], outs[8], outs[9:11], outs[11:13]


def second_stage(levels, diffusion, middle, base, growth, x_ghosts, y_ghosts, below_plane, above_plane):
    rows = 8

    def kernel(levels_ref, diffusion_ref, *refs):
        middle_refs, base_refs, growth_refs = refs[:4], refs[4:8], refs[8:12]
        x_low_ref, x_high_ref, y_a, y_b, lower_ref, upper_ref, out_ref, held_ref, sems = refs[12:]
        use_low, use_high, factor = box_facts(levels_ref)
        scale = factor * column_of(diffusion_ref[...])
        copies = []
        for i in range(S // rows):
            part = slice(i * rows, (i + 1) * rows)
            lower = jnp.where(use_low, lower_ref[part], x_low_ref[part])
            upper = jnp.where(use_high, upper_ref[part], x_high_ref[part])
            spread = laplacian([ref[part] for ref in middle_refs], lower, upper, [y_a[part], y_b[part]])
            for x in range(X):
                rate = scale[part] * spread[x] + STEP * growth_refs[x][part]
                held_ref[part, x, :] = base_refs[x][part] + 0.5 * rate
            copies.append(pltpu.make_async_copy(held_ref.at[part], out_ref.at[part], sems.at[i]))
            copies[-1].start()
        for copy in copies:
            copy.wait()

    return pl.pallas_call(
        kernel,
        out_shape=sds(S, X, PLANE),
        in_specs=[SMEM] + [VMEM] * 19,
        out_specs=pl.BlockSpec(memory_space=pl.ANY),
        scratch_shapes=[pltpu.VMEM((S, X, PLANE), f32), pltpu.SemaphoreType.DMA((S // rows,))],
        compiler_params=pltpu.CompilerParams(vmem_limit_bytes=40 * MIB),
        cost_estimate=COST,
        name="second_stage",
    )(levels, diffusion, *middle, *base, *growth, *x_ghosts, *y_ghosts, below_plane, above_plane)


def finish_coarse(coarse, growth, parts):
    def kernel(coarse_ref, growth_ref, a, b, c, d, out_ref):
        total = (a[...] + b[...]) + (c[...] + d[...])
        out_ref[...] = coarse_ref[...] + STEP * growth_ref[...] - total

    return call(kernel, sds(S, CELLS), [VMEM] * 6, coarse, growth, *parts, name="finish_coarse")


def shifted(value, axis, shift):
    size = lax.axis_size(axis)
    return lax.ppermute(value, axis, [(i, (i + shift) % size) for i in range(size)])


def after(value, before):
    return lax.optimization_barrier((value, before))[0]


def on_device(fine_state, coarse_state, coag_kernel, diffusion, levels, ghost_src):
    fine = fine_state[0, 0]
    coarse = coarse_state[0, 0]
    row = diffusion.reshape(1, S)
    request = ghost_src[0]

    far = {k: shifted(coarse, "x", k) for k in (2, 1, 3)}
    spread = request + jnp.zeros((SPREAD, 1), i32)
    near = shifted(spread, "y", 1)
    mate = shifted(coarse, "core", 1)
    folded = fold_kernel(coag_kernel)
    near, folded = lax.optimization_barrier((near, folded))
    requests = jnp.concatenate([spread[: SPREAD // 2], near[: SPREAD // 2]], axis=0)
    requests = [requests, shifted(requests, "y", 2)]
    planes, held_coarse = split_planes(fine, after(coarse, (folded, requests[0])))
    below_plane, above_plane = shifted(planes[3], "box", 1), shifted(planes[0], "box", 7)
    growth = coagulate(after(folded, held_coarse), planes, "coagulate_fine")
    far, requests, growth = lax.optimization_barrier((far, requests, growth))

    sources, shifts = [held_coarse, mate], [(0, False), (0, True)]
    for k in (1, 3, 2):
        sources += [far[k], shifted(far[k], "core", 1)]
        shifts += [(k, False), (k, True)]
    part, strips = {}, {}
    part[2], rows, request_rows = gather_first(requests, sources, shifts, 2)
    strips[2] = shifted(part[2], "y", 2)
    part[1], part[3] = gather_next(request_rows, rows, shifts, (1, 3), "gather_near")
    strips[1], strips[3] = shifted(part[1], "y", 3), shifted(part[3], "y", 1)
    (strips[0],) = gather_next(after(request_rows, (part[3], strips[2])), rows, shifts, (0,), "gather_own")
    coarse_growth = coagulate(after(folded, (strips[0], strips[1])), [held_coarse], "coagulate_coarse")[0]
    mate_rows = shifted(request_rows, "core", 1)
    cells = cells_by_row([request_rows, after(mate_rows, coarse_growth)])
    strips, cells = lax.optimization_barrier((strips, cells))
    strips = [strips[k] for k in range(4)]

    middle, base, registers, x_ghosts, y_ghosts = first_stage(
        levels, row, planes, growth, strips, below_plane, above_plane
    )

    held = {k: shifted(registers, "y", k) for k in (2, 1, 3)}
    held[0] = registers
    growth = coagulate(folded, middle, "coagulate_middle")
    ends = (middle[3], middle[0])
    below_plane, above_plane = shifted(ends[0], "box", 1), shifted(ends[1], "box", 7)
    held = [after(held[k], growth[0]) for k in range(4)]
    held += [shifted(value, "core", 1) for value in held]
    cells = after(cells, (below_plane, above_plane))
    sent = {}
    (part,) = scatter_columns([request_rows, mate_rows], cells, held, (2,), "scatter_far")
    sent[2] = shifted(part, "x", 2)
    parts = scatter_columns([request_rows, mate_rows], after(cells, part), held, (1, 3), "scatter_near")
    sent[1], sent[3] = shifted(parts[0], "x", 1), shifted(parts[1], "x", 3)
    (sent[0],) = scatter_columns([request_rows, mate_rows], after(cells, parts[0]), held, (0,), "scatter_own")
    base = after(base, (sent[0], sent[2]))
    fine_out = second_stage(levels, row, middle, base, growth, x_ghosts, y_ghosts, below_plane, above_plane)
    sent = [sent[k] for k in range(4)]
    sent, fine_out, coarse_growth = lax.optimization_barrier((sent, fine_out, coarse_growth))
    coarse_out = finish_coarse(held_coarse, coarse_growth, sent)
    return fine_out[None, None], coarse_out[None, None]


def solution(mesh):
    group = ("x", "y", "core")
    split = Mesh(mesh.devices.reshape(4, 4, 2, 8), group + ("box",))
    return jax.shard_map(
        on_device,
        mesh=split,
        in_specs=(
            P(group, "box", None, None, None),
            P(group, "box", None, None),
            P(),
            P(),
            P(group, None),
            P(group, "box", None),
        ),
        out_specs=(P(group, "box", None, None, None), P(group, "box", None, None)),
        check_vma=False,
    )
```

```python
import jax
import jax.numpy as jnp
from jax import lax
from jax.experimental import pallas as pl
from jax.experimental.pallas import tpu as pltpu
from jax.sharding import Mesh, PartitionSpec as P

S = 48
X = 4
PLANE = 1024
CELLS = 1152
GHOSTS = 576
WIDE = 640
STEP = 0.25
FOLDED = 1280
MIB = 1024 * 1024
LIMIT = 53
SPREAD = 24
COST = pl.CostEstimate(flops=0, bytes_accessed=0, transcendentals=0)

f32 = jnp.float32
bf16 = jnp.bfloat16
i32 = jnp.int32
VMEM = pl.BlockSpec(memory_space=pltpu.VMEM)
SMEM = pl.BlockSpec(memory_space=pltpu.SMEM)


def sds(*shape):
    return jax.ShapeDtypeStruct(shape, f32)


def call(kernel, out_shape, in_specs, *operands, scratch=(), name=None):
    many = isinstance(out_shape, list)
    return pl.pallas_call(
        kernel,
        out_shape=out_shape,
        in_specs=in_specs,
        out_specs=[VMEM] * len(out_shape) if many else VMEM,
        scratch_shapes=list(scratch),
        compiler_params=pltpu.CompilerParams(vmem_limit_bytes=40 * MIB),
        cost_estimate=COST,
        name=name,
    )(*operands)


def mm(a, b):
    return jnp.dot(a, b, preferred_element_type=f32)


def halves(value):
    high = value.astype(bf16)
    return high, (value - high.astype(f32)).astype(bf16)


def rows_of(values):
    parts = []
    for value in values:
        parts.extend(halves(value))
    return jnp.concatenate(parts, axis=0)


def sums_of(product, count):
    return [product[2 * S * i : 2 * S * i + S] + product[2 * S * i + S : 2 * S * (i + 1)] for i in range(count)]


def ones_where(mask):
    return jnp.where(mask, 1.0, 0.0).astype(bf16)


def fold_kernel(kernel_matrix):
    pairs = S * S

    def kernel(matrix_ref, folded_ref):
        pair = lax.broadcasted_iota(i32, (pairs, 128), 0)
        first = (pair * 43691) >> 21
        second = pair - first * S
        gap = second - first
        gap = jnp.where(gap < 0, gap + S, gap)
        place = jnp.where(gap <= S // 2, gap * S + first, (S - gap) * S + second)
        lane = lax.broadcasted_iota(i32, (1, 128), 1)
        for start in range(0, FOLDED, 256):
            marks = [ones_where(place == lane + (start + t)) for t in (0, 128)]
            high, low = halves(mm(matrix_ref[...], jnp.concatenate(marks, axis=1)))
            folded_ref[:S, start : start + 256] = high
            folded_ref[S:, start : start + 256] = low

    out = jax.ShapeDtypeStruct((2 * S, FOLDED), bf16)
    return call(kernel, out, [VMEM], kernel_matrix, name="fold_kernel")


def split_planes(fine, coarse):
    rows = 8

    def kernel(fine_ref, coarse_ref, *refs):
        planes, coarse_out, fine_held, sems = refs[:X], refs[X], refs[X + 1], refs[X + 2]
        parts = [slice(i * rows, (i + 1) * rows) for i in range(S // rows)]
        copies = [pltpu.make_async_copy(fine_ref.at[p], fine_held.at[p], sems.at[i]) for i, p in enumerate(parts)]
        copies.append(pltpu.make_async_copy(coarse_ref, coarse_out, sems.at[len(parts)]))
        for copy in copies:
            copy.start()
        for part, copy in zip(parts, copies):
            copy.wait()
            for x in range(X):
                planes[x][part] = fine_held[part, x, :]
        copies[-1].wait()

    outs = pl.pallas_call(
        kernel,
        out_shape=[sds(S, PLANE)] * X + [sds(S, CELLS)],
        in_specs=[pl.BlockSpec(memory_space=pl.ANY)] * 2,
        out_specs=[VMEM] * (X + 1),
        scratch_shapes=[pltpu.VMEM((S, X, PLANE), f32), pltpu.SemaphoreType.DMA((1 + S // rows,))],
        compiler_params=pltpu.CompilerParams(vmem_limit_bytes=LIMIT * MIB - MIB // 2),
        cost_estimate=COST,
        name="split_planes",
    )(fine, coarse)
    return outs[:X], outs[X]


def coagulate(folded, fields, name):
    count = len(fields)

    def kernel(matrix_ref, *refs):
        for field_ref, out_ref in zip(refs[:count], refs[count:]):
            width = field_ref.shape[1]
            for start in range(0, width, 1024):
                stop = min(start + 1024, width)
                v = field_ref[:, start:stop]
                twice = jnp.concatenate([v, v], axis=0)
                turned = [twice] + [pltpu.roll(twice, 2 * S - b, 0) for b in range(1, 8)]
                pairs = [
                    (v * turned[d % 8][d - d % 8 : d - d % 8 + S]).astype(bf16) for d in range(S // 2 + 1)
                ]
                pairs.append(jnp.zeros((FOLDED - S * (S // 2 + 1), stop - start), bf16))
                product = mm(matrix_ref[...], jnp.concatenate(pairs, axis=0))
                out_ref[:, start:stop] = product[:S] + product[S:]

    return call(
        kernel,
        [sds(*f.shape) for f in fields],
        [VMEM] * (count + 1),
        folded,
        *fields,
        name=name,
    )


def owner_and_cell(request):
    y_count = GHOSTS - 512
    none = jnp.full((1, WIDE - GHOSTS), -1, i32)
    request = jnp.concatenate([request[:, y_count:], request[:, :y_count], none], axis=1)
    owner = jnp.floor((request.astype(f32) + 0.5) * (1.0 / CELLS)).astype(i32)
    return owner, jnp.where(request < 0, -1, request - owner * CELLS)


def column_of(row):
    same = lax.broadcasted_iota(i32, (S, S), 0) == lax.broadcasted_iota(i32, (S, S), 1)
    return jnp.sum(jnp.where(same, jnp.broadcast_to(row, (S, S)), 0.0), axis=1, keepdims=True)


def pick(rows, requests, shifts):
    x, y, c = lax.axis_index("x"), lax.axis_index("y"), lax.axis_index("core")
    owner, cell = [jnp.concatenate(both, axis=1) for both in zip(*map(owner_and_cell, requests))]
    cell_id = lax.broadcasted_iota(i32, (CELLS, cell.shape[1]), 0)
    product = mm(rows, ones_where(jnp.broadcast_to(cell, cell_id.shape) == cell_id))
    total = jnp.zeros((S, cell.shape[1]), f32)
    for part, (shift, mate) in zip(sums_of(product, len(shifts)), shifts):
        from_x = jnp.bitwise_and(x - shift, 3)
        source_owner = (from_x * 4 + y) * 2 + (1 - c if mate else c)
        total = total + jnp.where(owner == source_owner, part, 0.0)
    return total


def gather_first(requests, sources, shifts, row):
    count = len(sources)

    def kernel(*refs):
        request_refs, source_refs, (out_ref, rows_ref, request_out) = refs[:2], refs[2 : 2 + count], refs[2 + count :]
        for i in range(4):
            at = i % 2 * (SPREAD // 2)
            request_out[i : i + 1, :] = request_refs[i // 2][at : at + 1, :]
        for i, ref in enumerate(source_refs):
            high, low = halves(ref[...])
            rows_ref[2 * S * i : 2 * S * i + S] = high
            rows_ref[2 * S * i + S : 2 * S * (i + 1)] = low
        out_ref[...] = pick(rows_ref[...], [request_out[row : row + 1, :]], shifts)

    return call(
        kernel,
        [
            sds(S, WIDE),
            jax.ShapeDtypeStruct((2 * S * count, CELLS), bf16),
            jax.ShapeDtypeStruct((4, GHOSTS), i32),
        ],
        [VMEM] * (2 + count),
        *requests,
        *sources,
        name="gather_first",
    )


def gather_next(requests, rows, shifts, boxes, name):
    def kernel(request_ref, rows_ref, *outs):
        total = pick(rows_ref[...], [request_ref[i : i + 1, :] for i in boxes], shifts)
        for i, out in enumerate(outs):
            out[...] = total[:, i * WIDE : (i + 1) * WIDE]

    return call(kernel, [sds(S, WIDE)] * len(boxes), [VMEM] * 2, requests, rows, name=name)


def side_by_side(boxes):
    columns = []
    for first, second in zip(boxes[::2], boxes[1::2]):
        both = jnp.concatenate([first[:, 512:GHOSTS], second[:, 512:GHOSTS]], axis=1)
        columns += [first[:, :512], both, second[:, :512]]
    return columns


def cells_by_row(requests):
    def kernel(request_a, request_b, out_ref):
        cells = [
            owner_and_cell((request_a if i < 4 else request_b)[i % 4 : i % 4 + 1, :])[1].astype(f32) for i in range(8)
        ]
        row = 0
        for part in side_by_side(cells):
            for t in range(part.shape[1] // 128):
                block = jnp.broadcast_to(part[:, t * 128 : (t + 1) * 128], (128, 128))
                out_ref[row : row + 128, :] = block.T.astype(i32)
                row += 128

    out = jax.ShapeDtypeStruct((8 * GHOSTS, 128), i32)
    return call(kernel, out, [VMEM] * 2, *requests, name="cells_by_row")


def scatter_columns(requests, cells, registers, steps, name):
    total = 8 * GHOSTS

    def kernel(request_a, request_b, cell_ref, *refs):
        register_refs, outs, rows_ref = refs[:8], refs[8:-1], refs[-1]
        x, y, c = lax.axis_index("x"), lax.axis_index("y"), lax.axis_index("core")
        lane = lax.broadcasted_iota(i32, (1, 128), 1)
        owners = side_by_side(
            [owner_and_cell((request_a if i < 4 else request_b)[i % 4 : i % 4 + 1, :])[0].astype(f32) for i in range(8)]
        )
        at = 0
        for owner, value in zip(owners, side_by_side([ref[...] for ref in register_refs])):
            width = value.shape[1]
            high, low = halves(value)
            for k, step in enumerate(steps):
                to = ((jnp.bitwise_and(x + step, 3) * 4 + y) * 2 + c).astype(f32)
                mine = jnp.broadcast_to(jnp.where(owner == to, 1.0, 0.0).astype(bf16), (S, width))
                rows_ref[2 * S * k : 2 * S * k + S, at : at + width] = high * mine
                rows_ref[2 * S * k + S : 2 * S * (k + 1), at : at + width] = low * mine
            at += width

        def block(start, width):
            marks = [ones_where(cell_ref[...] == lane + (start + 128 * t)) for t in range(width // 128)]
            return sums_of(mm(rows_ref[...], jnp.concatenate(marks, axis=1)), len(steps))

        def body(i, carry):
            start = pl.multiple_of(i * 256, 256)
            for out, part in zip(outs, block(start, 256)):
                out[:, pl.ds(start, 256)] = part
            return carry

        lax.fori_loop(0, 4, body, 0)
        for out, part in zip(outs, block(1024, 128)):
            out[:, 1024:CELLS] = part

    return call(
        kernel,
        [sds(S, CELLS)] * len(steps),
        [VMEM] * 11,
        *requests,
        cells,
        *registers,
        scratch=[pltpu.VMEM((2 * S * len(steps), total), bf16)],
        name=name,
    )


def box_facts(levels_ref):
    box = lax.axis_index("box")
    last = 7
    own = levels_ref[0, box]
    use_low = (box > 0) & (levels_ref[0, jnp.maximum(box - 1, 0)] == own)
    use_high = (box < last) & (levels_ref[0, jnp.minimum(box + 1, last)] == own)
    factor = lax.shift_left(1, own).astype(f32)
    return use_low, use_high, factor


def laplacian(planes, lower, upper, y_ghosts):
    rows = planes[0].shape[0]
    z = jnp.bitwise_and(lax.broadcasted_iota(i32, (rows, PLANE), 1), 31)
    wide = lax.broadcasted_iota(i32, (rows, 128), 1)
    result = []
    for x in range(X):
        v = planes[x]
        ghost = y_ghosts[x // 2]
        before_y = pltpu.roll(v, 32, 1)
        after_y = pltpu.roll(v, PLANE - 32, 1)
        before_y = jnp.concatenate(
            [jnp.where(wide < 32, ghost[:, :128], before_y[:, :128]), before_y[:, 128:]], axis=1
        )
        after_y = jnp.concatenate(
            [after_y[:, :896], jnp.where(wide >= 96, ghost[:, 128:], after_y[:, 896:])], axis=1
        )
        before_z = jnp.where(z == 0, v, pltpu.roll(v, 1, 1))
        after_z = jnp.where(z == 31, v, pltpu.roll(v, PLANE - 1, 1))
        before_x = planes[x - 1] if x > 0 else lower
        after_x = planes[x + 1] if x < X - 1 else upper
        result.append(before_x + after_x + before_y + after_y + before_z + after_z - 6.0 * v)
    return result


def y_code(shape, lane_dim, row_dim, half):
    lane = lax.broadcasted_iota(i32, shape, lane_dim)
    row = lax.broadcasted_iota(i32, shape, row_dim)
    fine = jnp.where(lane < 32, lane, lane - 192)
    code = jnp.where(lane < 32, half * 16 + (lane >> 1), 32 + half * 16 + ((lane - 224) >> 1))
    return ones_where((code == row) & ((lane < 32) | (lane >= 224)))


def x_code(shape, lane_dim, row_dim):
    lane = lax.broadcasted_iota(i32, shape, lane_dim)
    row = lax.broadcasted_iota(i32, shape, row_dim)
    return ones_where((((lane >> 6) << 4) | ((lane >> 1) & 15)) == row)


def first_stage(levels, diffusion, planes, growth, strips, below_plane, above_plane):
    def kernel(levels_ref, diffusion_ref, *refs):
        plane_refs, growth_refs, strip_refs = refs[:4], refs[4:8], refs[8:12]
        lower_ref, upper_ref = refs[12:14]
        middle_refs, base_refs = refs[14:18], refs[18:22]
        registers_ref, x_low_ref, x_high_ref = refs[22:25]
        y_refs = refs[25:27]
        use_low, use_high, factor = box_facts(levels_ref)
        diffusion_column = column_of(diffusion_ref[...])
        strip = strip_refs[0][...] + strip_refs[1][...] + strip_refs[2][...] + strip_refs[3][...]
        x_low, x_high = sums_of(mm(rows_of([strip[:, :256], strip[:, 256:512]]), x_code((256, PLANE), 1, 0)), 2)
        y_rows = rows_of([strip[:, 512:640]])
        y_ghosts = [sums_of(mm(y_rows, y_code((128, 256), 1, 0, half)), 1)[0] for half in range(2)]
        x_low_ref[...] = x_low
        x_high_ref[...] = x_high
        for ref, ghost in zip(y_refs, y_ghosts):
            ref[...] = ghost
        lower = jnp.where(use_low, lower_ref[...], x_low)
        upper = jnp.where(use_high, upper_ref[...], x_high)
        values = [ref[...] for ref in plane_refs]
        spread = laplacian(values, lower, upper, y_ghosts)
        means = []
        for x in range(X):
            rate = (factor * diffusion_column) * spread[x] + STEP * growth_refs[x][...]
            middle = values[x] + rate
            middle_refs[x][...] = middle
            base_refs[x][...] = values[x] + 0.5 * rate
            means.append(0.5 * (values[x] + middle))
        x_below = sums_of(mm(rows_of([means[0], means[3]]), x_code((PLANE, 256), 0, 1)), 2)
        y_below = jnp.zeros((S, 128), f32)
        for half in range(2):
            both = means[2 * half] + means[2 * half + 1]
            ends = jnp.concatenate([both[:, :128], both[:, 896:]], axis=1)
            y_below = y_below + sums_of(mm(rows_of([ends]), y_code((256, 128), 0, 1, half)), 1)[0]
        below = 0.25 * jnp.concatenate(x_below + [y_below], axis=1)
        column = lax.broadcasted_iota(i32, (1, WIDE), 1)
        keep_low = jnp.where(use_low, 0.0, 1.0)
        keep_high = jnp.where(use_high, 0.0, 1.0)
        keep = jnp.where(column < 256, keep_low, jnp.where(column < 512, keep_high, 1.0))
        registers_ref[...] = ((factor - 1.0) * diffusion_column) * (strip - below) * keep

    outs = call(
        kernel,
        [sds(S, PLANE)] * 8 + [sds(S, WIDE)] + [sds(S, PLANE)] * 2 + [sds(S, 256)] * 2,
        [SMEM] + [VMEM] * 15,
        levels,
        diffusion,
        *planes,
        *growth,
        *strips,
        below_plane,
        above_plane,
        name="first_stage",
    )
    return outs[:4], outs[4:8], outs[8], outs[9:11], outs[11:13]


def second_stage(levels, diffusion, middle, base, growth, x_ghosts, y_ghosts, below_plane, above_plane):
    rows = 8

    def kernel(levels_ref, diffusion_ref, *refs):
        middle_refs, base_refs, growth_refs = refs[:4], refs[4:8], refs[8:12]
        x_low_ref, x_high_ref, y_a, y_b, lower_ref, upper_ref, out_ref, held_ref, sems = refs[12:]
        use_low, use_high, factor = box_facts(levels_ref)
        scale = factor * column_of(diffusion_ref[...])
        copies = []
        for i in range(S // rows):
            part = slice(i * rows, (i + 1) * rows)
            lower = jnp.where(use_low, lower_ref[part], x_low_ref[part])
            upper = jnp.where(use_high, upper_ref[part], x_high_ref[part])
            spread = laplacian([ref[part] for ref in middle_refs], lower, upper, [y_a[part], y_b[part]])
            for x in range(X):
                rate = scale[part] * spread[x] + STEP * growth_refs[x][part]
                held_ref[part, x, :] = base_refs[x][part] + 0.5 * rate
            copies.append(pltpu.make_async_copy(held_ref.at[part], out_ref.at[part], sems.at[i]))
            copies[-1].start()
        for copy in copies:
            copy.wait()

    return pl.pallas_call(
        kernel,
        out_shape=sds(S, X, PLANE),
        in_specs=[SMEM] + [VMEM] * 19,
        out_specs=pl.BlockSpec(memory_space=pl.ANY),
        scratch_shapes=[pltpu.VMEM((S, X, PLANE), f32), pltpu.SemaphoreType.DMA((S // rows,))],
        compiler_params=pltpu.CompilerParams(vmem_limit_bytes=40 * MIB),
        cost_estimate=COST,
        name="second_stage",
    )(levels, diffusion, *middle, *base, *growth, *x_ghosts, *y_ghosts, below_plane, above_plane)


def finish_coarse(coarse, growth, parts):
    def kernel(coarse_ref, growth_ref, a, b, c, d, out_ref):
        total = (a[...] + b[...]) + (c[...] + d[...])
        out_ref[...] = coarse_ref[...] + STEP * growth_ref[...] - total

    return call(kernel, sds(S, CELLS), [VMEM] * 6, coarse, growth, *parts, name="finish_coarse")


def shifted(value, axis, shift):
    size = lax.axis_size(axis)
    return lax.ppermute(value, axis, [(i, (i + shift) % size) for i in range(size)])


def after(value, before):
    return lax.optimization_barrier((value, before))[0]


def on_device(fine_state, coarse_state, coag_kernel, diffusion, levels, ghost_src):
    fine = fine_state[0, 0]
    coarse = coarse_state[0, 0]
    row = diffusion.reshape(1, S)
    request = ghost_src[0]

    far = {k: shifted(coarse, "x", k) for k in (2, 1, 3)}
    spread = request + jnp.zeros((SPREAD, 1), i32)
    near = shifted(spread, "y", 1)
    mate = shifted(coarse, "core", 1)
    folded = fold_kernel(coag_kernel)
    near, folded = lax.optimization_barrier((near, folded))
    requests = jnp.concatenate([spread[: SPREAD // 2], near[: SPREAD // 2]], axis=0)
    requests = [requests, shifted(requests, "y", 2)]
    planes, held_coarse = split_planes(fine, after(coarse, (folded, requests[0])))
    below_plane, above_plane = shifted(planes[3], "box", 1), shifted(planes[0], "box", 7)
    growth = coagulate(after(folded, held_coarse), planes, "coagulate_fine")
    far, requests, growth = lax.optimization_barrier((far, requests, growth))

    sources, shifts = [held_coarse, mate], [(0, False), (0, True)]
    for k in (1, 3, 2):
        sources += [far[k], shifted(far[k], "core", 1)]
        shifts += [(k, False), (k, True)]
    part, strips = {}, {}
    part[2], rows, request_rows = gather_first(requests, sources, shifts, 2)
    strips[2] = shifted(part[2], "y", 2)
    part[1], part[3] = gather_next(request_rows, rows, shifts, (1, 3), "gather_near")
    strips[1], strips[3] = shifted(part[1], "y", 3), shifted(part[3], "y", 1)
    (strips[0],) = gather_next(after(request_rows, (part[3], strips[2])), rows, shifts, (0,), "gather_own")
    coarse_growth = coagulate(after(folded, (strips[0], strips[1])), [held_coarse], "coagulate_coarse")[0]
    mate_rows = shifted(request_rows, "core", 1)
    cells = cells_by_row([request_rows, after(mate_rows, coarse_growth)])
    strips, cells = lax.optimization_barrier((strips, cells))
    strips = [strips[k] for k in range(4)]

    middle, base, registers, x_ghosts, y_ghosts = first_stage(
        levels, row, planes, growth, strips, below_plane, above_plane
    )

    held = {k: shifted(registers, "y", k) for k in (2, 1, 3)}
    held[0] = registers
    growth = coagulate(folded, middle, "coagulate_middle")
    own_mate = shifted(registers, "core", 1)
    ends = after((middle[3], middle[0]), own_mate)
    below_plane, above_plane = shifted(ends[0], "box", 1), shifted(ends[1], "box", 7)
    held = [after(held[k], growth[0]) for k in range(4)]
    held += [own_mate] + [shifted(value, "core", 1) for value in held[1:]]
    cells = after(cells, (below_plane, above_plane))
    sent = {}
    (part,) = scatter_columns([request_rows, mate_rows], cells, held, (2,), "scatter_far")
    sent[2] = shifted(part, "x", 2)
    parts = scatter_columns([request_rows, mate_rows], after(cells, part), held, (1, 3), "scatter_near")
    sent[1], sent[3] = shifted(parts[0], "x", 1), shifted(parts[1], "x", 3)
    (sent[0],) = scatter_columns([request_rows, mate_rows], after(cells, parts[0]), held, (0,), "scatter_own")
    base = after(base, (sent[0], sent[2]))
    fine_out = second_stage(levels, row, middle, base, growth, x_ghosts, y_ghosts, below_plane, above_plane)
    sent = [sent[k] for k in range(4)]
    sent, fine_out, coarse_growth = lax.optimization_barrier((sent, fine_out, coarse_growth))
    coarse_out = finish_coarse(held_coarse, coarse_growth, sent)
    return fine_out[None, None], coarse_out[None, None]


def solution(mesh):
    group = ("x", "y", "core")
    split = Mesh(mesh.devices.reshape(4, 4, 2, 8), group + ("box",))
    return jax.shard_map(
        on_device,
        mesh=split,
        in_specs=(
            P(group, "box", None, None, None),
            P(group, "box", None, None),
            P(),
            P(),
            P(group, None),
            P(group, "box", None),
        ),
        out_specs=(P(group, "box", None, None, None), P(group, "box", None, None)),
        check_vma=False,
    )
```
